32 devices in a mesh: group: 4 (over y, core), dp: 8 (over z, x).
Axes of the slice: x: 2, y: 2, z: 4, core: 2. Of those that a mesh axis runs over, the one named last changes fastest.
Arguments:
- pixels: bfloat16 [4, 96, 64, 12, 256], P('group', 'dp'), may hold values from -6 to 6
- patch_index: int32 [4, 96, 64], P('group', 'dp'), may hold values from 0 to 195, as said below
- kept_count: int32 [4, 96], P('group', 'dp'), may hold values from 21 to 64, as said below
- wavelength: int32 [4, 12], P('group'), may hold values from 400 to 2499
- weight_tokens: bfloat16 [128, 128], replicated, may hold values from -6 to 6
- bias_token: bfloat16 [128], replicated, may hold values from -6 to 6
- hyper_project: bfloat16 [128, 384], replicated, may hold values from -0.5 to 0.5
- hyper_output: bfloat16 [128, 128], replicated, may hold values from -0.5 to 0.5
- hyper_gains: bfloat16 [2, 128], replicated, may hold values from 0.5 to 1.5
- hyper_shifts: bfloat16 [2, 128], replicated, may hold values from -3 to 3
- hyper_up: bfloat16 [128, 2048], replicated, may hold values from -0.5 to 0.5
- hyper_down: bfloat16 [2048, 128], replicated, may hold values from -0.125 to 0.125
- kernel_weight: bfloat16 [128, 256, 768], P(None, 'dp'), may hold values from -0.5 to 0.5
- kernel_bias: bfloat16 [256, 768], P('dp'), may hold values from -6 to 6
- bias_weight: bfloat16 [128, 768], replicated, may hold values from -2 to 2
- bias_shift: bfloat16 [768], replicated, may hold values from -120 to 120
- attention_in: bfloat16 [768, 2304], P('dp'), may hold values from -0.21875 to 0.21875
- attention_out: bfloat16 [768, 768], P('dp'), may hold values from -0.625 to 0.625
- expand_weight: bfloat16 [768, 3072], P('dp'), may hold values from -0.21875 to 0.21875
- reduce_weight: bfloat16 [3072, 768], P('dp'), may hold values from -0.15625 to 0.15625
- norm_gains: bfloat16 [2, 768], replicated, may hold values from 0.5 to 1.5
- norm_shifts: bfloat16 [2, 768], replicated, may hold values from -3 to 3
- attention_bias: bfloat16 [2, 768], replicated, may hold values from -3 to 3
- output_bias: bfloat16 [768], replicated, may hold values from -3 to 3
- expand_bias: bfloat16 [3072], replicated, may hold values from -3 to 3
- reduce_bias: bfloat16 [768], replicated, may hold values from -3 to 3
- cotangent: bfloat16 [4, 96, 64, 768], P('group', 'dp'), may hold values from -6 to 6
Outputs:
- encoded: bfloat16 [4, 96, 64, 768], P('group', 'dp')
- pixel_grad: bfloat16 [4, 96, 64, 12, 256], P('group', 'dp')
- weight_tokens_grad: float32 [128, 128], replicated
- bias_token_grad: float32 [128], replicated
- hyper_project_grad: float32 [128, 384], replicated
- hyper_output_grad: float32 [128, 128], replicated
- hyper_gains_grad: float32 [2, 128], replicated
- hyper_shifts_grad: float32 [2, 128], replicated
- hyper_up_grad: float32 [128, 2048], replicated
- hyper_down_grad: float32 [2048, 128], replicated
- kernel_weight_grad: float32 [128, 256, 768], P(None, 'dp')
- kernel_bias_grad: float32 [256, 768], P('dp')
- bias_weight_grad: float32 [128, 768], replicated
- bias_shift_grad: float32 [768], replicated
- attention_in_grad: float32 [768, 2304], P('dp')
- attention_out_grad: float32 [768, 768], P('dp')
- expand_weight_grad: float32 [768, 3072], P('dp')
- reduce_weight_grad: float32 [3072, 768], P('dp')
- norm_gains_grad: float32 [2, 768], replicated
- norm_shifts_grad: float32 [2, 768], replicated
- attention_bias_grad: float32 [2, 768], replicated
- output_bias_grad: float32 [768], replicated
- expand_bias_grad: float32 [3072], replicated
- reduce_bias_grad: float32 [768], replicated
The draws below stay inside these ranges and needn't reach their ends.
Inputs may be any that keep to these rules, and one draw needn't show every extreme that they name: `patch_index`: within an image the 64 entries are distinct patch numbers; slots at or past the image's kept_count are padding. `kept_count`: in every group at least one image keeps all 64 slots.
All inputs are finite; a program needn't handle non-finite values.
Results may differ from the reference program's by a relative error of at most 0.019.
Values may be sent and summed in bfloat16 or wider, within the bound.
No kernel may reach another device: no remote copies, remote signals or barrier semaphores. Data moves between devices by JAX's collectives and lax.ppermute only.
A program may use at most 256 MiB of HBM per device.

```python
import jax
import jax.numpy as jnp
from jax import lax

HEADS = 12
HEAD_DIM = 64
D = 768
FF = 3072
HE = 128
HH = 4
HFF = 2048
WT = 128
PIX = 256
NB = 12
SIDE = 14
PATCHES = 196
SLOTS = 64
IMG_DEV = 12
IMAGES = 96
GROUPS = 4
N_DP = 8


def draw_kept_count(key, part):
    key = jax.random.fold_in(key, 11)
    count_key, peak_key = jax.random.split(key)
    counts = jax.random.randint(count_key, (GROUPS, IMAGES), max(1, SLOTS // 3), SLOTS + 1)
    fullest = jax.random.randint(peak_key, (GROUPS,), 0, IMAGES)
    fullest_mask = jnp.arange(IMAGES, dtype=jnp.int32)[None, :] == fullest[:, None]
    return jnp.where(fullest_mask, SLOTS, counts).astype(jnp.int32)


def draw_patch_index(key, part):
    key = jax.random.fold_in(key, 23)
    scores = jax.random.randint(key, (GROUPS, IMAGES, PATCHES), 0, 1 << 20) * PATCHES + jnp.arange(PATCHES, dtype=jnp.int32)
    ranking = jnp.argsort(scores, axis=-1, stable=True)
    return ranking[..., :SLOTS].astype(jnp.int32)


def plant(entries, own_key, smallest, high):
    longest = entries.shape.index(max(entries.shape))
    spots = []
    for shift in (0, 1):
        where = [jax.random.randint(jax.random.fold_in(own_key, axis), (), 0, length) for axis, length in enumerate(entries.shape)]
        where[longest] = (where[longest] + shift) % entries.shape[longest]
        spots.append(tuple(where))
    return entries.at[spots[0]].set(smallest).at[spots[1]].set(high)


def level_of(stream_key, shape, cuts, low, top_value):
    gain = 1.0
    for dim, shards_of in cuts:
        heights = jax.random.uniform(jax.random.fold_in(jax.random.fold_in(stream_key, 6), dim), (shards_of,), jnp.float32, low / len(cuts), top_value / len(cuts))
        gain = gain * jnp.repeat(jnp.exp(heights), shape[dim] // shards_of).reshape((-1,) + (1,) * (len(shape) - 1 - dim))
    return gain


def scatter_about(key, shape, spread, most, shards=(), held_as=jnp.bfloat16):
    entries = spread * jax.random.normal(key, shape, jnp.float32)
    if shards:
        entries = entries * level_of(key, shape, shards, -0.22, 0.18)
    return jnp.clip(entries, -most, most).astype(held_as)


def setup_inputs(seed: int = 0) -> dict:
    arg_keys = jax.random.split(jax.random.key(seed), 28)
    return {
        "pixels": scatter_about(arg_keys[0], (GROUPS, IMAGES, SLOTS, NB, PIX), 1.0, 6.0, ((0, 4), (1, 8))),
        "patch_index": draw_patch_index(jax.random.fold_in(arg_keys[27], 71), 0),
        "kept_count": draw_kept_count(jax.random.fold_in(arg_keys[27], 71), 0),
        "wavelength": plant(jax.random.randint(arg_keys[3], (GROUPS, NB), 400, 2500), jax.random.fold_in(arg_keys[3], 1), 400, 2499).astype(jnp.int32),
        "weight_tokens": scatter_about(arg_keys[4], (WT, HE), 1.0, 6.0),
        "bias_token": scatter_about(arg_keys[5], (HE,), 1.0, 6.0),
        "hyper_project": scatter_about(arg_keys[6], (HE, 3 * HE), HE ** -0.5, 0.5),
        "hyper_output": scatter_about(arg_keys[7], (HE, HE), HE ** -0.5, 0.5),
        "hyper_gains": jnp.clip(1.0 + 0.1 * jax.random.normal(arg_keys[8], (2, HE), jnp.float32), 0.5, 1.5).astype(jnp.bfloat16),
        "hyper_shifts": scatter_about(arg_keys[9], (2, HE), 0.5, 3.0),
        "hyper_up": scatter_about(arg_keys[10], (HE, HFF), HE ** -0.5, 0.5),
        "hyper_down": scatter_about(arg_keys[11], (HFF, HE), HFF ** -0.5, 0.125),
        "kernel_weight": scatter_about(arg_keys[12], (HE, PIX, D), HE ** -0.5, 0.5, ((1, 8),)),
        "kernel_bias": scatter_about(arg_keys[13], (PIX, D), 1.0, 6.0, ((0, 8),)),
        "bias_weight": scatter_about(arg_keys[14], (HE, D), (HE // 16) ** -0.5, 2.0),
        "bias_shift": scatter_about(arg_keys[15], (D,), 30.0, 120.0),
        "attention_in": scatter_about(arg_keys[16], (D, 3 * D), D ** -0.5, 0.21875, ((0, 8),)),
        "attention_out": scatter_about(arg_keys[17], (D, D), (D // 8) ** -0.5, 0.625, ((0, 8),)),
        "expand_weight": scatter_about(arg_keys[18], (D, FF), D ** -0.5, 0.21875, ((0, 8),)),
        "reduce_weight": scatter_about(arg_keys[19], (FF, D), (FF // 2) ** -0.5, 0.15625, ((0, 8),)),
        "norm_gains": jnp.clip(1.0 + 0.1 * jax.random.normal(arg_keys[20], (2, D), jnp.float32), 0.5, 1.5).astype(jnp.bfloat16),
        "norm_shifts": scatter_about(arg_keys[21], (2, D), 0.5, 3.0),
        "attention_bias": scatter_about(arg_keys[22], (2, D), 0.5, 3.0),
        "output_bias": scatter_about(arg_keys[23], (D,), 0.5, 3.0),
        "expand_bias": scatter_about(arg_keys[24], (FF,), 0.5, 3.0),
        "reduce_bias": scatter_about(arg_keys[25], (D,), 0.5, 3.0),
        "cotangent": scatter_about(arg_keys[26], (GROUPS, IMAGES, SLOTS, D), 1.0, 6.0, ((0, 4), (1, 8))),
    }


@jax.custom_vjp
def low(v):
    return lax.optimization_barrier(v.astype(jnp.bfloat16)).astype(jnp.float32)

@jax.custom_vjp
def low_back(v):
    return v

def low_keep(v):
    return (low(v), None)

def low_pass(kept, grad):
    return (grad,)

def back_keep(v):
    return (v, None)

def back_low(kept, grad):
    return (low(grad),)
low.defvjp(low_keep, low_pass)
low_back.defvjp(back_keep, back_low)
scaler = 0.01
highest = lax.Precision.HIGHEST

def layer_norm(values, gain_row, shift_row, epsilon):
    center = values - lax.optimization_barrier(jnp.mean(values, -1, keepdims=True))
    scaled = center * lax.rsqrt(lax.optimization_barrier(jnp.mean(center * center, -1, keepdims=True)) + epsilon)
    return scaled * gain_row + shift_row

def wave_embed(wave_ids):
    half_width = HE // 2
    frequency = 1.0 / 10000.0 ** (jnp.arange(half_width, dtype=jnp.float32) / half_width)
    angles = wave_ids.astype(jnp.float32)[:, None] * frequency
    return jnp.concatenate([jnp.sin(angles), jnp.cos(angles)], -1)

def place_embed(patch_ids, model_width):
    quarter = model_width // 4
    frequency = 1.0 / 10000.0 ** (jnp.arange(quarter, dtype=jnp.float32) / quarter)
    row_angle = (patch_ids // SIDE).astype(jnp.float32)[..., None] * frequency
    col_angle = (patch_ids % SIDE).astype(jnp.float32)[..., None] * frequency
    return jnp.concatenate([jnp.sin(row_angle), jnp.cos(row_angle), jnp.sin(col_angle), jnp.cos(col_angle)], -1)

def hyper_core(wave_rows, weight_tokens, bias_token, hyper_project, hyper_output, hyper_gains, hyper_shifts, hyper_up, hyper_down):
    token_count = weight_tokens.shape[0]
    band_count = wave_rows.shape[0]
    sequence = jnp.concatenate([weight_tokens, wave_rows, bias_token[None, :]], 0)
    length = sequence.shape[0]
    project = jnp.dot(sequence, hyper_project, precision=highest)
    split_heads = project.reshape(length, 3, HH, -1)
    queries = split_heads[:, 0]
    keys_all = split_heads[:, 1]
    values_all = split_heads[:, 2]
    scores = jnp.einsum('qhd,khd->hqk', queries, keys_all, precision=highest) * queries.shape[-1] ** (-0.5)
    weights = jax.nn.softmax(scores, -1)
    mixed_rows = jnp.einsum('hqk,khd->qhd', weights, values_all, precision=highest).reshape(length, -1)
    hidden = layer_norm(sequence + jnp.dot(mixed_rows, hyper_output, precision=highest), hyper_gains[0], hyper_shifts[0], 1e-05)
    expanded = jax.nn.gelu(jnp.dot(hidden, hyper_up, precision=highest), approximate=False)
    hidden = layer_norm(hidden + jnp.dot(expanded, hyper_down, precision=highest), hyper_gains[1], hyper_shifts[1], 1e-05)
    band_feats = hidden[token_count:token_count + band_count] + wave_rows
    return (band_feats, hidden[length - 1])

def block_forward(pixel_block, patch_ids, count_block, kernel, conv_bias, attention_in, attention_out, expand_weight, reduce_weight, norm_gains, norm_shifts, attention_bias, output_bias, expand_bias, reduce_bias):
    image_count = pixel_block.shape[0]
    valid_mask = jnp.arange(SLOTS, dtype=jnp.int32)[None, :] < count_block[:, None]
    conv_out = low_back(jnp.einsum('isbp,pbd->isd', pixel_block, kernel, precision=highest))
    start = conv_out + conv_bias + place_embed(patch_ids, D)
    hidden_one = low(layer_norm(start, norm_gains[0], norm_shifts[0], 1e-06))
    bias_full = jnp.concatenate([attention_bias[0], jnp.zeros((D,), jnp.float32), attention_bias[1]])
    project = low_back(low(jnp.einsum('isd,de->ise', hidden_one, attention_in, precision=highest) + bias_full))
    split_heads = project.reshape(image_count, SLOTS, 3, HEADS, HEAD_DIM)
    queries = split_heads[:, :, 0]
    keys_all = split_heads[:, :, 1]
    values_all = split_heads[:, :, 2]
    scores = low_back(jnp.einsum('iqhd,ikhd->ihqk', queries, keys_all, precision=highest) * HEAD_DIM ** (-0.5))
    masked = jnp.where(valid_mask[:, None, None, :], scores, -1000000000.0)
    probs_low = low(jax.nn.softmax(masked, -1))
    mixed_rows = low_back(low(jnp.einsum('ihqk,ikhd->iqhd', probs_low, values_all, precision=highest))).reshape(image_count, SLOTS, D)
    middle = start + low_back(jnp.einsum('isd,de->ise', mixed_rows, attention_out, precision=highest)) + output_bias
    hidden_two = low(layer_norm(middle, norm_gains[1], norm_shifts[1], 1e-06))
    expand_pre = low_back(jnp.einsum('isd,df->isf', hidden_two, expand_weight, precision=highest)) + expand_bias
    activated = low(jax.nn.gelu(expand_pre, approximate=False))
    final_rows = middle + low_back(jnp.einsum('isf,fd->isd', activated, reduce_weight, precision=highest)) + reduce_bias
    return final_rows * valid_mask[..., None].astype(jnp.float32)

def reference(pixels, patch_index, kept_count, wavelength, weight_tokens, bias_token, hyper_project, hyper_output, hyper_gains, hyper_shifts, hyper_up, hyper_down, kernel_weight, kernel_bias, bias_weight, bias_shift, attention_in, attention_out, expand_weight, reduce_weight, norm_gains, norm_shifts, attention_bias, output_bias, expand_bias, reduce_bias, cotangent):
    floaty = jnp.float32
    hyper_params = tuple((member.astype(floaty) for member in (weight_tokens, bias_token, hyper_project, hyper_output, hyper_gains, hyper_shifts, hyper_up, hyper_down)))
    head_params = tuple((member.astype(floaty) for member in (kernel_weight, kernel_bias, bias_weight, bias_shift)))
    block_params = tuple((member.astype(floaty) for member in (attention_in, attention_out, expand_weight, reduce_weight, norm_gains, norm_shifts, attention_bias, output_bias, expand_bias, reduce_bias)))
    hyper_total = tuple((jnp.zeros_like(member) for member in hyper_params))
    head_total = tuple((jnp.zeros_like(member) for member in head_params))
    block_total = tuple((jnp.zeros_like(member) for member in block_params))
    encoded_all = []
    pixel_all = []
    for group_id in range(GROUPS):
        wave_rows = wave_embed(wavelength[group_id])

        def hyper_all(hyper_in, head_in):
            band_feats, bias_feat = hyper_core(wave_rows, *hyper_in)
            kernel = low(scaler * (jnp.einsum('bh,hpd->pbd', band_feats, head_in[0], precision=highest) + head_in[1][:, None, :]))
            conv_bias = scaler * (jnp.dot(bias_feat, head_in[2], precision=highest) + head_in[3])
            return (kernel, conv_bias)
        (kernel, conv_bias), hyper_back = jax.vjp(hyper_all, hyper_params, head_params)

        def block_step(running, block_items):
            pixel_block, index_block, count_block, grad_block = block_items

            def forward(pixel_in, kernel_in, bias_in, params_in):
                return block_forward(pixel_in, index_block, count_block, kernel_in, bias_in, *params_in)
            result, block_back = jax.vjp(forward, pixel_block.astype(floaty), kernel, conv_bias, block_params)
            pixel_part, kernel_part, bias_part, params_part = block_back(grad_block.astype(floaty))
            running = (running[0] + kernel_part, running[1] + bias_part, jax.tree.map(jnp.add, running[2], params_part))
            return (running, (result.astype(jnp.bfloat16), pixel_part.astype(jnp.bfloat16)))
        block_items = (pixels[group_id].reshape(N_DP, IMG_DEV, SLOTS, NB, PIX), patch_index[group_id].reshape(N_DP, IMG_DEV, SLOTS), kept_count[group_id].reshape(N_DP, IMG_DEV), cotangent[group_id].reshape(N_DP, IMG_DEV, SLOTS, D))
        start_carry = (jnp.zeros_like(kernel), jnp.zeros_like(conv_bias), tuple((jnp.zeros_like(member) for member in block_params)))
        running, (encoded_rows, pixel_rows) = lax.scan(block_step, start_carry, block_items)
        hyper_grad, head_grad = hyper_back((running[0], running[1]))
        hyper_total = jax.tree.map(jnp.add, hyper_total, tuple(hyper_grad))
        head_total = jax.tree.map(jnp.add, head_total, tuple(head_grad))
        block_total = jax.tree.map(jnp.add, block_total, tuple(running[2]))
        encoded_all.append(encoded_rows.reshape(IMAGES, SLOTS, D))
        pixel_all.append(pixel_rows.reshape(IMAGES, SLOTS, NB, PIX))
    return (jnp.stack(encoded_all), jnp.stack(pixel_all), hyper_total[0], hyper_total[1], hyper_total[2], hyper_total[3], hyper_total[4], hyper_total[5], hyper_total[6], hyper_total[7], head_total[0], head_total[1], head_total[2], head_total[3], block_total[0], block_total[1], block_total[2], block_total[3], block_total[4], block_total[5], block_total[6], block_total[7], block_total[8], block_total[9])
```

```python
from functools import partial

import jax
import jax.numpy as jnp
import numpy as np
from jax import lax
from jax.experimental import pallas as pl
from jax.experimental.pallas import tpu as pltpu
from jax.sharding import PartitionSpec as P

HE = 128
HH = 4
SIDE = 14


scaler = 0.01
highest = lax.Precision.HIGHEST


def contract_rows(operand, partner):
    return lax.dot_general(
        operand, partner, (((0,), (0,)), ((), ())), preferred_element_type=jnp.float32
    )


def wave_embed(wave_ids):
    half_width = HE // 2
    frequency = 1.0 / 10000.0 ** (jnp.arange(half_width, dtype=jnp.float32) / half_width)
    angles = wave_ids.astype(jnp.float32)[:, None] * frequency
    return jnp.concatenate([jnp.sin(angles), jnp.cos(angles)], -1)


def place_table(model_width):
    quarter = model_width // 4
    frequency = 1.0 / 10000.0 ** (jnp.arange(quarter, dtype=jnp.float32) / quarter)
    angle = jnp.arange(SIDE, dtype=jnp.float32)[:, None] * frequency
    waves = jnp.concatenate([jnp.sin(angle), jnp.cos(angle)], -1)
    blank = jnp.zeros_like(waves)
    return jnp.concatenate(
        [jnp.concatenate([waves, blank], -1), jnp.concatenate([blank, waves], -1)], 0
    )


def place_spots(patch_ids, copies):
    lanes = jnp.arange(128, dtype=jnp.int32)[None, :]
    spot = lanes % (2 * SIDE + 1)
    row_id = (patch_ids // SIDE)[:, None]
    col_id = (patch_ids % SIDE)[:, None] + SIDE
    hit = (spot == row_id) | (spot == col_id) | (spot == 2 * SIDE)
    return (hit & (lanes < copies * (2 * SIDE + 1))).astype(jnp.bfloat16)


def split_low(values, count, axis):
    pieces = []
    for _ in range(count):
        piece = values.astype(jnp.bfloat16)
        pieces.append(piece)
        values = values - piece.astype(jnp.float32)
    return jnp.concatenate(pieces, axis)


def stage(*values):
    return lax.optimization_barrier(values)


class Links:
    def __init__(self, group_size, dp_size):
        self.group_size = group_size
        self.dp_size = dp_size
        group_id = lax.axis_index("group")
        dp_id = lax.axis_index("dp")
        self.y = group_id // 2
        self.c = group_id % 2
        self.x = dp_id % 2
        self.digits = []
        stride = 2
        while stride < dp_size:
            size = min(4, dp_size // stride)
            self.digits.insert(0, (size, stride, dp_id // stride % size))
            stride *= size
        self.line = dp_size // 2
        self.z = dp_id // 2

    def core(self, block):
        return lax.ppermute(block, "group", [(i, i ^ 1) for i in range(self.group_size)])

    def yside(self, block):
        return lax.ppermute(block, "group", [(i, i ^ 2) for i in range(self.group_size)])

    def xside(self, block):
        return lax.ppermute(block, "dp", [(i, i ^ 1) for i in range(self.dp_size)])

    def zside(self, block, step):
        return lax.ppermute(block, "dp", [(i, i ^ step) for i in range(self.dp_size)])

    def owner_pairs(self, target_of):
        pairs = []
        for group_id in range(self.group_size):
            for dp_id in range(self.dp_size):
                target = target_of(group_id, dp_id)
                if target is not None:
                    pairs.append(
                        (group_id * self.dp_size + dp_id, target[0] * self.dp_size + target[1])
                    )
        return pairs

    def owner_line(self, block):
        top = self.dp_size // 2
        pairs = self.owner_pairs(lambda g, d: (g, d ^ top) if d // top != g % 2 else None)
        return lax.ppermute(block, ("group", "dp"), pairs)

    def owner_core(self, block):
        top = self.dp_size // 2
        pairs = self.owner_pairs(lambda g, d: (g ^ 1, d) if d // top == g % 2 else None)
        return lax.ppermute(block, ("group", "dp"), pairs)


def pick(block, index, axis, count=1):
    return lax.dynamic_slice_in_dim(block, index, count, axis)


def add_low(one, two):
    return (one.astype(jnp.float32) + two.astype(jnp.float32)).astype(jnp.bfloat16)


def pair_up(block, other, bit, axis):
    return jnp.where(
        bit == 0,
        jnp.concatenate([block, other], axis),
        jnp.concatenate([other, block], axis),
    )


def place_digit(block, received, me, axis):
    size = len(received) + 1
    shape = block.shape[:axis] + (size,) + block.shape[axis + 1 :]
    out = jnp.zeros(shape, block.dtype)
    for step, piece in zip(range(size), [block] + received):
        at = tuple(me ^ step if i == axis else 0 for i in range(len(shape)))
        out = lax.dynamic_update_slice(out, piece, at)
    return out


def gather_line(links, piece, axis):
    lead, tail = piece.shape[:axis], piece.shape[axis + 1 :]
    count = len(links.digits)
    block = piece.reshape(lead + (1,) * count + tail)
    for place, (size, stride, me) in reversed(list(enumerate(links.digits))):
        received = [links.zside(block, stride * step) for step in range(1, size)]
        block = place_digit(block, received, me, axis + place)
    return block.reshape(lead + (links.line,) + tail)


def reduce_line(links, block, axis, sender):
    lead, tail = block.shape[:axis], block.shape[axis + 1 :]
    block = block.reshape(lead + tuple(size for size, _, _ in links.digits) + tail)
    for place, (size, stride, me) in enumerate(links.digits):
        if place:
            block = block.astype(jnp.bfloat16)
        received = [
            sender(pick(block, me ^ step, axis + place), stride * step) for step in range(1, size)
        ]
        block = pick(block, me, axis + place).astype(jnp.float32)
        for piece in received:
            block = block + piece.astype(jnp.float32)
    return block.reshape(lead + tail)


def attention_piece(links, attention_in, attention_out):
    width = attention_out.shape[1]
    thirds = [attention_in[:, i * width : (i + 1) * width] for i in range(3)]
    return lax.dynamic_index_in_dim(
        jnp.stack(thirds + [attention_out]), lax.axis_index("group"), 0, False
    )


def gather_feed(links, expand_weight, reduce_weight):
    width = reduce_weight.shape[1]
    count = links.group_size
    group_id = lax.axis_index("group")
    up = pick(expand_weight, group_id * width, 1, width)
    rows = reduce_weight.shape[0] // count
    down = pick(reduce_weight, group_id * rows, 0, rows)
    wide = lax.all_gather(jnp.stack([up, down]), ("dp", "group"), axis=0)
    wide = wide.reshape(links.dp_size, count, 2, rows, width)
    if rows % 16:
        up = wide[:, :, 0].transpose(1, 0, 2, 3).reshape(count, 8, width // 8, width)
        down = wide[:, :, 1].reshape(8, count, width // 8, width)
        wide = jnp.stack([up.transpose(1, 0, 2, 3), down], 2)
    return wide


def spread_group(links, piece):
    piece = piece.reshape((1, 1) + piece.shape)
    piece = pair_up(piece, links.yside(piece), links.y, 0)
    piece = pair_up(piece, links.core(piece), links.c, 1)
    return piece.reshape((-1,) + piece.shape[2:])


def sum_dp(links, values):
    step = 1
    while step < links.dp_size:
        values = values + links.zside(values, step)
        step *= 2
    return values


VMEM_BYTES = 60 * 1024 * 1024


def kernel_params():
    return pltpu.CompilerParams(vmem_limit_bytes=VMEM_BYTES)


def whole_spec(shape):
    return pl.BlockSpec(shape, lambda *_: (0,) * len(shape))


def norm_rows(values, epsilon):
    center = values - jnp.mean(values, -1, keepdims=True)
    inverse = lax.rsqrt(jnp.mean(center * center, -1, keepdims=True) + epsilon)
    return center * inverse, inverse


def dot_nn(one, two):
    return lax.dot_general(one, two, (((1,), (0,)), ((), ())), preferred_element_type=jnp.float32)


def dot_nt(one, two):
    return lax.dot_general(one, two, (((1,), (1,)), ((), ())), preferred_element_type=jnp.float32)


def dot_tn(one, two):
    return lax.dot_general(one, two, (((0,), (0,)), ((), ())), preferred_element_type=jnp.float32)


def embed_body(part_ref, pixel_ref, kernel_ref, norm_ref, start_ref, hidden_ref):
    start = part_ref[...] + dot_nn(pixel_ref[...], kernel_ref[...])
    start_ref[...] = start
    normed, _ = norm_rows(start, 1e-06)
    hidden_ref[...] = (normed * norm_ref[0:1, :] + norm_ref[1:2, :]).astype(jnp.bfloat16)


def embed_rows(part, pixel_rows, wide_kernel, norm_one, block_rows):
    rows = part.shape[0]
    depth = wide_kernel.shape[0]
    last = pixel_rows.shape[1] // depth - 1
    width = wide_kernel.shape[1]
    row_spec = lambda cols: pl.BlockSpec((block_rows, cols), lambda i: (i, 0))
    return pl.pallas_call(
        embed_body,
        grid=(rows // block_rows,),
        in_specs=[
            row_spec(width),
            pl.BlockSpec((block_rows, depth), lambda i: (i, last)),
            whole_spec(wide_kernel.shape),
            whole_spec(norm_one.shape),
        ],
        out_specs=[row_spec(width), row_spec(width)],
        out_shape=[
            jax.ShapeDtypeStruct((rows, width), jnp.float32),
            jax.ShapeDtypeStruct((rows, width), jnp.bfloat16),
        ],
        compiler_params=kernel_params(),
        cost_estimate=pl.CostEstimate(
            flops=2 * rows * depth * width,
            bytes_accessed=2 * (rows * depth + depth * width) + 6 * rows * width,
            transcendentals=0,
        ),
        name="embed_rows",
    )(part, pixel_rows, wide_kernel, norm_one)


def pair_stack(block, low_half):
    zero = jnp.zeros_like(block)
    return jnp.concatenate(
        [jnp.where(low_half, block, zero), jnp.where(low_half, zero, block)], 0
    )


def half_reduce(values, low_half, reducer, filler):
    first = reducer(jnp.where(low_half, values, filler), -1, keepdims=True)
    second = reducer(jnp.where(low_half, filler, values), -1, keepdims=True)
    return jnp.where(low_half, first, second)


def attend_body(
    first,
    count_ref,
    hidden_ref,
    start_ref,
    weight_ref,
    bias_ref,
    rows_ref,
    project_ref,
    probs_ref,
    mixed_ref,
    middle_ref,
    hidden_two_ref,
):
    block_rows, width = hidden_ref.shape
    slots = 64
    images = block_rows // slots
    base = (pl.program_id(0) + first) * images
    for third in range(3):
        at = third * width
        weight = weight_ref[:, third].reshape(width, width)
        project_ref[:, at : at + width] = (
            dot_nn(hidden_ref[...], weight) + bias_ref[:, at : at + width]
        ).astype(jnp.bfloat16)
    lanes = lax.broadcasted_iota(jnp.int32, (slots, 128), 1)
    low_half = lanes < 64
    key_id = jnp.where(low_half, lanes, lanes - 64)
    for image in range(images):
        count = count_ref[base + image]
        keep = key_id < count
        here = slice(image * slots, (image + 1) * slots)
        for pair in range(width // 128):
            at = pair * 128
            queries = project_ref[here, at : at + 128]
            keys = pair_stack(project_ref[here, width + at : width + at + 128], low_half)
            values = pair_stack(project_ref[here, 2 * width + at : 2 * width + at + 128], low_half)
            scores = jnp.where(keep, dot_nt(queries, keys) * 0.125, -1000000000.0)
            peak = half_reduce(scores, low_half, jnp.max, -3e38)
            probs = jnp.exp(scores - peak)
            total = half_reduce(probs, low_half, jnp.sum, 0.0)
            probs_low = (probs / total).astype(jnp.bfloat16)
            probs_ref[here, at : at + 128] = probs_low
            mixed_ref[here, at : at + 128] = dot_nn(probs_low, values).astype(jnp.bfloat16)
    middle = start_ref[...] + dot_nn(mixed_ref[...], weight_ref[:, 3].reshape(width, width)) + rows_ref[0:1, :]
    middle_ref[...] = middle
    normed, _ = norm_rows(middle, 1e-06)
    hidden_two_ref[...] = (normed * rows_ref[1:2, :] + rows_ref[2:3, :]).astype(jnp.bfloat16)


def attend_rows(first, steps, earlier, counts, hidden_one, start, weights, bias_full, rows_in):
    rows, width = hidden_one.shape
    block_rows = 128
    row_spec = lambda cols: pl.BlockSpec((block_rows, cols), lambda i, *_: (i + first, 0))
    low = jnp.bfloat16
    keep = list(earlier or ())

    def body(count_ref, *refs):
        refs = refs[:5] + refs[5 + len(keep) :]
        attend_body(first, count_ref, *refs)

    return pl.pallas_call(
        body,
        grid_spec=pltpu.PrefetchScalarGridSpec(
            num_scalar_prefetch=1,
            grid=(steps,),
            in_specs=[
                row_spec(width),
                row_spec(width),
                whole_spec(weights.shape),
                whole_spec(bias_full.shape),
                whole_spec(rows_in.shape),
                *(pl.BlockSpec(memory_space=pl.ANY) for _ in keep),
            ],
            out_specs=[
                row_spec(3 * width),
                row_spec(width),
                row_spec(width),
                row_spec(width),
                row_spec(width),
            ],
        ),
        out_shape=[
            jax.ShapeDtypeStruct((rows, 3 * width), low),
            jax.ShapeDtypeStruct((rows, width), low),
            jax.ShapeDtypeStruct((rows, width), low),
            jax.ShapeDtypeStruct((rows, width), jnp.float32),
            jax.ShapeDtypeStruct((rows, width), low),
        ],
        input_output_aliases={6 + i: i for i in range(len(keep))},
        compiler_params=kernel_params(),
        cost_estimate=pl.CostEstimate(
            flops=16 * steps * block_rows * width * width,
            bytes_accessed=8 * width * width + 20 * steps * block_rows * width,
            transcendentals=rows * width,
        ),
        name="attend_rows",
    )(counts, hidden_one, start, weights, bias_full, rows_in, *keep)


def expand_step(hidden_ref, turned_ref, out_ref, up_ref, bias_ref, down_ref):
    low = jnp.bfloat16
    out_low = out_ref[...]
    width = out_low.shape[1]
    up = up_ref[...].reshape(width, -1)
    down = down_ref[...].reshape(-1, width)
    pre = dot_nn(hidden_ref[...], up) + bias_ref[...]
    cumulative = 0.5 + 0.5 * lax.erf(pre * 0.7071067811865476)
    slope = cumulative + pre * (jnp.exp(pre * pre * -0.5) * 0.3989422804014327)
    activated = (pre * cumulative).astype(low)
    pre_grad = dot_nt(out_low, down) * slope
    pre_low = pre_grad.astype(low)
    return (
        jnp.sum(pre_grad, 0, keepdims=True),
        dot_nn(activated, down),
        dot_nt(pre_low, up),
        dot_nn(turned_ref[...], pre_low),
        dot_tn(activated, out_low),
    )


def accumulate(ref, part):
    @pl.when(pl.program_id(0) == 0)
    def _():
        ref[...] = part

    @pl.when(pl.program_id(0) > 0)
    def _():
        ref[...] += part


def first_body(
    half_ref,
    hidden_ref,
    out_ref,
    up_ref,
    bias_ref,
    down_ref,
    grad_up_ref,
    grad_down_ref,
    bias_grad_ref,
    forward_ref,
    back_ref,
    turned_ref,
):
    @pl.when(pl.program_id(0) == 0)
    def _():
        turned_ref[...] = hidden_ref[...].T

    bias_grad, forward_part, back_part, grad_up, grad_down = expand_step(
        hidden_ref, turned_ref, out_ref, up_ref, bias_ref, down_ref
    )
    bias_grad_ref[...] = bias_grad
    grad_up_ref[...] = grad_up.astype(jnp.bfloat16)
    grad_down_ref[...] = grad_down.astype(jnp.bfloat16)
    accumulate(forward_ref, forward_part)
    accumulate(back_ref, back_part)


def second_body(
    half_ref,
    hidden_ref,
    out_ref,
    up_ref,
    bias_ref,
    down_ref,
    forward_ref,
    back_ref,
    middle_ref,
    valid_ref,
    rows_ref,
    grad_up_ref,
    grad_down_ref,
    bias_grad_ref,
    encoded_ref,
    middle_grad_ref,
    middle_low_ref,
    sums_ref,
    forward_acc,
    back_acc,
    turned_ref,
):
    step = pl.program_id(0)
    low = jnp.bfloat16

    @pl.when(step == 0)
    def _():
        turned_ref[...] = hidden_ref[...].T
        forward_acc[...] = forward_ref[...]
        back_acc[...] = back_ref[...]

    bias_grad, forward_part, back_part, grad_up, grad_down = expand_step(
        hidden_ref, turned_ref, out_ref, up_ref, bias_ref, down_ref
    )
    bias_grad_ref[...] = bias_grad
    grad_up_ref[...] = grad_up.astype(low)
    grad_down_ref[...] = grad_down.astype(low)
    forward_acc[...] += forward_part
    back_acc[...] += back_part

    @pl.when(step == pl.num_programs(0) - 1)
    def _():
        middle = middle_ref[...]
        encoded_ref[...] = (
            (middle + forward_acc[...] + rows_ref[0:1, :]) * valid_ref[...]
        ).astype(low)
        normed, inverse = norm_rows(middle, 1e-06)
        grad = back_acc[...]
        out_grad = out_ref[...].astype(jnp.float32)
        scaled = grad * rows_ref[1:2, :]
        middle_grad = out_grad + inverse * (
            scaled
            - jnp.mean(scaled, -1, keepdims=True)
            - normed * jnp.mean(scaled * normed, -1, keepdims=True)
        )
        middle_grad_ref[...] = middle_grad
        middle_low_ref[...] = middle_grad.astype(low)
        sums_ref[0:1, :] = jnp.sum(grad * normed, 0, keepdims=True)
        sums_ref[1:2, :] = jnp.sum(grad, 0, keepdims=True)
        sums_ref[2:3, :] = jnp.sum(middle_grad, 0, keepdims=True)
        sums_ref[3:4, :] = jnp.sum(out_grad, 0, keepdims=True)


def expand_call(name, body, half, rows, width, ins, extra_ins, extra_outs, scratch):
    packed = ins[2].shape
    low = jnp.bfloat16
    steps = packed[1] // 2
    full = whole_spec((rows, width))
    place = lambda i, half: steps * half[0] + i
    return pl.pallas_call(
        body,
        grid_spec=pltpu.PrefetchScalarGridSpec(
            num_scalar_prefetch=1,
            grid=(steps,),
            in_specs=[
                full,
                full,
                pl.BlockSpec(
                    (packed[0], 1, 1) + packed[3:], lambda i, half: (0, place(i, half), 0, 0, 0)
                ),
                pl.BlockSpec((1, width), lambda i, half: (0, place(i, half))),
                pl.BlockSpec(
                    (packed[0] // packed[1], packed[1], 1) + packed[3:],
                    lambda i, half: (place(i, half), 0, 1, 0, 0),
                ),
                *extra_ins,
            ],
            out_specs=[
                pl.BlockSpec((width, width), lambda i, half: (0, i)),
                pl.BlockSpec((width, width), lambda i, half: (i, 0)),
                pl.BlockSpec((1, width), lambda i, half: (0, i)),
                *(whole_spec(item.shape) for item in extra_outs),
            ],
            scratch_shapes=scratch,
        ),
        out_shape=[
            jax.ShapeDtypeStruct((width, steps * width), low),
            jax.ShapeDtypeStruct((steps * width, width), low),
            jax.ShapeDtypeStruct((1, steps * width), jnp.float32),
            *extra_outs,
        ],
        compiler_params=kernel_params(),
        cost_estimate=pl.CostEstimate(
            flops=12 * rows * width * width * steps,
            bytes_accessed=8 * width * width * steps + 16 * rows * width,
            transcendentals=2 * rows * width * steps,
        ),
        name=name,
    )(half, *ins)


def expand_first(half, hidden_two, out_low, packed, bias):
    rows, width = hidden_two.shape
    total = jax.ShapeDtypeStruct((rows, width), jnp.float32)
    return expand_call(
        "expand_first",
        first_body,
        half,
        rows,
        width,
        (hidden_two, out_low, packed, bias, packed),
        [],
        [total, total],
        [pltpu.VMEM((width, rows), jnp.bfloat16)],
    )


def expand_second(
    half,
    hidden_two,
    out_low,
    packed,
    bias,
    forward_part,
    back_part,
    middle,
    valid_rows,
    rows_in,
):
    rows, width = hidden_two.shape
    full = whole_spec((rows, width))
    total = pltpu.VMEM((rows, width), jnp.float32)
    return expand_call(
        "expand_second",
        second_body,
        half,
        rows,
        width,
        (
            hidden_two,
            out_low,
            packed,
            bias,
            packed,
            forward_part,
            back_part,
            middle,
            valid_rows,
            rows_in,
        ),
        [full, full, full, whole_spec(valid_rows.shape), whole_spec(rows_in.shape)],
        [
            jax.ShapeDtypeStruct((rows, width), jnp.bfloat16),
            jax.ShapeDtypeStruct((rows, width), jnp.float32),
            jax.ShapeDtypeStruct((rows, width), jnp.bfloat16),
            jax.ShapeDtypeStruct((4, width), jnp.float32),
        ],
        [total, total, pltpu.VMEM((width, rows), jnp.bfloat16)],
    )


def attend_back_body(
    project_ref,
    probs_ref,
    start_ref,
    middle_grad_ref,
    middle_low_ref,
    weight_ref,
    rows_ref,
    project_low_ref,
    conv_low_ref,
    sums_ref,
    third_ref,
    mixed_low,
):
    block_rows, width = start_ref.shape
    slots = 64
    low = jnp.bfloat16
    wide_out = weight_ref[:, 3].reshape(width, width)
    mixed_low[...] = dot_nt(middle_low_ref[...], wide_out).astype(low)
    lanes = lax.broadcasted_iota(jnp.int32, (slots, 128), 1)
    low_half = lanes < 64

    def fold(block):
        return jnp.where(low_half, block[:slots], block[slots:])

    for image in range(block_rows // slots):
        here = slice(image * slots, (image + 1) * slots)
        for pair in range(width // 128):
            at = pair * 128
            queries = project_ref[here, at : at + 128]
            keys = pair_stack(project_ref[here, width + at : width + at + 128], low_half)
            values = pair_stack(project_ref[here, 2 * width + at : 2 * width + at + 128], low_half)
            probs_low = probs_ref[here, at : at + 128]
            mixed = mixed_low[here, at : at + 128]
            probs = probs_low.astype(jnp.float32)
            prob_grad = dot_nt(mixed, values)
            value_grad = fold(dot_tn(probs_low, mixed))
            centre = half_reduce(prob_grad * probs, low_half, jnp.sum, 0.0)
            score_low = (probs * (prob_grad - centre)).astype(low)
            project_low_ref[here, at : at + 128] = (dot_nn(score_low, keys) * 0.125).astype(low)
            project_low_ref[here, width + at : width + at + 128] = (
                fold(dot_tn(score_low, queries)) * 0.125
            ).astype(low)
            project_low_ref[here, 2 * width + at : 2 * width + at + 128] = value_grad.astype(low)
    project_low = project_low_ref[...]
    grad = dot_nt(project_low[:, :width], weight_ref[:, 0].reshape(width, width))
    for third in (1, 2):
        at = third * width
        weight = weight_ref[:, third].reshape(width, width)
        grad = grad + dot_nt(project_low[:, at : at + width], weight)
    normed, inverse = norm_rows(start_ref[...], 1e-06)
    scaled = grad * rows_ref[0:1, :]
    start_grad = middle_grad_ref[...] + inverse * (
        scaled
        - jnp.mean(scaled, -1, keepdims=True)
        - normed * jnp.mean(scaled * normed, -1, keepdims=True)
    )
    conv_low_ref[...] = start_grad.astype(low)
    sums = jnp.concatenate(
        [
            jnp.sum(grad * normed, 0, keepdims=True),
            jnp.sum(grad, 0, keepdims=True),
            jnp.sum(start_grad, 0, keepdims=True),
        ],
        0,
    )
    third = jnp.sum(project_low.astype(jnp.float32), 0, keepdims=True)

    @pl.when(pl.program_id(0) == 0)
    def _():
        sums_ref[...] = sums
        third_ref[...] = third

    @pl.when(pl.program_id(0) > 0)
    def _():
        sums_ref[...] += sums
        third_ref[...] += third


def attend_back(
    project, probs_low, start, middle_grad, middle_low, weights, rows_in, block_rows
):
    rows, width = start.shape
    row_spec = lambda cols: pl.BlockSpec((block_rows, cols), lambda i: (i, 0))
    low = jnp.bfloat16
    return pl.pallas_call(
        attend_back_body,
        grid=(rows // block_rows,),
        in_specs=[
            row_spec(3 * width),
            row_spec(width),
            row_spec(width),
            row_spec(width),
            row_spec(width),
            whole_spec(weights.shape),
            whole_spec(rows_in.shape),
        ],
        out_specs=[
            row_spec(3 * width),
            row_spec(width),
            whole_spec((3, width)),
            whole_spec((1, 3 * width)),
        ],
        out_shape=[
            jax.ShapeDtypeStruct((rows, 3 * width), low),
            jax.ShapeDtypeStruct((rows, width), low),
            jax.ShapeDtypeStruct((3, width), jnp.float32),
            jax.ShapeDtypeStruct((1, 3 * width), jnp.float32),
        ],
        scratch_shapes=[pltpu.VMEM((block_rows, width), low)],
        compiler_params=kernel_params(),
        cost_estimate=pl.CostEstimate(
            flops=24 * rows * width * width,
            bytes_accessed=8 * width * width + 30 * rows * width,
            transcendentals=0,
        ),
        name="attend_back",
    )(project, probs_low, start, middle_grad, middle_low, weights, rows_in)


def dot_full(one, two, dims):
    return lax.dot_general(
        one, two, (dims, ((), ())), precision=highest, preferred_element_type=jnp.float32
    )


def hyper_rows(
    pick_rows,
    bias_mask,
    key_rows,
    hyper_project,
    hyper_output,
    hyper_gains,
    hyper_shifts,
    hyper_up,
    hyper_down,
):
    width = key_rows.shape[1]
    query_rows = dot_full(pick_rows, key_rows, ((1,), (0,)))
    queries = dot_full(query_rows, hyper_project[:, :width], ((1,), (0,)))
    keys_all = dot_full(key_rows, hyper_project[:, width : 2 * width], ((1,), (0,)))
    values_all = dot_full(key_rows, hyper_project[:, 2 * width :], ((1,), (0,)))
    head_size = width // HH
    head_of = lax.broadcasted_iota(jnp.int32, (1, width), 1) // head_size
    mixed_rows = jnp.zeros_like(query_rows)
    for head in range(HH):
        here = (head_of == head).astype(jnp.float32)
        scores = dot_full(queries * here, keys_all, ((1,), (1,))) * head_size ** (-0.5) + bias_mask
        peak = lax.stop_gradient(jnp.max(scores, -1, keepdims=True))
        weights = jnp.exp(scores - peak)
        weights = weights / jnp.sum(weights, -1, keepdims=True)
        mixed_rows = mixed_rows + dot_full(weights, values_all * here, ((1,), (0,)))

    def norm(values, index):
        center = values - jnp.mean(values, -1, keepdims=True)
        inverse = lax.rsqrt(jnp.mean(center * center, -1, keepdims=True) + 1e-05)
        gain = hyper_gains[index : index + 1, :]
        return center * inverse * gain + hyper_shifts[index : index + 1, :]

    hidden = norm(query_rows + dot_full(mixed_rows, hyper_output, ((1,), (0,))), 0)
    expand = dot_full(hidden, hyper_up, ((1,), (0,)))
    expanded = expand * (0.5 + 0.5 * lax.erf(expand * 0.7071067811865476))
    return norm(hidden + dot_full(expanded, hyper_down, ((1,), (0,))), 1)


def hyper_forward_body(*refs):
    refs[-1][...] = hyper_rows(*(ref[...].astype(jnp.float32) for ref in refs[:-1]))


def hyper_forward(pick_rows, bias_mask, key_rows, params):
    return pl.pallas_call(
        hyper_forward_body,
        out_shape=jax.ShapeDtypeStruct((pick_rows.shape[0], key_rows.shape[1]), jnp.float32),
        compiler_params=kernel_params(),
        name="hyper_forward",
    )(pick_rows, bias_mask, key_rows, *params)


def hyper_backward_body(count, pick_ref, mask_ref, key_ref, *refs):
    params = [ref[...].astype(jnp.float32) for ref in refs[:6]]
    feats_ref, conv_ref, matrix_ref = refs[6:9]
    key_out, *param_outs = refs[9:16]
    matrix_out, shift_out = refs[16:]
    conv = conv_ref[...] * scaler
    hidden, pull = jax.vjp(
        lambda *items: hyper_rows(pick_ref[...], mask_ref[...], *items), key_ref[...], *params
    )
    rows = count + conv.shape[0]
    bias_grad = dot_full(conv, matrix_ref[...].astype(jnp.float32), ((1,), (1,)))
    blank = jnp.zeros((hidden.shape[0] - rows, hidden.shape[1]), jnp.float32)
    grads = pull(jnp.concatenate([feats_ref[...], bias_grad, blank], 0))
    key_out[...] = grads[0]
    for out, grad in zip(param_outs, grads[1:]):
        out[...] = grad
    matrix_out[...] = dot_full(hidden[count:rows], conv, ((0,), (0,)))
    shift_out[...] = jnp.sum(conv, 0, keepdims=True)


def hyper_backward(pick_rows, bias_mask, key_rows, params, feats_grad, conv_grad, bias_weight):
    out = lambda item: jax.ShapeDtypeStruct(item.shape, jnp.float32)
    return pl.pallas_call(
        partial(hyper_backward_body, feats_grad.shape[0]),
        out_shape=[
            out(key_rows),
            *(out(item) for item in params),
            out(bias_weight),
            jax.ShapeDtypeStruct((1, bias_weight.shape[1]), jnp.float32),
        ],
        compiler_params=kernel_params(),
        name="hyper_backward",
    )(pick_rows, bias_mask, key_rows, *params, feats_grad, conv_grad, bias_weight)


def hyper_layout(weight_tokens, bias_token, wave_rows):
    group_count, band_count, width = wave_rows.shape
    tokens = weight_tokens.shape[0]
    waves = group_count * band_count
    key_count = -(-(tokens + waves + 1) // 16) * 16
    query_count = -(-(waves + group_count) // 8) * 8
    key_rows = jnp.concatenate(
        [
            weight_tokens.astype(jnp.float32),
            wave_rows.reshape(waves, width),
            bias_token.astype(jnp.float32)[None, :],
            jnp.zeros((key_count - tokens - waves - 1, width), jnp.float32),
        ],
        0,
    )
    query_id = np.arange(query_count)[:, None]
    key_id = np.arange(key_count)[None, :]
    source = np.where(query_id < waves, tokens + query_id, tokens + waves)
    pick_rows = (key_id == source) & (query_id < waves + group_count)
    query_group = np.where(query_id < waves, query_id // band_count, query_id - waves)
    key_group = (key_id - tokens) // band_count
    allowed = (
        (key_id < tokens)
        | (key_id == tokens + waves)
        | ((key_id < tokens + waves) & (key_group == query_group))
    )
    return (
        jnp.asarray(pick_rows.astype(np.float32)),
        jnp.asarray(np.where(allowed, 0.0, -1e30).astype(np.float32)),
        key_rows,
    )


def spread_eye(rows, copies):
    count, width = rows.shape
    iota = lambda shape, axis: lax.broadcasted_iota(jnp.int32, shape, axis)
    wide = (iota((width, width * copies), 1) // copies == iota((width, width * copies), 0)).astype(
        jnp.bfloat16
    )
    tall = (iota((count * copies, count), 0) // copies == iota((count * copies, count), 1)).astype(
        jnp.bfloat16
    )
    spread = dot_nn(tall, dot_nn(rows, wide).astype(jnp.bfloat16))
    same = iota(spread.shape, 0) % copies == iota(spread.shape, 1) % copies
    return jnp.where(same, spread, 0.0).astype(jnp.bfloat16)


def make_kernel_body(feats_ref, weight_ref, bias_ref, part_ref, spread_ref):
    bands, block, width = part_ref.shape
    hidden = weight_ref.shape[0]

    @pl.when(pl.program_id(0) == 0)
    def _():
        spread_ref[...] = spread_eye(feats_ref[...], block)

    product = dot_nn(spread_ref[...], weight_ref[...].reshape(hidden * block, width))
    product = product.reshape(-1, bands, block, width)
    bias = bias_ref[...].astype(jnp.float32)
    part_ref[...] = (scaler * (product[0] + product[1] + bias[None])).astype(part_ref.dtype)


def make_kernel(band_feats, kernel_weight, kernel_bias):
    bands = band_feats.shape[0]
    hidden, rows, width = kernel_weight.shape
    block = 16
    feats = split_low(band_feats, 2, 0)
    if rows % block:
        product = jnp.einsum(
            "sh,hpd->spd", feats, kernel_weight, preferred_element_type=jnp.float32
        )
        total = jnp.sum(product.reshape(2, bands, rows, width), 0)
        return (scaler * (total + kernel_bias.astype(jnp.float32))).astype(jnp.bfloat16)
    return pl.pallas_call(
        make_kernel_body,
        grid=(rows // block,),
        in_specs=[
            whole_spec(feats.shape),
            pl.BlockSpec((hidden, block, width), lambda i: (0, i, 0)),
            pl.BlockSpec((block, width), lambda i: (i, 0)),
        ],
        out_specs=pl.BlockSpec((bands, block, width), lambda i: (0, i, 0)),
        out_shape=jax.ShapeDtypeStruct((bands, rows, width), jnp.bfloat16),
        scratch_shapes=[pltpu.VMEM((2 * bands * block, hidden * block), jnp.bfloat16)],
        compiler_params=kernel_params(),
        name="make_kernel",
    )(feats, kernel_weight, kernel_bias)


def weight_grad_body(feats_ref, grad_ref, out_ref, spread_ref):
    hidden, block, width = out_ref.shape

    @pl.when(pl.program_id(0) == 0)
    def _():
        spread_ref[...] = spread_eye(feats_ref[...], block)

    grad = grad_ref[...].reshape(-1, width)
    out_ref[...] = dot_nn(spread_ref[...], grad).reshape(hidden, block, width)


def weight_grad(feats, kernel_all):
    count, rows, width = kernel_all.shape
    hidden = feats.shape[1]
    block = 16
    feats = (scaler * feats).astype(jnp.bfloat16)
    if rows % block:
        return jnp.einsum("sh,spd->hpd", feats, kernel_all, preferred_element_type=jnp.float32)
    table = feats.T
    return pl.pallas_call(
        weight_grad_body,
        grid=(rows // block,),
        in_specs=[
            whole_spec(table.shape),
            pl.BlockSpec((count, block, width), lambda i: (0, i, 0)),
        ],
        out_specs=pl.BlockSpec((hidden, block, width), lambda i: (0, i, 0)),
        out_shape=jax.ShapeDtypeStruct((hidden, rows, width), jnp.float32),
        scratch_shapes=[pltpu.VMEM((hidden * block, count * block), jnp.bfloat16)],
        compiler_params=kernel_params(),
        name="weight_grad",
    )(table, kernel_all)


def on_device(
    group_size,
    dp_size,
    pixels,
    patch_index,
    kept_count,
    wavelength,
    weight_tokens,
    bias_token,
    hyper_project,
    hyper_output,
    hyper_gains,
    hyper_shifts,
    hyper_up,
    hyper_down,
    kernel_weight,
    kernel_bias,
    bias_weight,
    bias_shift,
    attention_in,
    attention_out,
    expand_weight,
    reduce_weight,
    norm_gains,
    norm_shifts,
    attention_bias,
    output_bias,
    expand_bias,
    reduce_bias,
    cotangent,
):
    floaty = jnp.float32
    low = jnp.bfloat16
    links = Links(group_size, dp_size)
    image_count, slot_count, band_count, pixel_count = pixels.shape[1:]
    model_width = cotangent.shape[-1]
    row_count = image_count * slot_count
    widen = lambda item: item.astype(floaty)
    hyper_params = (
        hyper_project,
        hyper_output,
        hyper_gains,
        hyper_shifts,
        hyper_up,
        hyper_down,
    )

    feed = gather_feed(links, expand_weight, reduce_weight)
    piece = attention_piece(links, attention_in, attention_out)
    piece = piece.reshape((1, 1, 1, 1) + piece.shape)
    block = gather_line(links, piece, 0)
    wave_rows = wave_embed(wavelength[0])
    own_hidden = hyper_forward(
        *hyper_layout(weight_tokens, bias_token, wave_rows[None]), hyper_params
    )
    band_feats = own_hidden[:band_count] + wave_rows
    bias_feat = own_hidden[band_count]
    kernel_part = make_kernel(band_feats, kernel_weight, kernel_bias)
    chunk_count = 3
    chunk_bands = band_count // chunk_count
    depth = chunk_bands * pixel_count
    kernel_part, block, wavelength, bias_feat = stage(kernel_part, block, wavelength, bias_feat)
    chunks = [
        kernel_part[i * chunk_bands : (i + 1) * chunk_bands][:, None, None]
        for i in range(chunk_count)
    ]

    line_one = gather_line(links, chunks[0], 1)
    other = links.xside(block)
    all_waves = spread_group(links, wavelength[0])
    line_one, other, chunks, pixels, all_waves = stage(line_one, other, chunks, pixels, all_waves)
    block = pair_up(block, other, links.x, 1)

    line_one, block, chunks = stage(line_one, block, chunks)
    line_two = gather_line(links, chunks[1], 1)
    other_one = links.xside(line_one)
    other = links.yside(block)
    pixel_rows = pixels.reshape(row_count, band_count * pixel_count)
    line_two, other_one, other, chunks, pixel_rows, all_waves, bias_feat = stage(
        line_two, other_one, other, chunks, pixel_rows, all_waves, bias_feat
    )
    kernel_one = pair_up(line_one, other_one, links.x, 2).reshape(depth, model_width)
    block = pair_up(block, other, links.y, 2)

    line_two, block, kernel_one, chunks = stage(line_two, block, kernel_one, chunks)
    line_three = gather_line(links, chunks[2], 1)
    other_two = links.xside(line_two)
    other = links.core(block)
    valid_rows = (
        lax.broadcasted_iota(jnp.int32, (image_count, slot_count), 1) < kept_count[0][:, None]
    )
    valid_rows = valid_rows.reshape(row_count, 1).astype(floaty)
    out_low = cotangent.reshape(row_count, model_width) * valid_rows.astype(low)
    conv_bias = scaler * (
        jnp.dot(bias_feat, widen(bias_weight), precision=highest) + widen(bias_shift)
    )
    spots = place_spots(patch_index[0].reshape(row_count), 3)
    table = split_low(jnp.concatenate([place_table(model_width), conv_bias[None, :]], 0), 3, 0)
    table = jnp.pad(table, ((0, 128 - table.shape[0]), (0, 0)))
    embed_part = dot_nn(spots, table) + dot_nn(pixel_rows[:, :depth], kernel_one)
    line_three, other_two, other, embed_part, out_low, all_waves = stage(
        line_three, other_two, other, embed_part, out_low, all_waves
    )
    kernel_two = pair_up(line_two, other_two, links.x, 2).reshape(depth, model_width)
    weights = pair_up(block, other, links.c, 3).reshape(8, 4, -1, model_width)

    line_three, weights, kernel_two, all_waves = stage(line_three, weights, kernel_two, all_waves)
    other_three = links.xside(line_three)
    embed_part = embed_part + dot_nn(pixel_rows[:, depth : 2 * depth], kernel_two)
    wave_all = jax.vmap(wave_embed)(all_waves)
    pick_rows, bias_mask, key_rows = hyper_layout(weight_tokens, bias_token, wave_all)
    all_hidden = hyper_forward(pick_rows, bias_mask, key_rows, hyper_params)
    wave_count = group_size * band_count
    feats_all = all_hidden[:wave_count] + wave_all.reshape(wave_count, HE)
    other_three, embed_part, weights, feats_all = stage(
        other_three, embed_part, weights, feats_all
    )
    kernel_three = pair_up(line_three, other_three, links.x, 2).reshape(depth, model_width)

    gains = widen(norm_gains)
    shifts = widen(norm_shifts)
    start, hidden_one = embed_rows(
        embed_part, pixel_rows, kernel_three, jnp.stack([gains[0], shifts[0]]), 256
    )
    bias_full = jnp.concatenate(
        [widen(attention_bias[0]), jnp.zeros((model_width,), floaty), widen(attention_bias[1])]
    )[None, :]
    attended = attend_rows(
        0,
        6,
        None,
        kept_count[0],
        hidden_one,
        start,
        weights,
        bias_full,
        jnp.stack([widen(output_bias), gains[1], shifts[1]]),
    )
    project, probs_low, mixed_rows, middle, hidden_two = attended

    half_other = (1 - links.c).reshape(1)
    half_own = links.c.reshape(1)
    wide_bias = widen(expand_bias)[None, :]
    up_other, down_other, bias_other, forward_part, back_part = expand_first(
        half_other, hidden_two, out_low, feed, wide_bias
    )
    up_other, down_other, forward_part = stage(up_other, down_other, forward_part)
    up_other = links.core(up_other)
    down_other = links.core(down_other)
    up_own, down_own, bias_own, encoded, middle_grad, middle_low, sums_two = expand_second(
        half_own,
        hidden_two,
        out_low,
        feed,
        wide_bias,
        forward_part,
        back_part,
        middle,
        valid_rows,
        jnp.stack([widen(reduce_bias), gains[1]]),
    )
    encoded = encoded.reshape(cotangent.shape)
    up_other, down_other, up_own, down_own, middle_low = stage(
        up_other, down_other, up_own, down_own, middle_low
    )
    shard_rows = model_width // dp_size
    down_rows = reduce_weight.shape[0]
    up_shape = (links.line, 2, shard_rows, up_own.shape[1])
    up_sum = add_low(up_own.reshape(up_shape), up_other.reshape(up_shape))
    down_shape = (-1, 2, down_rows // 2, model_width)
    down_sum = add_low(down_own.reshape(down_shape), down_other.reshape(down_shape))

    send_up = pick(up_sum, 1 - links.x, 1)
    send_down = pick(down_sum, 1 - links.y, 1)
    send_up, send_down, middle_low = stage(send_up, send_down, middle_low)
    other_up = links.xside(send_up)
    other_down = links.yside(send_down)
    project_low, conv_low, sums_one, third_sums = attend_back(
        project, probs_low, start, middle_grad, middle_low, weights, gains[0:1], 256
    )
    other_up, other_down, conv_low, project_low = stage(
        other_up, other_down, conv_low, project_low
    )
    up_sum = add_low(pick(up_sum, links.x, 1), other_up).reshape(
        links.line, 2, shard_rows // 2, -1
    )
    down_sum = add_low(pick(down_sum, links.y, 1), other_down)

    send_up = pick(up_sum, 1 - links.y, 1)
    down_sum = down_sum.reshape(-1, 2, down_rows // 2, model_width)
    send_down = pick(down_sum, 1 - links.x, 1)
    send_up, send_down, conv_low = stage(send_up, send_down, conv_low)
    other_up = links.yside(send_up)
    other_down = links.xside(send_down)
    kernel_grad = contract_rows(pixel_rows, conv_low).astype(low)
    kernel_grad = kernel_grad.reshape(band_count, links.line, 2, -1, model_width)
    piece_count = 2
    piece_pixels = kernel_grad.shape[3] // piece_count
    piece_of = lambda i, side: pick(
        kernel_grad[:, :, :, i * piece_pixels : (i + 1) * piece_pixels], side, 2
    )
    sends = [piece_of(i, 1 - links.x) for i in range(piece_count)]
    small = jnp.concatenate(
        [
            sums_one[0:1],
            sums_two[0:1],
            sums_one[1:2],
            sums_two[1:2],
            third_sums[:, :model_width],
            third_sums[:, 2 * model_width :],
            sums_two[2:4],
            pair_up(bias_own, bias_other, links.c, 1).reshape(-1, model_width),
            sums_one[2:3],
        ],
        0,
    )
    other_up, other_down, sends, kernel_grad, small = stage(
        other_up, other_down, sends, kernel_grad, small
    )
    up_sum = add_low(pick(up_sum, links.y, 1), other_up)
    down_sum = add_low(pick(down_sum, links.x, 1), other_down)
    line_parts = lambda block: block.reshape(band_count, links.line, -1, model_width)
    finish_piece = lambda total: total.astype(low).reshape(band_count, -1, model_width)

    up_sum, sends, project_low, middle_low = stage(up_sum, sends, project_low, middle_low)
    other = links.xside(sends[0])
    up_total = reduce_line(links, up_sum, 0, links.zside).astype(low)
    grad_units = [
        contract_rows(hidden_one, project_low[:, i * model_width : (i + 1) * model_width])
        for i in range(3)
    ] + [contract_rows(mixed_rows, middle_low)]
    grad_units = [unit.astype(low) for unit in grad_units]
    units_of = lambda side: jnp.stack(
        [
            jnp.where(side == 0, grad_units[0], grad_units[1]),
            jnp.where(side == 0, grad_units[2], grad_units[3]),
        ]
    )
    send_units = units_of(1 - links.c)
    keep_units = units_of(links.c)
    other, up_total, send_units, keep_units, sends, small = stage(
        other, up_total, send_units, keep_units, sends, small
    )
    ready = line_parts(add_low(piece_of(0, links.x), other))

    ready, send_units, sends, small = stage(ready, send_units, sends, small)
    other = links.xside(sends[1])
    total_one = reduce_line(links, ready, 1, links.zside)
    other_units = links.core(send_units)
    small = small + links.zside(small, 1)
    wide_kernel = jnp.concatenate([kernel_one, kernel_two, kernel_three], 0)
    pixel_grad = dot_nt(conv_low, wide_kernel).astype(low)
    other, total_one, other_units, small, pixel_grad = stage(
        other, total_one, other_units, small, pixel_grad
    )
    units = add_low(keep_units, other_units)
    ready = line_parts(add_low(piece_of(1, links.x), other))
    pixel_grad = pixel_grad.reshape(pixels.shape)

    send_units = pick(units, 1 - links.y, 0)
    ready, send_units, down_sum, small = stage(ready, send_units, down_sum, small)
    total_two = reduce_line(links, ready, 1, links.zside)
    other_units = links.yside(send_units)
    step = 2
    while step < dp_size:
        small = small + links.zside(small, step)
        step *= 2
    total_two, other_units, small, down_sum = stage(total_two, other_units, small, down_sum)
    units = add_low(pick(units, links.y, 0), other_units)
    units = units.reshape(links.line, 2, shard_rows, model_width)
    kernel_low = jnp.concatenate([finish_piece(total) for total in (total_one, total_two)], 1)
    feats_part = scaler * jnp.einsum(
        "spd,hpd->sh", kernel_low, kernel_weight, preferred_element_type=floaty
    )

    send_units = pick(units, 1 - links.x, 1)
    send_units, down_sum, feats_part, kernel_low, small = stage(
        send_units, down_sum, feats_part, kernel_low, small
    )
    kernel_all = spread_group(links, kernel_low)
    other_units = links.xside(send_units)
    stride = 2
    while stride < dp_size // 2:
        bit = lax.axis_index("dp") // stride % 2
        down_sum = down_sum.reshape(-1, 2, down_rows // 2, model_width)
        other_down = links.zside(pick(down_sum, 1 - bit, 1), stride)
        down_sum = add_low(pick(down_sum, bit, 1), other_down)
        stride *= 2
    down_sum = down_sum.reshape(down_rows // 2, model_width)
    down_total = add_low(down_sum, links.owner_line(down_sum))
    conv_all = spread_group(links, small[-1:])
    small = small[:-1]
    small = small + links.core(small)
    small = small + links.yside(small)
    feats_grad = spread_group(links, sum_dp(links, feats_part)).reshape(-1, HE)
    units = add_low(pick(units, links.x, 1), other_units).reshape(links.line, shard_rows, -1)
    unit_total = reduce_line(links, units, 0, links.zside).astype(low)
    key_grad, *param_grads, bias_weight_grad, bias_shift_grad = hyper_backward(
        pick_rows,
        bias_mask,
        key_rows,
        hyper_params,
        feats_grad,
        conv_all.reshape(group_size, model_width),
        bias_weight,
    )
    token_count = weight_tokens.shape[0]
    kernel_all = kernel_all.reshape((wave_count,) + kernel_low.shape[1:])
    weight_shard_grad = weight_grad(feats_all, kernel_all)
    bias_shard_grad = scaler * jnp.sum(kernel_all.astype(floaty), 0)
    up_total = up_total.reshape(1, shard_rows // 2, -1)
    up_total = pair_up(up_total, links.yside(up_total), links.y, 0).reshape(shard_rows, -1)
    up_total = pair_up(up_total, links.core(up_total), links.c, 1)
    down_total = down_total.reshape(1, down_rows // 2, model_width)
    down_total = pair_up(down_total, links.yside(down_total), links.y, 0)
    down_other = links.owner_core(down_total)
    is_owner = lax.axis_index("dp") // (dp_size // 2) == links.c
    down_total = jnp.where(is_owner, down_total, down_other)
    unit_all = spread_group(links, unit_total.reshape(shard_rows, model_width))
    block_shards = (
        widen(jnp.concatenate([unit_all[i] for i in range(3)], 1)),
        widen(unit_all[3]),
        widen(up_total),
        widen(down_total.reshape(down_rows, model_width)),
    )
    return (
        encoded,
        pixel_grad,
        key_grad[:token_count],
        key_grad[token_count + wave_count],
        *param_grads,
        weight_shard_grad,
        bias_shard_grad,
        bias_weight_grad,
        bias_shift_grad.reshape(-1),
        *block_shards,
        small[0:2],
        small[2:4],
        small[4:6],
        small[6],
        small[8:].reshape(-1),
        small[7],
    )


def solution(mesh):
    placed = (
        P("group", "dp", None, None, None),
        P("group", "dp", None),
        P("group", "dp"),
        P("group", None),
        P(),
        P(),
        P(),
        P(),
        P(),
        P(),
        P(),
        P(),
        P(None, "dp", None),
        P("dp", None),
        P(),
        P(),
        P("dp", None),
        P("dp", None),
        P("dp", None),
        P("dp", None),
        P(),
        P(),
        P(),
        P(),
        P(),
        P(),
        P("group", "dp", None, None),
    )
    return jax.shard_map(
        partial(on_device, mesh.shape["group"], mesh.shape["dp"]),
        mesh=mesh,
        in_specs=placed,
        out_specs=(
            P("group", "dp", None, None),
            P("group", "dp", None, None, None),
            P(),
            P(),
            P(),
            P(),
            P(),
            P(),
            P(),
            P(),
            P(None, "dp", None),
            P("dp", None),
            P(),
            P(),
            P("dp", None),
            P("dp", None),
            P("dp", None),
            P("dp", None),
            P(),
            P(),
            P(),
            P(),
            P(),
            P(),
        ),
        check_vma=False,
    )
```

```python
from functools import partial

import jax
import jax.numpy as jnp
import numpy as np
from jax import lax
from jax.experimental import pallas as pl
from jax.experimental.pallas import tpu as pltpu
from jax.sharding import PartitionSpec as P

HE = 128
HH = 4
SIDE = 14


scaler = 0.01
highest = lax.Precision.HIGHEST


def contract_rows(operand, partner):
    return lax.dot_general(
        operand, partner, (((0,), (0,)), ((), ())), preferred_element_type=jnp.float32
    )


def wave_embed(wave_ids):
    half_width = HE // 2
    frequency = 1.0 / 10000.0 ** (jnp.arange(half_width, dtype=jnp.float32) / half_width)
    angles = wave_ids.astype(jnp.float32)[:, None] * frequency
    return jnp.concatenate([jnp.sin(angles), jnp.cos(angles)], -1)


def place_table(model_width):
    quarter = model_width // 4
    frequency = 1.0 / 10000.0 ** (jnp.arange(quarter, dtype=jnp.float32) / quarter)
    angle = jnp.arange(SIDE, dtype=jnp.float32)[:, None] * frequency
    waves = jnp.concatenate([jnp.sin(angle), jnp.cos(angle)], -1)
    blank = jnp.zeros_like(waves)
    return jnp.concatenate(
        [jnp.concatenate([waves, blank], -1), jnp.concatenate([blank, waves], -1)], 0
    )


def place_spots(patch_ids, copies):
    lanes = jnp.arange(128, dtype=jnp.int32)[None, :]
    spot = lanes % (2 * SIDE + 1)
    row_id = (patch_ids // SIDE)[:, None]
    col_id = (patch_ids % SIDE)[:, None] + SIDE
    hit = (spot == row_id) | (spot == col_id) | (spot == 2 * SIDE)
    return (hit & (lanes < copies * (2 * SIDE + 1))).astype(jnp.bfloat16)


def split_low(values, count, axis):
    pieces = []
    for _ in range(count):
        piece = values.astype(jnp.bfloat16)
        pieces.append(piece)
        values = values - piece.astype(jnp.float32)
    return jnp.concatenate(pieces, axis)


def stage(*values):
    return lax.optimization_barrier(values)


class Links:
    def __init__(self, group_size, dp_size):
        self.group_size = group_size
        self.dp_size = dp_size
        group_id = lax.axis_index("group")
        dp_id = lax.axis_index("dp")
        self.y = group_id // 2
        self.c = group_id % 2
        self.x = dp_id % 2
        self.digits = []
        stride = 2
        while stride < dp_size:
            size = min(4, dp_size // stride)
            self.digits.insert(0, (size, stride, dp_id // stride % size))
            stride *= size
        self.line = dp_size // 2
        self.z = dp_id // 2

    def core(self, block):
        return lax.ppermute(block, "group", [(i, i ^ 1) for i in range(self.group_size)])

    def yside(self, block):
        return lax.ppermute(block, "group", [(i, i ^ 2) for i in range(self.group_size)])

    def xside(self, block):
        return lax.ppermute(block, "dp", [(i, i ^ 1) for i in range(self.dp_size)])

    def zside(self, block, step):
        return lax.ppermute(block, "dp", [(i, i ^ step) for i in range(self.dp_size)])

    def owner_pairs(self, target_of):
        pairs = []
        for group_id in range(self.group_size):
            for dp_id in range(self.dp_size):
                target = target_of(group_id, dp_id)
                if target is not None:
                    pairs.append(
                        (group_id * self.dp_size + dp_id, target[0] * self.dp_size + target[1])
                    )
        return pairs

    def owner_line(self, block):
        top = self.dp_size // 2
        pairs = self.owner_pairs(lambda g, d: (g, d ^ top) if d // top != g % 2 else None)
        return lax.ppermute(block, ("group", "dp"), pairs)

    def owner_core(self, block):
        top = self.dp_size // 2
        pairs = self.owner_pairs(lambda g, d: (g ^ 1, d) if d // top == g % 2 else None)
        return lax.ppermute(block, ("group", "dp"), pairs)


def pick(block, index, axis, count=1):
    return lax.dynamic_slice_in_dim(block, index, count, axis)


def add_low(*items):
    total = items[0].astype(jnp.float32)
    for item in items[1:]:
        total = total + item.astype(jnp.float32)
    return total.astype(jnp.bfloat16)


def pair_up(block, other, bit, axis):
    return jnp.where(
        bit == 0,
        jnp.concatenate([block, other], axis),
        jnp.concatenate([other, block], axis),
    )


def place_digit(block, received, me, axis):
    size = len(received) + 1
    shape = block.shape[:axis] + (size,) + block.shape[axis + 1 :]
    out = jnp.zeros(shape, block.dtype)
    for step, piece in zip(range(size), [block] + received):
        at = tuple(me ^ step if i == axis else 0 for i in range(len(shape)))
        out = lax.dynamic_update_slice(out, piece, at)
    return out


def gather_line(links, piece, axis):
    lead, tail = piece.shape[:axis], piece.shape[axis + 1 :]
    count = len(links.digits)
    block = piece.reshape(lead + (1,) * count + tail)
    for place, (size, stride, me) in reversed(list(enumerate(links.digits))):
        received = [links.zside(block, stride * step) for step in range(1, size)]
        block = place_digit(block, received, me, axis + place)
    return block.reshape(lead + (links.line,) + tail)


def send_line(links, block, axis, sender):
    lead, tail = block.shape[:axis], block.shape[axis + 1 :]
    block = block.reshape(lead + tuple(size for size, _, _ in links.digits) + tail)
    for place, (size, stride, me) in enumerate(links.digits):
        if place:
            block = add_low(*terms)
        terms = [pick(block, me, axis + place)] + [
            sender(pick(block, me ^ step, axis + place), stride * step) for step in range(1, size)
        ]
    return [term.reshape(lead + tail) for term in terms]


def attention_piece(links, attention_in, attention_out):
    width = attention_out.shape[1]
    thirds = [attention_in[:, i * width : (i + 1) * width] for i in range(3)]
    return lax.dynamic_index_in_dim(
        jnp.stack(thirds + [attention_out]), lax.axis_index("group"), 0, False
    )


def gather_feed(links, expand_weight, reduce_weight):
    width = reduce_weight.shape[1]
    count = links.group_size
    group_id = lax.axis_index("group")
    up = pick(expand_weight, group_id * width, 1, width)
    rows = reduce_weight.shape[0] // count
    down = pick(reduce_weight, group_id * rows, 0, rows)
    wide = lax.all_gather(jnp.stack([up, down]), ("dp", "group"), axis=0)
    wide = wide.reshape(links.dp_size, count, 2, rows, width)
    if rows % 16:
        up = wide[:, :, 0].transpose(1, 0, 2, 3).reshape(count, 8, width // 8, width)
        down = wide[:, :, 1].reshape(8, count, width // 8, width)
        wide = jnp.stack([up.transpose(1, 0, 2, 3), down], 2)
    return wide


def spread_group(links, piece):
    piece = piece.reshape((1, 1) + piece.shape)
    piece = pair_up(piece, links.yside(piece), links.y, 0)
    piece = pair_up(piece, links.core(piece), links.c, 1)
    return piece.reshape((-1,) + piece.shape[2:])


def sum_dp(links, values):
    step = 1
    while step < links.dp_size:
        values = values + links.zside(values, step)
        step *= 2
    return values


VMEM_BYTES = 60 * 1024 * 1024


def kernel_params():
    return pltpu.CompilerParams(vmem_limit_bytes=VMEM_BYTES)


def whole_spec(shape):
    return pl.BlockSpec(shape, lambda *_: (0,) * len(shape))


def norm_rows(values, epsilon):
    center = values - jnp.mean(values, -1, keepdims=True)
    inverse = lax.rsqrt(jnp.mean(center * center, -1, keepdims=True) + epsilon)
    return center * inverse, inverse


def dot_nn(one, two):
    return lax.dot_general(one, two, (((1,), (0,)), ((), ())), preferred_element_type=jnp.float32)


def dot_nt(one, two):
    return lax.dot_general(one, two, (((1,), (1,)), ((), ())), preferred_element_type=jnp.float32)


def dot_tn(one, two):
    return lax.dot_general(one, two, (((0,), (0,)), ((), ())), preferred_element_type=jnp.float32)


def embed_body(part_ref, pixel_ref, kernel_ref, norm_ref, start_ref, hidden_ref):
    start = part_ref[...] + dot_nn(pixel_ref[...], kernel_ref[...])
    start_ref[...] = start
    normed, _ = norm_rows(start, 1e-06)
    hidden_ref[...] = (normed * norm_ref[0:1, :] + norm_ref[1:2, :]).astype(jnp.bfloat16)


def embed_rows(part, pixel_rows, wide_kernel, norm_one, block_rows):
    rows = part.shape[0]
    depth = wide_kernel.shape[0]
    last = pixel_rows.shape[1] // depth - 1
    width = wide_kernel.shape[1]
    row_spec = lambda cols: pl.BlockSpec((block_rows, cols), lambda i: (i, 0))
    return pl.pallas_call(
        embed_body,
        grid=(rows // block_rows,),
        in_specs=[
            row_spec(width),
            pl.BlockSpec((block_rows, depth), lambda i: (i, last)),
            whole_spec(wide_kernel.shape),
            whole_spec(norm_one.shape),
        ],
        out_specs=[row_spec(width), row_spec(width)],
        out_shape=[
            jax.ShapeDtypeStruct((rows, width), jnp.float32),
            jax.ShapeDtypeStruct((rows, width), jnp.bfloat16),
        ],
        compiler_params=kernel_params(),
        cost_estimate=pl.CostEstimate(
            flops=2 * rows * depth * width,
            bytes_accessed=2 * (rows * depth + depth * width) + 6 * rows * width,
            transcendentals=0,
        ),
        name="embed_rows",
    )(part, pixel_rows, wide_kernel, norm_one)


def pixel_grad_body(grad_ref, kernel_ref, out_ref, *wide_refs):
    rows, bands, depth = out_ref.shape
    padded = wide_refs[0].shape[0] // rows
    for band in range(bands):
        part = dot_nt(grad_ref[...], kernel_ref[band * depth : (band + 1) * depth, :])
        for place, ref in enumerate(wide_refs):
            ref[pl.ds(band, rows, stride=padded), :] = part[:, place * 128 : (place + 1) * 128]
    for place, ref in enumerate(wide_refs):
        wide = ref[...].reshape(rows, padded, 128)
        out_ref[:, :, place * 128 : (place + 1) * 128] = wide[:, :bands].astype(out_ref.dtype)


def pixel_gradient(conv_low, wide_kernel, bands):
    rows, width = conv_low.shape
    depth = wide_kernel.shape[0] // bands
    block_rows = 128
    padded = -(-bands // 8) * 8
    return pl.pallas_call(
        pixel_grad_body,
        grid=(rows // block_rows,),
        in_specs=[
            pl.BlockSpec((block_rows, width), lambda i: (i, 0)),
            whole_spec(wide_kernel.shape),
        ],
        out_specs=pl.BlockSpec((block_rows, bands, depth), lambda i: (i, 0, 0)),
        out_shape=jax.ShapeDtypeStruct((rows, bands, depth), jnp.bfloat16),
        scratch_shapes=[pltpu.VMEM((block_rows * padded, 128), jnp.float32)] * (depth // 128),
        compiler_params=kernel_params(),
        cost_estimate=pl.CostEstimate(
            flops=2 * rows * width * bands * depth,
            bytes_accessed=4 * bands * depth * (width + rows),
            transcendentals=0,
        ),
        name="pixel_gradient",
    )(conv_low, wide_kernel)


def pair_stack(block, low_half):
    zero = jnp.zeros_like(block)
    return jnp.concatenate(
        [jnp.where(low_half, block, zero), jnp.where(low_half, zero, block)], 0
    )


def half_reduce(values, low_half, reducer, filler):
    first = reducer(jnp.where(low_half, values, filler), -1, keepdims=True)
    second = reducer(jnp.where(low_half, filler, values), -1, keepdims=True)
    return jnp.where(low_half, first, second)


def attend_body(
    first,
    count_ref,
    hidden_ref,
    start_ref,
    weight_ref,
    bias_ref,
    rows_ref,
    project_ref,
    probs_ref,
    mixed_ref,
    middle_ref,
    hidden_two_ref,
    score_ref,
):
    block_rows, width = hidden_ref.shape
    slots = 64
    images = block_rows // slots
    base = (pl.program_id(0) + first) * images
    for third in range(3):
        at = third * width
        weight = weight_ref[:, third].reshape(width, width)
        project_ref[:, at : at + width] = (
            dot_nn(hidden_ref[...], weight) + bias_ref[:, at : at + width]
        ).astype(jnp.bfloat16)
    lanes = lax.broadcasted_iota(jnp.int32, (slots, 128), 1)
    low_half = lanes < 64
    key_id = jnp.where(low_half, lanes, lanes - 64)
    pairs = width // 128
    blocks = [(image, pair) for image in range(images) for pair in range(pairs)]
    for place, (image, pair) in enumerate(blocks):
        here = slice(image * slots, (image + 1) * slots)
        at = pair * 128
        queries = project_ref[here, at : at + 128]
        keys = pair_stack(project_ref[here, width + at : width + at + 128], low_half)
        keep = key_id < count_ref[base + image]
        score_ref[place * slots : (place + 1) * slots, :] = jnp.where(
            keep, dot_nt(queries, keys) * 0.125, -1000000000.0
        )
    for image in range(images):
        here = slice(image * pairs * slots, (image + 1) * pairs * slots)
        scores = score_ref[here, :]
        wide_half = lax.broadcasted_iota(jnp.int32, scores.shape, 1) < 64
        probs = jnp.exp(scores - half_reduce(scores, wide_half, jnp.max, -3e38))
        score_ref[here, :] = probs / half_reduce(probs, wide_half, jnp.sum, 0.0)
    for place, (image, pair) in enumerate(blocks):
        here = slice(image * slots, (image + 1) * slots)
        at = pair * 128
        values = pair_stack(project_ref[here, 2 * width + at : 2 * width + at + 128], low_half)
        probs_low = score_ref[place * slots : (place + 1) * slots, :].astype(jnp.bfloat16)
        probs_ref[here, at : at + 128] = probs_low
        mixed_ref[here, at : at + 128] = dot_nn(probs_low, values).astype(jnp.bfloat16)
    middle = start_ref[...] + dot_nn(mixed_ref[...], weight_ref[:, 3].reshape(width, width)) + rows_ref[0:1, :]
    middle_ref[...] = middle
    normed, _ = norm_rows(middle, 1e-06)
    hidden_two_ref[...] = (normed * rows_ref[1:2, :] + rows_ref[2:3, :]).astype(jnp.bfloat16)


def attend_rows(first, steps, earlier, counts, hidden_one, start, weights, bias_full, rows_in):
    rows, width = hidden_one.shape
    block_rows = 128
    row_spec = lambda cols: pl.BlockSpec((block_rows, cols), lambda i, *_: (i + first, 0))
    low = jnp.bfloat16
    keep = list(earlier or ())

    def body(count_ref, *refs):
        refs = refs[:5] + refs[5 + len(keep) :]
        attend_body(first, count_ref, *refs)

    return pl.pallas_call(
        body,
        grid_spec=pltpu.PrefetchScalarGridSpec(
            num_scalar_prefetch=1,
            grid=(steps,),
            in_specs=[
                row_spec(width),
                row_spec(width),
                whole_spec(weights.shape),
                whole_spec(bias_full.shape),
                whole_spec(rows_in.shape),
                *(pl.BlockSpec(memory_space=pl.ANY) for _ in keep),
            ],
            out_specs=[
                row_spec(3 * width),
                row_spec(width),
                row_spec(width),
                row_spec(width),
                row_spec(width),
            ],
            scratch_shapes=[pltpu.VMEM((block_rows * width // 128, 128), jnp.float32)],
        ),
        out_shape=[
            jax.ShapeDtypeStruct((rows, 3 * width), low),
            jax.ShapeDtypeStruct((rows, width), low),
            jax.ShapeDtypeStruct((rows, width), low),
            jax.ShapeDtypeStruct((rows, width), jnp.float32),
            jax.ShapeDtypeStruct((rows, width), low),
        ],
        input_output_aliases={6 + i: i for i in range(len(keep))},
        compiler_params=kernel_params(),
        cost_estimate=pl.CostEstimate(
            flops=16 * steps * block_rows * width * width,
            bytes_accessed=8 * width * width + 20 * steps * block_rows * width,
            transcendentals=rows * width,
        ),
        name="attend_rows",
    )(counts, hidden_one, start, weights, bias_full, rows_in, *keep)


def expand_step(hidden_ref, turned_ref, out_ref, up_ref, bias_ref, down_ref):
    low = jnp.bfloat16
    out_low = out_ref[...]
    width = out_low.shape[1]
    up = up_ref[...].reshape(width, -1)
    down = down_ref[...].reshape(-1, width)
    pre = dot_nn(hidden_ref[...], up) + bias_ref[...]
    cumulative = 0.5 + 0.5 * lax.erf(pre * 0.7071067811865476)
    slope = cumulative + pre * (jnp.exp(pre * pre * -0.5) * 0.3989422804014327)
    activated = (pre * cumulative).astype(low)
    pre_grad = dot_nt(out_low, down) * slope
    pre_low = pre_grad.astype(low)
    return (
        jnp.sum(pre_grad, 0, keepdims=True),
        dot_nn(activated, down),
        dot_nt(pre_low, up),
        dot_nn(turned_ref[...], pre_low),
        dot_tn(activated, out_low),
    )


def accumulate(ref, part):
    @pl.when(pl.program_id(0) == 0)
    def _():
        ref[...] = part

    @pl.when(pl.program_id(0) > 0)
    def _():
        ref[...] += part


def first_body(
    half_ref,
    hidden_ref,
    out_ref,
    up_ref,
    bias_ref,
    down_ref,
    grad_up_ref,
    grad_down_ref,
    bias_grad_ref,
    forward_ref,
    back_ref,
    turned_ref,
):
    @pl.when(pl.program_id(0) == 0)
    def _():
        turned_ref[...] = hidden_ref[...].T

    bias_grad, forward_part, back_part, grad_up, grad_down = expand_step(
        hidden_ref, turned_ref, out_ref, up_ref, bias_ref, down_ref
    )
    bias_grad_ref[...] = bias_grad
    grad_up_ref[...] = grad_up.astype(jnp.bfloat16)
    grad_down_ref[...] = grad_down.astype(jnp.bfloat16)
    accumulate(forward_ref, forward_part)
    accumulate(back_ref, back_part)


def second_body(
    half_ref,
    hidden_ref,
    out_ref,
    up_ref,
    bias_ref,
    down_ref,
    forward_ref,
    back_ref,
    middle_ref,
    valid_ref,
    rows_ref,
    grad_up_ref,
    grad_down_ref,
    bias_grad_ref,
    encoded_ref,
    middle_grad_ref,
    middle_low_ref,
    sums_ref,
    forward_acc,
    back_acc,
    turned_ref,
):
    step = pl.program_id(0)
    low = jnp.bfloat16

    @pl.when(step == 0)
    def _():
        turned_ref[...] = hidden_ref[...].T
        forward_acc[...] = forward_ref[...]
        back_acc[...] = back_ref[...]

    bias_grad, forward_part, back_part, grad_up, grad_down = expand_step(
        hidden_ref, turned_ref, out_ref, up_ref, bias_ref, down_ref
    )
    bias_grad_ref[...] = bias_grad
    grad_up_ref[...] = grad_up.astype(low)
    grad_down_ref[...] = grad_down.astype(low)
    forward_acc[...] += forward_part
    back_acc[...] += back_part

    @pl.when(step == pl.num_programs(0) - 1)
    def _():
        middle = middle_ref[...]
        encoded_ref[...] = (
            (middle + forward_acc[...] + rows_ref[0:1, :]) * valid_ref[...]
        ).astype(low)
        normed, inverse = norm_rows(middle, 1e-06)
        grad = back_acc[...]
        out_grad = out_ref[...].astype(jnp.float32)
        scaled = grad * rows_ref[1:2, :]
        middle_grad = out_grad + inverse * (
            scaled
            - jnp.mean(scaled, -1, keepdims=True)
            - normed * jnp.mean(scaled * normed, -1, keepdims=True)
        )
        middle_grad_ref[...] = middle_grad
        middle_low_ref[...] = middle_grad.astype(low)
        sums_ref[0:1, :] = jnp.sum(grad * normed, 0, keepdims=True)
        sums_ref[1:2, :] = jnp.sum(grad, 0, keepdims=True)
        sums_ref[2:3, :] = jnp.sum(middle_grad, 0, keepdims=True)
        sums_ref[3:4, :] = jnp.sum(out_grad, 0, keepdims=True)


def expand_call(name, body, half, rows, width, ins, extra_ins, extra_outs, scratch):
    packed = ins[2].shape
    low = jnp.bfloat16
    steps = packed[1] // 2
    full = whole_spec((rows, width))
    place = lambda i, half: steps * half[0] + i
    return pl.pallas_call(
        body,
        grid_spec=pltpu.PrefetchScalarGridSpec(
            num_scalar_prefetch=1,
            grid=(steps,),
            in_specs=[
                full,
                full,
                pl.BlockSpec(
                    (packed[0], 1, 1) + packed[3:], lambda i, half: (0, place(i, half), 0, 0, 0)
                ),
                pl.BlockSpec((1, width), lambda i, half: (0, place(i, half))),
                pl.BlockSpec(
                    (packed[0] // packed[1], packed[1], 1) + packed[3:],
                    lambda i, half: (place(i, half), 0, 1, 0, 0),
                ),
                *extra_ins,
            ],
            out_specs=[
                pl.BlockSpec((width, width), lambda i, half: (0, i)),
                pl.BlockSpec((width, width), lambda i, half: (i, 0)),
                pl.BlockSpec((1, width), lambda i, half: (0, i)),
                *(whole_spec(item.shape) for item in extra_outs),
            ],
            scratch_shapes=scratch,
        ),
        out_shape=[
            jax.ShapeDtypeStruct((width, steps * width), low),
            jax.ShapeDtypeStruct((steps * width, width), low),
            jax.ShapeDtypeStruct((1, steps * width), jnp.float32),
            *extra_outs,
        ],
        compiler_params=kernel_params(),
        cost_estimate=pl.CostEstimate(
            flops=12 * rows * width * width * steps,
            bytes_accessed=8 * width * width * steps + 16 * rows * width,
            transcendentals=2 * rows * width * steps,
        ),
        name=name,
    )(half, *ins)


def expand_first(half, hidden_two, out_low, packed, bias):
    rows, width = hidden_two.shape
    total = jax.ShapeDtypeStruct((rows, width), jnp.float32)
    return expand_call(
        "expand_first",
        first_body,
        half,
        rows,
        width,
        (hidden_two, out_low, packed, bias, packed),
        [],
        [total, total],
        [pltpu.VMEM((width, rows), jnp.bfloat16)],
    )


def expand_second(
    half,
    hidden_two,
    out_low,
    packed,
    bias,
    forward_part,
    back_part,
    middle,
    valid_rows,
    rows_in,
):
    rows, width = hidden_two.shape
    full = whole_spec((rows, width))
    total = pltpu.VMEM((rows, width), jnp.float32)
    return expand_call(
        "expand_second",
        second_body,
        half,
        rows,
        width,
        (
            hidden_two,
            out_low,
            packed,
            bias,
            packed,
            forward_part,
            back_part,
            middle,
            valid_rows,
            rows_in,
        ),
        [full, full, full, whole_spec(valid_rows.shape), whole_spec(rows_in.shape)],
        [
            jax.ShapeDtypeStruct((rows, width), jnp.bfloat16),
            jax.ShapeDtypeStruct((rows, width), jnp.float32),
            jax.ShapeDtypeStruct((rows, width), jnp.bfloat16),
            jax.ShapeDtypeStruct((4, width), jnp.float32),
        ],
        [total, total, pltpu.VMEM((width, rows), jnp.bfloat16)],
    )


def attend_back_body(
    project_ref,
    probs_ref,
    start_ref,
    middle_grad_ref,
    middle_low_ref,
    weight_ref,
    rows_ref,
    project_low_ref,
    conv_low_ref,
    sums_ref,
    third_ref,
    mixed_low,
    grad_ref,
):
    block_rows, width = start_ref.shape
    slots = 64
    low = jnp.bfloat16
    wide_out = weight_ref[:, 3].reshape(width, width)
    mixed_low[...] = dot_nt(middle_low_ref[...], wide_out).astype(low)
    lanes = lax.broadcasted_iota(jnp.int32, (slots, 128), 1)
    low_half = lanes < 64

    def fold(block):
        return jnp.where(low_half, block[:slots], block[slots:])

    pairs = width // 128
    images = block_rows // slots
    blocks = [(image, pair) for image in range(images) for pair in range(pairs)]
    for place, (image, pair) in enumerate(blocks):
        here = slice(image * slots, (image + 1) * slots)
        at = pair * 128
        values = pair_stack(project_ref[here, 2 * width + at : 2 * width + at + 128], low_half)
        mixed = mixed_low[here, at : at + 128]
        grad_ref[place * slots : (place + 1) * slots, :] = dot_nt(mixed, values)
        project_low_ref[here, 2 * width + at : 2 * width + at + 128] = fold(
            dot_tn(probs_ref[here, at : at + 128], mixed)
        ).astype(low)
    for image in range(images):
        rows = slice(image * slots, (image + 1) * slots)
        probs = jnp.concatenate(
            [probs_ref[rows, pair * 128 : (pair + 1) * 128] for pair in range(pairs)], 0
        ).astype(jnp.float32)
        here = slice(image * pairs * slots, (image + 1) * pairs * slots)
        prob_grad = grad_ref[here, :]
        wide_half = lax.broadcasted_iota(jnp.int32, prob_grad.shape, 1) < 64
        centre = half_reduce(prob_grad * probs, wide_half, jnp.sum, 0.0)
        grad_ref[here, :] = probs * (prob_grad - centre)
    for place, (image, pair) in enumerate(blocks):
        here = slice(image * slots, (image + 1) * slots)
        at = pair * 128
        queries = project_ref[here, at : at + 128]
        keys = pair_stack(project_ref[here, width + at : width + at + 128], low_half)
        score_low = grad_ref[place * slots : (place + 1) * slots, :].astype(low)
        project_low_ref[here, at : at + 128] = (dot_nn(score_low, keys) * 0.125).astype(low)
        project_low_ref[here, width + at : width + at + 128] = (
            fold(dot_tn(score_low, queries)) * 0.125
        ).astype(low)
    project_low = project_low_ref[...]
    grad = dot_nt(project_low[:, :width], weight_ref[:, 0].reshape(width, width))
    for third in (1, 2):
        at = third * width
        weight = weight_ref[:, third].reshape(width, width)
        grad = grad + dot_nt(project_low[:, at : at + width], weight)
    normed, inverse = norm_rows(start_ref[...], 1e-06)
    scaled = grad * rows_ref[0:1, :]
    start_grad = middle_grad_ref[...] + inverse * (
        scaled
        - jnp.mean(scaled, -1, keepdims=True)
        - normed * jnp.mean(scaled * normed, -1, keepdims=True)
    )
    conv_low_ref[...] = start_grad.astype(low)
    sums = jnp.concatenate(
        [
            jnp.sum(grad * normed, 0, keepdims=True),
            jnp.sum(grad, 0, keepdims=True),
            jnp.sum(start_grad, 0, keepdims=True),
        ],
        0,
    )
    third = jnp.sum(project_low.astype(jnp.float32), 0, keepdims=True)

    @pl.when(pl.program_id(0) == 0)
    def _():
        sums_ref[...] = sums
        third_ref[...] = third

    @pl.when(pl.program_id(0) > 0)
    def _():
        sums_ref[...] += sums
        third_ref[...] += third


def attend_back(
    project, probs_low, start, middle_grad, middle_low, weights, rows_in, block_rows
):
    rows, width = start.shape
    row_spec = lambda cols: pl.BlockSpec((block_rows, cols), lambda i: (i, 0))
    low = jnp.bfloat16
    return pl.pallas_call(
        attend_back_body,
        grid=(rows // block_rows,),
        in_specs=[
            row_spec(3 * width),
            row_spec(width),
            row_spec(width),
            row_spec(width),
            row_spec(width),
            whole_spec(weights.shape),
            whole_spec(rows_in.shape),
        ],
        out_specs=[
            row_spec(3 * width),
            row_spec(width),
            whole_spec((3, width)),
            whole_spec((1, 3 * width)),
        ],
        out_shape=[
            jax.ShapeDtypeStruct((rows, 3 * width), low),
            jax.ShapeDtypeStruct((rows, width), low),
            jax.ShapeDtypeStruct((3, width), jnp.float32),
            jax.ShapeDtypeStruct((1, 3 * width), jnp.float32),
        ],
        scratch_shapes=[
            pltpu.VMEM((block_rows, width), low),
            pltpu.VMEM((block_rows * width // 128, 128), jnp.float32),
        ],
        compiler_params=kernel_params(),
        cost_estimate=pl.CostEstimate(
            flops=24 * rows * width * width,
            bytes_accessed=8 * width * width + 30 * rows * width,
            transcendentals=0,
        ),
        name="attend_back",
    )(project, probs_low, start, middle_grad, middle_low, weights, rows_in)


def dot_full(one, two, dims, precision=highest):
    return lax.dot_general(
        one, two, (dims, ((), ())), precision=precision, preferred_element_type=jnp.float32
    )


def hyper_rows(
    precision,
    pick_rows,
    bias_mask,
    key_rows,
    hyper_project,
    hyper_output,
    hyper_gains,
    hyper_shifts,
    hyper_up,
    hyper_down,
):
    width = key_rows.shape[1]
    query_rows = dot_full(pick_rows, key_rows, ((1,), (0,)))
    queries = dot_full(query_rows, hyper_project[:, :width], ((1,), (0,)), precision)
    keys_all = dot_full(key_rows, hyper_project[:, width : 2 * width], ((1,), (0,)), precision)
    values_all = dot_full(key_rows, hyper_project[:, 2 * width :], ((1,), (0,)), precision)
    head_size = width // HH
    head_of = lax.broadcasted_iota(jnp.int32, (1, width), 1) // head_size
    mixed_rows = jnp.zeros_like(query_rows)
    for head in range(HH):
        here = (head_of == head).astype(jnp.float32)
        scores = dot_full(queries * here, keys_all, ((1,), (1,)), precision) * head_size ** (-0.5) + bias_mask
        peak = lax.stop_gradient(jnp.max(scores, -1, keepdims=True))
        weights = jnp.exp(scores - peak)
        weights = weights / jnp.sum(weights, -1, keepdims=True)
        mixed_rows = mixed_rows + dot_full(weights, values_all * here, ((1,), (0,)), precision)

    def norm(values, index):
        center = values - jnp.mean(values, -1, keepdims=True)
        inverse = lax.rsqrt(jnp.mean(center * center, -1, keepdims=True) + 1e-05)
        gain = hyper_gains[index : index + 1, :]
        return center * inverse * gain + hyper_shifts[index : index + 1, :]

    hidden = norm(query_rows + dot_full(mixed_rows, hyper_output, ((1,), (0,)), precision), 0)
    expand = dot_full(hidden, hyper_up, ((1,), (0,)), precision)
    expanded = expand * (0.5 + 0.5 * lax.erf(expand * 0.7071067811865476))
    return norm(hidden + dot_full(expanded, hyper_down, ((1,), (0,)), precision), 1)


def hyper_forward_body(*refs):
    refs[-1][...] = hyper_rows(highest, *(ref[...].astype(jnp.float32) for ref in refs[:-1]))


def hyper_forward(pick_rows, bias_mask, key_rows, params):
    return pl.pallas_call(
        hyper_forward_body,
        out_shape=jax.ShapeDtypeStruct((pick_rows.shape[0], key_rows.shape[1]), jnp.float32),
        compiler_params=kernel_params(),
        name="hyper_forward",
    )(pick_rows, bias_mask, key_rows, *params)


def hyper_backward_body(count, pick_ref, mask_ref, key_ref, *refs):
    params = [ref[...].astype(jnp.float32) for ref in refs[:6]]
    feats_ref, conv_ref, matrix_ref = refs[6:9]
    key_out, *param_outs = refs[9:16]
    matrix_out, shift_out = refs[16:]
    conv = conv_ref[...] * scaler
    hidden, pull = jax.vjp(
        lambda *items: hyper_rows(None, pick_ref[...], mask_ref[...], *items), key_ref[...], *params
    )
    rows = count + conv.shape[0]
    bias_grad = dot_full(conv, matrix_ref[...].astype(jnp.float32), ((1,), (1,)))
    blank = jnp.zeros((hidden.shape[0] - rows, hidden.shape[1]), jnp.float32)
    grads = pull(jnp.concatenate([feats_ref[...], bias_grad, blank], 0))
    key_out[...] = grads[0]
    for out, grad in zip(param_outs, grads[1:]):
        out[...] = grad
    matrix_out[...] = dot_full(hidden[count:rows], conv, ((0,), (0,)))
    shift_out[...] = jnp.sum(conv, 0, keepdims=True)


def hyper_backward(pick_rows, bias_mask, key_rows, params, feats_grad, conv_grad, bias_weight):
    out = lambda item: jax.ShapeDtypeStruct(item.shape, jnp.float32)
    return pl.pallas_call(
        partial(hyper_backward_body, feats_grad.shape[0]),
        out_shape=[
            out(key_rows),
            *(out(item) for item in params),
            out(bias_weight),
            jax.ShapeDtypeStruct((1, bias_weight.shape[1]), jnp.float32),
        ],
        compiler_params=kernel_params(),
        name="hyper_backward",
    )(pick_rows, bias_mask, key_rows, *params, feats_grad, conv_grad, bias_weight)


def hyper_layout(weight_tokens, bias_token, wave_rows):
    group_count, band_count, width = wave_rows.shape
    tokens = weight_tokens.shape[0]
    waves = group_count * band_count
    key_count = -(-(tokens + waves + 1) // 16) * 16
    query_count = -(-(waves + group_count) // 8) * 8
    key_rows = jnp.concatenate(
        [
            weight_tokens.astype(jnp.float32),
            wave_rows.reshape(waves, width),
            bias_token.astype(jnp.float32)[None, :],
            jnp.zeros((key_count - tokens - waves - 1, width), jnp.float32),
        ],
        0,
    )
    query_id = np.arange(query_count)[:, None]
    key_id = np.arange(key_count)[None, :]
    source = np.where(query_id < waves, tokens + query_id, tokens + waves)
    pick_rows = (key_id == source) & (query_id < waves + group_count)
    query_group = np.where(query_id < waves, query_id // band_count, query_id - waves)
    key_group = (key_id - tokens) // band_count
    allowed = (
        (key_id < tokens)
        | (key_id == tokens + waves)
        | ((key_id < tokens + waves) & (key_group == query_group))
    )
    return (
        jnp.asarray(pick_rows.astype(np.float32)),
        jnp.asarray(np.where(allowed, 0.0, -1e30).astype(np.float32)),
        key_rows,
    )


def spread_eye(rows, copies):
    count, width = rows.shape
    iota = lambda shape, axis: lax.broadcasted_iota(jnp.int32, shape, axis)
    wide = (iota((width, width * copies), 1) // copies == iota((width, width * copies), 0)).astype(
        jnp.bfloat16
    )
    tall = (iota((count * copies, count), 0) // copies == iota((count * copies, count), 1)).astype(
        jnp.bfloat16
    )
    spread = dot_nn(tall, dot_nn(rows, wide).astype(jnp.bfloat16))
    same = iota(spread.shape, 0) % copies == iota(spread.shape, 1) % copies
    return jnp.where(same, spread, 0.0).astype(jnp.bfloat16)


def make_kernel_body(feats_ref, weight_ref, bias_ref, part_ref, spread_ref):
    bands, block, width = part_ref.shape
    hidden = weight_ref.shape[0]

    @pl.when(pl.program_id(0) == 0)
    def _():
        spread_ref[...] = spread_eye(feats_ref[...], block)

    product = dot_nn(spread_ref[...], weight_ref[...].reshape(hidden * block, width))
    product = product.reshape(-1, bands, block, width)
    bias = bias_ref[...].astype(jnp.float32)
    part_ref[...] = (scaler * (product[0] + product[1] + bias[None])).astype(part_ref.dtype)


def make_kernel(band_feats, kernel_weight, kernel_bias):
    bands = band_feats.shape[0]
    hidden, rows, width = kernel_weight.shape
    block = 16
    feats = split_low(band_feats, 2, 0)
    if rows % block:
        product = jnp.einsum(
            "sh,hpd->spd", feats, kernel_weight, preferred_element_type=jnp.float32
        )
        total = jnp.sum(product.reshape(2, bands, rows, width), 0)
        return (scaler * (total + kernel_bias.astype(jnp.float32))).astype(jnp.bfloat16)
    return pl.pallas_call(
        make_kernel_body,
        grid=(rows // block,),
        in_specs=[
            whole_spec(feats.shape),
            pl.BlockSpec((hidden, block, width), lambda i: (0, i, 0)),
            pl.BlockSpec((block, width), lambda i: (i, 0)),
        ],
        out_specs=pl.BlockSpec((bands, block, width), lambda i: (0, i, 0)),
        out_shape=jax.ShapeDtypeStruct((bands, rows, width), jnp.bfloat16),
        scratch_shapes=[pltpu.VMEM((2 * bands * block, hidden * block), jnp.bfloat16)],
        compiler_params=kernel_params(),
        name="make_kernel",
    )(feats, kernel_weight, kernel_bias)


def table_body(feats_ref, out_ref):
    out_ref[...] = spread_eye(feats_ref[...], out_ref.shape[0] // feats_ref.shape[0])


def weight_table(feats, block):
    feats = (scaler * feats).astype(jnp.bfloat16).T
    if block != 16:
        return feats
    return pl.pallas_call(
        table_body,
        out_shape=jax.ShapeDtypeStruct(tuple(size * block for size in feats.shape), jnp.bfloat16),
        compiler_params=kernel_params(),
        name="weight_table",
    )(feats)


def weight_grad_body(table_ref, grad_ref, *refs):
    out_ref = refs[-1]
    hidden, block, width = out_ref.shape
    grad = grad_ref[...].reshape(-1, width)
    out_ref[...] = dot_nn(table_ref[...], grad).reshape(hidden, block, width)


def weight_grad(table, piece, place, rows, out):
    count, block, width = piece.shape
    if block != 16:
        part = jnp.einsum("hs,spd->hpd", table, piece, preferred_element_type=jnp.float32)
        return part if out is None else jnp.concatenate([out, part], 1)
    hidden = table.shape[0] // block
    halves = 2
    keep = [] if out is None else [out]
    return pl.pallas_call(
        weight_grad_body,
        grid=(halves,),
        in_specs=[
            pl.BlockSpec((hidden * block // halves, count * block), lambda i: (i, 0)),
            whole_spec(piece.shape),
            *(pl.BlockSpec(memory_space=pl.ANY) for _ in keep),
        ],
        out_specs=pl.BlockSpec((hidden // halves, block, width), lambda i: (i, place, 0)),
        out_shape=jax.ShapeDtypeStruct((hidden, rows, width), jnp.float32),
        input_output_aliases={2: 0} if keep else {},
        compiler_params=kernel_params(),
        name="weight_grad",
    )(table, piece, *keep)


def feats_body(grad_ref, weight_ref, out_ref):
    bands, block, width = grad_ref.shape
    hidden = weight_ref.shape[0]
    product = dot_nt(
        grad_ref[...].reshape(bands * block, width), weight_ref[...].reshape(hidden * block, width)
    )
    iota = lambda shape, axis: lax.broadcasted_iota(jnp.int32, shape, axis)
    same = iota(product.shape, 0) % block == iota(product.shape, 1) % block
    kept = jnp.sum(jnp.where(same, product, 0.0).reshape(bands, block, hidden * block), 1)
    fold_shape = (hidden * block, hidden)
    fold = (iota(fold_shape, 0) // block == iota(fold_shape, 1)).astype(jnp.float32)
    out_ref[...] = scaler * dot_full(kept, fold, ((1,), (0,)))


def feats_piece(piece, kernel_weight, place):
    bands, block, width = piece.shape
    hidden = kernel_weight.shape[0]
    if block != 16:
        return scaler * jnp.einsum(
            "spd,hpd->sh",
            piece,
            kernel_weight[:, place * block : (place + 1) * block],
            preferred_element_type=jnp.float32,
        )
    return pl.pallas_call(
        feats_body,
        grid=(1,),
        in_specs=[
            whole_spec(piece.shape),
            pl.BlockSpec((hidden, block, width), lambda i: (0, place, 0)),
        ],
        out_specs=whole_spec((bands, hidden)),
        out_shape=jax.ShapeDtypeStruct((bands, hidden), jnp.float32),
        compiler_params=kernel_params(),
        name="feats_piece",
    )(piece, kernel_weight)


def finish_body(place_ref, own_ref, other_ref, in_ref, out_ref, up_ref, down_ref):
    rows, width = out_ref.shape
    half = rows // 2
    widen = lambda item: item.astype(jnp.float32)

    def emit(first, second):
        for core, ref in enumerate((first, second)):
            for y in range(2):
                for block in range(2):
                    at = (2 * core + block) * width
                    up_ref[y * half : (y + 1) * half, at : at + width] = widen(
                        ref[y, block * half : (block + 1) * half]
                    )
        in_ref[:, :width] = widen(first[0, rows : 2 * rows])
        in_ref[:, width : 2 * width] = widen(second[0, rows : 2 * rows])
        in_ref[:, 2 * width :] = widen(first[1, rows : 2 * rows])
        out_ref[...] = widen(second[1, rows : 2 * rows])

    def emit_down(ref):
        part = down_ref.shape[0] // 2
        for y in range(2):
            down_ref[y * part : (y + 1) * part] = widen(ref[y, 2 * rows :])

    pl.when(place_ref[0] == 0)(lambda: emit(own_ref, other_ref))
    pl.when(place_ref[0] == 1)(lambda: emit(other_ref, own_ref))
    pl.when(place_ref[1] == 1)(lambda: emit_down(own_ref))
    pl.when(place_ref[1] == 0)(lambda: emit_down(other_ref))


def finish_grads(place, own, other, rows, down_rows):
    width = own.shape[2]
    out = lambda *shape: jax.ShapeDtypeStruct(shape, jnp.float32)
    return pl.pallas_call(
        finish_body,
        in_specs=[
            pl.BlockSpec(memory_space=pltpu.SMEM),
            pl.BlockSpec(memory_space=pltpu.VMEM),
            pl.BlockSpec(memory_space=pltpu.VMEM),
        ],
        out_shape=[
            out(rows, 3 * width),
            out(rows, width),
            out(rows, 4 * width),
            out(down_rows, width),
        ],
        compiler_params=kernel_params(),
        name="finish_grads",
    )(place, own, other)


def on_device(
    group_size,
    dp_size,
    pixels,
    patch_index,
    kept_count,
    wavelength,
    weight_tokens,
    bias_token,
    hyper_project,
    hyper_output,
    hyper_gains,
    hyper_shifts,
    hyper_up,
    hyper_down,
    kernel_weight,
    kernel_bias,
    bias_weight,
    bias_shift,
    attention_in,
    attention_out,
    expand_weight,
    reduce_weight,
    norm_gains,
    norm_shifts,
    attention_bias,
    output_bias,
    expand_bias,
    reduce_bias,
    cotangent,
):
    floaty = jnp.float32
    low = jnp.bfloat16
    links = Links(group_size, dp_size)
    image_count, slot_count, band_count, pixel_count = pixels.shape[1:]
    model_width = cotangent.shape[-1]
    row_count = image_count * slot_count
    widen = lambda item: item.astype(floaty)
    hyper_params = (
        hyper_project,
        hyper_output,
        hyper_gains,
        hyper_shifts,
        hyper_up,
        hyper_down,
    )

    feed = gather_feed(links, expand_weight, reduce_weight)
    piece = attention_piece(links, attention_in, attention_out)
    piece = piece.reshape((1, 1, 1, 1) + piece.shape)
    block = gather_line(links, piece, 0)
    wave_rows = wave_embed(wavelength[0])
    own_hidden = hyper_forward(
        *hyper_layout(weight_tokens, bias_token, wave_rows[None]), hyper_params
    )
    band_feats = own_hidden[:band_count] + wave_rows
    bias_feat = own_hidden[band_count]
    kernel_part = make_kernel(band_feats, kernel_weight, kernel_bias)
    chunk_count = 3
    chunk_bands = band_count // chunk_count
    depth = chunk_bands * pixel_count
    kernel_part, block, wavelength, bias_feat = stage(kernel_part, block, wavelength, bias_feat)
    chunks = [
        kernel_part[i * chunk_bands : (i + 1) * chunk_bands][:, None, None]
        for i in range(chunk_count)
    ]

    line_one = gather_line(links, chunks[0], 1)
    other = links.xside(block)
    all_waves = spread_group(links, wavelength[0])
    line_one, other, chunks, pixels, all_waves = stage(line_one, other, chunks, pixels, all_waves)
    block = pair_up(block, other, links.x, 1)

    line_one, block, chunks = stage(line_one, block, chunks)
    line_two = gather_line(links, chunks[1], 1)
    other_one = links.xside(line_one)
    other = links.yside(block)
    pixel_rows = pixels.reshape(row_count, band_count * pixel_count)
    line_two, other_one, other, chunks, pixel_rows, all_waves, bias_feat = stage(
        line_two, other_one, other, chunks, pixel_rows, all_waves, bias_feat
    )
    kernel_one = pair_up(line_one, other_one, links.x, 2).reshape(depth, model_width)
    block = pair_up(block, other, links.y, 2)

    line_two, block, kernel_one, chunks = stage(line_two, block, kernel_one, chunks)
    line_three = gather_line(links, chunks[2], 1)
    other_two = links.xside(line_two)
    other = links.core(block)
    valid_rows = (
        lax.broadcasted_iota(jnp.int32, (image_count, slot_count), 1) < kept_count[0][:, None]
    )
    valid_rows = valid_rows.reshape(row_count, 1).astype(floaty)
    out_low = cotangent.reshape(row_count, model_width) * valid_rows.astype(low)
    conv_bias = scaler * (
        jnp.dot(bias_feat, widen(bias_weight), precision=highest) + widen(bias_shift)
    )
    spots = place_spots(patch_index[0].reshape(row_count), 3)
    table = split_low(jnp.concatenate([place_table(model_width), conv_bias[None, :]], 0), 3, 0)
    table = jnp.pad(table, ((0, 128 - table.shape[0]), (0, 0)))
    embed_part = dot_nn(spots, table) + dot_nn(pixel_rows[:, :depth], kernel_one)
    line_three, other_two, other, embed_part, out_low, all_waves = stage(
        line_three, other_two, other, embed_part, out_low, all_waves
    )
    kernel_two = pair_up(line_two, other_two, links.x, 2).reshape(depth, model_width)
    weights = pair_up(block, other, links.c, 3).reshape(8, 4, -1, model_width)

    line_three, weights, kernel_two, all_waves = stage(line_three, weights, kernel_two, all_waves)
    other_three = links.xside(line_three)
    embed_part = embed_part + dot_nn(pixel_rows[:, depth : 2 * depth], kernel_two)
    wave_all = jax.vmap(wave_embed)(all_waves)
    pick_rows, bias_mask, key_rows = hyper_layout(weight_tokens, bias_token, wave_all)
    all_hidden = hyper_forward(pick_rows, bias_mask, key_rows, hyper_params)
    wave_count = group_size * band_count
    feats_all = all_hidden[:wave_count] + wave_all.reshape(wave_count, HE)
    shard_pixels = kernel_bias.shape[0]
    piece_count = 2
    piece_pixels = shard_pixels // piece_count
    table_all = weight_table(feats_all, piece_pixels)
    other_three, embed_part, weights, table_all = stage(
        other_three, embed_part, weights, table_all
    )
    kernel_three = pair_up(line_three, other_three, links.x, 2).reshape(depth, model_width)

    gains = widen(norm_gains)
    shifts = widen(norm_shifts)
    start, hidden_one = embed_rows(
        embed_part, pixel_rows, kernel_three, jnp.stack([gains[0], shifts[0]]), 256
    )
    bias_full = jnp.concatenate(
        [widen(attention_bias[0]), jnp.zeros((model_width,), floaty), widen(attention_bias[1])]
    )[None, :]
    attended = attend_rows(
        0,
        6,
        None,
        kept_count[0],
        hidden_one,
        start,
        weights,
        bias_full,
        jnp.stack([widen(output_bias), gains[1], shifts[1]]),
    )
    project, probs_low, mixed_rows, middle, hidden_two = attended

    half_other = (1 - links.c).reshape(1)
    half_own = links.c.reshape(1)
    wide_bias = widen(expand_bias)[None, :]
    up_other, down_other, bias_other, forward_part, back_part = expand_first(
        half_other, hidden_two, out_low, feed, wide_bias
    )
    up_other, down_other, forward_part = stage(up_other, down_other, forward_part)
    up_other = links.core(up_other)
    down_other = links.core(down_other)
    up_own, down_own, bias_own, encoded, middle_grad, middle_low, sums_two = expand_second(
        half_own,
        hidden_two,
        out_low,
        feed,
        wide_bias,
        forward_part,
        back_part,
        middle,
        valid_rows,
        jnp.stack([widen(reduce_bias), gains[1]]),
    )
    encoded = encoded.reshape(cotangent.shape)
    up_other, down_other, up_own, down_own, middle_low = stage(
        up_other, down_other, up_own, down_own, middle_low
    )
    shard_rows = model_width // dp_size
    down_rows = reduce_weight.shape[0]
    up_shape = (links.line, 2, shard_rows, up_own.shape[1])
    up_pair = [up_own.reshape(up_shape), up_other.reshape(up_shape)]
    down_shape = (-1, 2, down_rows // 2, model_width)
    down_pair = [down_own.reshape(down_shape), down_other.reshape(down_shape)]

    send_up = add_low(*(pick(item, 1 - links.x, 1) for item in up_pair))
    send_down = add_low(*(pick(item, 1 - links.y, 1) for item in down_pair))
    send_up, send_down, middle_low = stage(send_up, send_down, middle_low)
    other_up = links.xside(send_up)
    other_down = links.yside(send_down)
    project_low, conv_low, sums_one, third_sums = attend_back(
        project, probs_low, start, middle_grad, middle_low, weights, gains[0:1], 256
    )
    kernel_grad = contract_rows(pixel_rows, conv_low).astype(low)
    kernel_grad = kernel_grad.reshape(band_count, links.line, 2, shard_pixels, model_width)
    piece_of = lambda i, side: pick(
        kernel_grad[:, :, :, i * piece_pixels : (i + 1) * piece_pixels], side, 2
    )
    send_one = piece_of(0, 1 - links.x)
    other_up, other_down, kernel_grad, send_one = stage(
        other_up, other_down, kernel_grad, send_one
    )
    up_sum = add_low(*(pick(item, links.x, 1) for item in up_pair), other_up)
    up_sum = up_sum.reshape(links.line, 2, shard_rows // 2, -1)
    down_sum = add_low(*(pick(item, links.y, 1) for item in down_pair), other_down)
    small = jnp.concatenate(
        [
            sums_one[0:1],
            sums_two[0:1],
            sums_one[1:2],
            sums_two[1:2],
            third_sums[:, :model_width],
            third_sums[:, 2 * model_width :],
            sums_two[2:4],
            pair_up(bias_own, bias_other, links.c, 1).reshape(-1, model_width),
            sums_one[2:3],
        ],
        0,
    )

    def halve_down(block, stride):
        block = block.reshape(2, -1, down_rows // 2, model_width)
        bit = lax.axis_index("dp") // stride % 2
        return pick(block, 1 - bit, 0), pick(block, bit, 0)

    send_up = pick(up_sum, 1 - links.y, 1)
    stride = dp_size // 4
    send_down, keep_down = halve_down(down_sum, stride)
    other_one = links.xside(send_one)
    send_up, send_down, keep_down, small, project_low = stage(
        send_up, send_down, keep_down, small, project_low
    )
    other_up = links.yside(send_up)
    other_down = links.zside(send_down, stride)
    step = 2
    while step < dp_size:
        small = small + links.zside(small, step)
        step *= 2
    grad_units = [
        contract_rows(hidden_one, project_low[:, i * model_width : (i + 1) * model_width])
        for i in range(3)
    ] + [contract_rows(mixed_rows, middle_low)]
    grad_units = [unit.astype(low) for unit in grad_units]
    units_of = lambda side: jnp.stack(
        [
            jnp.where(side == 0, grad_units[0], grad_units[1]),
            jnp.where(side == 0, grad_units[2], grad_units[3]),
        ]
    )
    send_units = units_of(1 - links.c)
    send_two = piece_of(1, 1 - links.x)
    other_one, other_up, other_down, small, send_units, send_two, kernel_grad = stage(
        other_one, other_up, other_down, small, send_units, send_two, kernel_grad
    )
    line_parts = lambda block: block.reshape(band_count, links.line, -1, model_width)
    finish_piece = lambda terms: add_low(*terms).reshape(band_count, -1, model_width)
    ready = line_parts(add_low(piece_of(0, links.x), other_one))

    ready, send_two, send_units, conv_low, other_up, other_down = stage(
        ready, send_two, send_units, conv_low, other_up, other_down
    )
    other_two = links.xside(send_two)
    total_one = send_line(links, ready, 1, links.zside)
    other_units = links.core(send_units)
    up_sum = add_low(pick(up_sum, links.y, 1), other_up)
    down_sum = add_low(keep_down, other_down)
    other_two, total_one, other_units, up_sum, down_sum, conv_low = stage(
        other_two, total_one, other_units, up_sum, down_sum, conv_low
    )
    ready = line_parts(add_low(piece_of(1, links.x), other_two))
    units = add_low(units_of(links.c), other_units)
    while stride > 2:
        stride //= 2
        send_down, keep_down = halve_down(down_sum, stride)
        down_sum = add_low(keep_down, links.zside(send_down, stride))

    send_units = pick(units, 1 - links.y, 0)
    send_down, keep_down = halve_down(down_sum, 1)
    ready, send_units, send_down, keep_down, total_one = stage(
        ready, send_units, send_down, keep_down, total_one
    )
    total_two = send_line(links, ready, 1, links.zside)
    other_units = links.yside(send_units)
    other_down = links.xside(send_down)
    low_one = finish_piece(total_one)
    feats_one = feats_piece(low_one, kernel_weight, 0)
    total_two, other_units, other_down, feats_one, low_one = stage(
        total_two, other_units, other_down, feats_one, low_one
    )
    low_two = finish_piece(total_two)

    low_two, feats_one = stage(low_two, feats_one)
    feats_part = feats_one + feats_piece(low_two, kernel_weight, 1)
    units = add_low(pick(units, links.y, 0), other_units)
    units = units.reshape(links.line, 2, shard_rows, model_width)
    send_units = pick(units, 1 - links.x, 1)
    tiny = jnp.concatenate([small, feats_part.reshape(-1, model_width)], 0)
    tiny, low_one, send_units = stage(tiny, low_one, send_units)
    tiny = tiny + links.xside(tiny)
    tiny, send_units = stage(tiny, send_units)
    other_units = links.xside(send_units)
    other_one = links.yside(low_one)
    small_count = small.shape[0]
    feats_part = tiny[small_count:].reshape(feats_part.shape)
    step = 2
    while step < dp_size:
        feats_part = feats_part + links.zside(feats_part, step)
        step *= 2
    small = tiny[: small_count - 1]
    conv_all = tiny[small_count - 1 : small_count]
    other_small = links.core(tiny[:small_count])
    small = small + other_small[:-1]
    conv_all = pair_up(conv_all, other_small[-1:], links.c, 0)
    down_sum = add_low(keep_down, other_down).reshape(down_rows // 2, model_width)
    feats_part, other_one, other_units, low_two, small, conv_all, down_sum = stage(
        feats_part, other_one, other_units, low_two, small, conv_all, down_sum
    )
    units = add_low(pick(units, links.x, 1), other_units).reshape(links.line, -1, model_width)
    half_shard = shard_rows // 2
    up_blocks = up_sum.reshape(links.line, half_shard, 2, model_width).transpose(0, 2, 1, 3)
    both = jnp.concatenate([up_blocks.reshape(units.shape), units], 1)
    all_one = pair_up(low_one[None], other_one[None], links.y, 0)[:, None]

    tiny = jnp.concatenate([small, conv_all, feats_part.reshape(-1, model_width)], 0)
    tiny, all_one, both, low_two, down_sum = stage(tiny, all_one, both, low_two, down_sum)
    both = send_line(links, both, 0, links.zside)
    other_tiny = links.yside(tiny)
    other_two = links.yside(low_two)
    other_one = links.core(all_one)
    small = small + other_tiny[: small_count - 1]
    conv_all = pair_up(conv_all, other_tiny[small_count - 1 : small_count + 1], links.y, 0)
    feats_part = feats_part[None]
    feats_y = other_tiny[small_count + 1 :].reshape(feats_part.shape)
    feats_two = pair_up(feats_part, feats_y, links.y, 0)
    feats_c = links.core(feats_two)
    feats_grad = pair_up(feats_two[:, None], feats_c[:, None], links.c, 1).reshape(-1, HE)
    feats_grad, other_one, other_two, small, conv_all, down_sum = stage(
        feats_grad, other_one, other_two, small, conv_all, down_sum
    )
    all_one = pair_up(all_one, other_one, links.c, 1).reshape((wave_count,) + low_one.shape[1:])
    all_two = pair_up(low_two[None], other_two[None], links.y, 0)[:, None]

    all_two, feats_grad, all_one, down_sum = stage(all_two, feats_grad, all_one, down_sum)
    other_two = links.core(all_two)
    other_down = links.owner_line(down_sum)
    key_grad, *param_grads, bias_weight_grad, bias_shift_grad = hyper_backward(
        pick_rows,
        bias_mask,
        key_rows,
        hyper_params,
        feats_grad,
        conv_all,
        bias_weight,
    )
    wide_kernel = jnp.concatenate([kernel_one, kernel_two, kernel_three], 0)
    pixel_grad = pixel_gradient(conv_low, wide_kernel, band_count)
    weight_shard_grad = weight_grad(table_all, all_one, 0, shard_pixels, None)
    other_two, key_grad, both, other_down, weight_shard_grad, pixel_grad = stage(
        other_two, key_grad, both, other_down, weight_shard_grad, pixel_grad
    )
    pixel_grad = pixel_grad.reshape(pixels.shape)
    both = jnp.concatenate([add_low(*both), add_low(down_sum, other_down)], 0)[None]
    all_two = pair_up(all_two, other_two, links.c, 1).reshape(all_one.shape)

    both, all_two = stage(both, all_two)
    other_both = links.yside(both)
    weight_shard_grad = weight_grad(table_all, all_two, 1, shard_pixels, weight_shard_grad)
    other_both, weight_shard_grad = stage(other_both, weight_shard_grad)
    both = pair_up(both, other_both, links.y, 0)
    other_both = links.core(both)
    token_count = weight_tokens.shape[0]
    bias_shard_grad = scaler * jnp.concatenate(
        [jnp.sum(item.astype(floaty), 0) for item in (all_one, all_two)], 0
    )
    is_owner = lax.axis_index("dp") // (dp_size // 2) == links.c
    if shard_rows % 32 == 0:
        place = jnp.stack([links.c, is_owner.astype(jnp.int32)])
        block_shards = finish_grads(place, both, other_both, shard_rows, down_rows)
    else:
        down_total = jnp.where(is_owner, both[:, 2 * shard_rows :], other_both[:, 2 * shard_rows :])
        cores = pair_up(both[:, None], other_both[:, None], links.c, 1)
        up_total = cores[:, :, :shard_rows].reshape(2, 2, 2, half_shard, model_width)
        unit_all = cores[:, :, shard_rows : 2 * shard_rows].reshape(4, shard_rows, model_width)
        block_shards = (
            widen(jnp.concatenate([unit_all[i] for i in range(3)], 1)),
            widen(unit_all[3]),
            widen(up_total.transpose(0, 3, 1, 2, 4).reshape(shard_rows, -1)),
            widen(down_total.reshape(down_rows, model_width)),
        )
    return (
        encoded,
        pixel_grad,
        key_grad[:token_count],
        key_grad[token_count + wave_count],
        *param_grads,
        weight_shard_grad,
        bias_shard_grad,
        bias_weight_grad,
        bias_shift_grad.reshape(-1),
        *block_shards,
        small[0:2],
        small[2:4],
        small[4:6],
        small[6],
        small[8:].reshape(-1),
        small[7],
    )


def solution(mesh):
    placed = (
        P("group", "dp", None, None, None),
        P("group", "dp", None),
        P("group", "dp"),
        P("group", None),
        P(),
        P(),
        P(),
        P(),
        P(),
        P(),
        P(),
        P(),
        P(None, "dp", None),
        P("dp", None),
        P(),
        P(),
        P("dp", None),
        P("dp", None),
        P("dp", None),
        P("dp", None),
        P(),
        P(),
        P(),
        P(),
        P(),
        P(),
        P("group", "dp", None, None),
    )
    return jax.shard_map(
        partial(on_device, mesh.shape["group"], mesh.shape["dp"]),
        mesh=mesh,
        in_specs=placed,
        out_specs=(
            P("group", "dp", None, None),
            P("group", "dp", None, None, None),
            P(),
            P(),
            P(),
            P(),
            P(),
            P(),
            P(),
            P(),
            P(None, "dp", None),
            P("dp", None),
            P(),
            P(),
            P("dp", None),
            P("dp", None),
            P("dp", None),
            P("dp", None),
            P(),
            P(),
            P(),
            P(),
            P(),
            P(),
        ),
        check_vma=False,
    )
```

```python
from functools import partial

import jax
import jax.numpy as jnp
import numpy as np
from jax import lax
from jax.experimental import pallas as pl
from jax.experimental.pallas import tpu as pltpu
from jax.sharding import PartitionSpec as P

HE = 128
HH = 4
SIDE = 14


scaler = 0.01
highest = lax.Precision.HIGHEST


def contract_rows(operand, partner):
    return lax.dot_general(
        operand, partner, (((0,), (0,)), ((), ())), preferred_element_type=jnp.float32
    )


def wave_embed(wave_ids):
    half_width = HE // 2
    frequency = 1.0 / 10000.0 ** (jnp.arange(half_width, dtype=jnp.float32) / half_width)
    angles = wave_ids.astype(jnp.float32)[:, None] * frequency
    return jnp.concatenate([jnp.sin(angles), jnp.cos(angles)], -1)


def place_table(model_width):
    quarter = model_width // 4
    frequency = 1.0 / 10000.0 ** (jnp.arange(quarter, dtype=jnp.float32) / quarter)
    angle = jnp.arange(SIDE, dtype=jnp.float32)[:, None] * frequency
    waves = jnp.concatenate([jnp.sin(angle), jnp.cos(angle)], -1)
    blank = jnp.zeros_like(waves)
    return jnp.concatenate(
        [jnp.concatenate([waves, blank], -1), jnp.concatenate([blank, waves], -1)], 0
    )


def place_spots(patch_ids, copies):
    lanes = jnp.arange(128, dtype=jnp.int32)[None, :]
    spot = lanes % (2 * SIDE + 1)
    row_id = (patch_ids // SIDE)[:, None]
    col_id = (patch_ids % SIDE)[:, None] + SIDE
    hit = (spot == row_id) | (spot == col_id) | (spot == 2 * SIDE)
    return (hit & (lanes < copies * (2 * SIDE + 1))).astype(jnp.bfloat16)


def split_low(values, count, axis):
    pieces = []
    for _ in range(count):
        piece = values.astype(jnp.bfloat16)
        pieces.append(piece)
        values = values - piece.astype(jnp.float32)
    return jnp.concatenate(pieces, axis)


def stage(*values):
    return lax.optimization_barrier(values)


class Links:
    def __init__(self, group_size, dp_size):
        self.group_size = group_size
        self.dp_size = dp_size
        group_id = lax.axis_index("group")
        dp_id = lax.axis_index("dp")
        self.y = group_id // 2
        self.c = group_id % 2
        self.x = dp_id % 2
        self.digits = []
        stride = 2
        while stride < dp_size:
            size = min(4, dp_size // stride)
            self.digits.insert(0, (size, stride, dp_id // stride % size))
            stride *= size
        self.line = dp_size // 2
        self.z = dp_id // 2

    def core(self, block):
        return lax.ppermute(block, "group", [(i, i ^ 1) for i in range(self.group_size)])

    def yside(self, block):
        return lax.ppermute(block, "group", [(i, i ^ 2) for i in range(self.group_size)])

    def xside(self, block):
        return lax.ppermute(block, "dp", [(i, i ^ 1) for i in range(self.dp_size)])

    def zside(self, block, step):
        return lax.ppermute(block, "dp", [(i, i ^ step) for i in range(self.dp_size)])

    def owner_pairs(self, target_of):
        pairs = []
        for group_id in range(self.group_size):
            for dp_id in range(self.dp_size):
                target = target_of(group_id, dp_id)
                if target is not None:
                    pairs.append(
                        (group_id * self.dp_size + dp_id, target[0] * self.dp_size + target[1])
                    )
        return pairs

    def owner_line(self, block):
        top = self.dp_size // 2
        pairs = self.owner_pairs(lambda g, d: (g, d ^ top) if d // top != g % 2 else None)
        return lax.ppermute(block, ("group", "dp"), pairs)

    def owner_core(self, block):
        top = self.dp_size // 2
        pairs = self.owner_pairs(lambda g, d: (g ^ 1, d) if d // top == g % 2 else None)
        return lax.ppermute(block, ("group", "dp"), pairs)


def pick(block, index, axis, count=1):
    return lax.dynamic_slice_in_dim(block, index, count, axis)


def add_low(*items):
    total = items[0].astype(jnp.float32)
    for item in items[1:]:
        total = total + item.astype(jnp.float32)
    return total.astype(jnp.bfloat16)


def pair_up(block, other, bit, axis):
    return jnp.where(
        bit == 0,
        jnp.concatenate([block, other], axis),
        jnp.concatenate([other, block], axis),
    )


def place_digit(block, received, me, axis):
    size = len(received) + 1
    shape = block.shape[:axis] + (size,) + block.shape[axis + 1 :]
    out = jnp.zeros(shape, block.dtype)
    for step, piece in zip(range(size), [block] + received):
        at = tuple(me ^ step if i == axis else 0 for i in range(len(shape)))
        out = lax.dynamic_update_slice(out, piece, at)
    return out


def gather_line(links, piece, axis):
    lead, tail = piece.shape[:axis], piece.shape[axis + 1 :]
    count = len(links.digits)
    block = piece.reshape(lead + (1,) * count + tail)
    for place, (size, stride, me) in reversed(list(enumerate(links.digits))):
        received = [links.zside(block, stride * step) for step in range(1, size)]
        block = place_digit(block, received, me, axis + place)
    return block.reshape(lead + (links.line,) + tail)


def send_line(links, block, axis, sender):
    lead, tail = block.shape[:axis], block.shape[axis + 1 :]
    block = block.reshape(lead + tuple(size for size, _, _ in links.digits) + tail)
    for place, (size, stride, me) in enumerate(links.digits):
        if place:
            block = add_low(*terms)
        terms = [pick(block, me, axis + place)] + [
            sender(pick(block, me ^ step, axis + place), stride * step) for step in range(1, size)
        ]
    return [term.reshape(lead + tail) for term in terms]


def attention_piece(links, attention_in, attention_out):
    width = attention_out.shape[1]
    thirds = [attention_in[:, i * width : (i + 1) * width] for i in range(3)]
    return lax.dynamic_index_in_dim(
        jnp.stack(thirds + [attention_out]), lax.axis_index("group"), 0, False
    )


def gather_feed(links, expand_weight, reduce_weight):
    width = reduce_weight.shape[1]
    count = links.group_size
    group_id = lax.axis_index("group")
    up = pick(expand_weight, group_id * width, 1, width)
    rows = reduce_weight.shape[0] // count
    down = pick(reduce_weight, group_id * rows, 0, rows)
    wide = lax.all_gather(jnp.stack([up, down]), ("dp", "group"), axis=0)
    wide = wide.reshape(links.dp_size, count, 2, rows, width)
    if rows % 16:
        up = wide[:, :, 0].transpose(1, 0, 2, 3).reshape(count, 8, width // 8, width)
        down = wide[:, :, 1].reshape(8, count, width // 8, width)
        wide = jnp.stack([up.transpose(1, 0, 2, 3), down], 2)
    return wide


def spread_group(links, piece):
    piece = piece.reshape((1, 1) + piece.shape)
    piece = pair_up(piece, links.yside(piece), links.y, 0)
    piece = pair_up(piece, links.core(piece), links.c, 1)
    return piece.reshape((-1,) + piece.shape[2:])


def sum_dp(links, values):
    step = 1
    while step < links.dp_size:
        values = values + links.zside(values, step)
        step *= 2
    return values


VMEM_BYTES = 60 * 1024 * 1024


def kernel_params():
    return pltpu.CompilerParams(vmem_limit_bytes=VMEM_BYTES)


def whole_spec(shape):
    return pl.BlockSpec(shape, lambda *_: (0,) * len(shape))


def norm_rows(values, epsilon):
    center = values - jnp.mean(values, -1, keepdims=True)
    inverse = lax.rsqrt(jnp.mean(center * center, -1, keepdims=True) + epsilon)
    return center * inverse, inverse


def dot_nn(one, two):
    return lax.dot_general(one, two, (((1,), (0,)), ((), ())), preferred_element_type=jnp.float32)


def dot_nt(one, two):
    return lax.dot_general(one, two, (((1,), (1,)), ((), ())), preferred_element_type=jnp.float32)


def dot_tn(one, two):
    return lax.dot_general(one, two, (((0,), (0,)), ((), ())), preferred_element_type=jnp.float32)


def embed_body(part_ref, pixel_ref, kernel_ref, norm_ref, start_ref, hidden_ref):
    start = part_ref[...] + dot_nn(pixel_ref[...], kernel_ref[...])
    start_ref[...] = start
    normed, _ = norm_rows(start, 1e-06)
    hidden_ref[...] = (normed * norm_ref[0:1, :] + norm_ref[1:2, :]).astype(jnp.bfloat16)


def embed_rows(part, pixel_rows, wide_kernel, norm_one, block_rows):
    rows = part.shape[0]
    depth = wide_kernel.shape[0]
    last = pixel_rows.shape[1] // depth - 1
    width = wide_kernel.shape[1]
    row_spec = lambda cols: pl.BlockSpec((block_rows, cols), lambda i: (i, 0))
    return pl.pallas_call(
        embed_body,
        grid=(rows // block_rows,),
        in_specs=[
            row_spec(width),
            pl.BlockSpec((block_rows, depth), lambda i: (i, last)),
            whole_spec(wide_kernel.shape),
            whole_spec(norm_one.shape),
        ],
        out_specs=[row_spec(width), row_spec(width)],
        out_shape=[
            jax.ShapeDtypeStruct((rows, width), jnp.float32),
            jax.ShapeDtypeStruct((rows, width), jnp.bfloat16),
        ],
        compiler_params=kernel_params(),
        cost_estimate=pl.CostEstimate(flops=0, bytes_accessed=0, transcendentals=0),
        name="embed_rows",
    )(part, pixel_rows, wide_kernel, norm_one)


def pixel_grad_body(grad_ref, kernel_ref, out_ref):
    images, bands, slots, depth = out_ref.shape
    for band in range(bands):
        part = dot_nt(grad_ref[...], kernel_ref[band * depth : (band + 1) * depth, :])
        out_ref[:, band] = part.astype(out_ref.dtype).reshape(images, slots, depth)


def pixel_gradient(conv_low, wide_kernel, images, bands):
    rows, width = conv_low.shape
    slots = rows // images
    depth = wide_kernel.shape[0] // bands
    block = images // 3
    return pl.pallas_call(
        pixel_grad_body,
        grid=(3,),
        in_specs=[
            pl.BlockSpec((block * slots, width), lambda i: (i, 0)),
            whole_spec(wide_kernel.shape),
        ],
        out_specs=pl.BlockSpec((block, bands, slots, depth), lambda i: (i, 0, 0, 0)),
        out_shape=jax.ShapeDtypeStruct((images, bands, slots, depth), jnp.bfloat16),
        compiler_params=kernel_params(),
        cost_estimate=pl.CostEstimate(flops=0, bytes_accessed=0, transcendentals=0),
        name="pixel_gradient",
    )(conv_low, wide_kernel)


def pair_stack(block, low_half):
    zero = jnp.zeros_like(block)
    return jnp.concatenate(
        [jnp.where(low_half, block, zero), jnp.where(low_half, zero, block)], 0
    )


def half_reduce(values, low_half, reducer, filler):
    first = reducer(jnp.where(low_half, values, filler), -1, keepdims=True)
    second = reducer(jnp.where(low_half, filler, values), -1, keepdims=True)
    return jnp.where(low_half, first, second)


def join_weights(count_ref, own_ref, other_ref, weight_ref):
    width = weight_ref.shape[1]

    def fill(refs):
        for unit in range(4):
            weight_ref[unit] = refs[unit % 2][:, unit // 2].reshape(width, width)

    core = count_ref[count_ref.shape[0] - 1]
    first = pl.program_id(0) == 0
    pl.when(first & (core == 0))(lambda: fill((own_ref, other_ref)))
    pl.when(first & (core == 1))(lambda: fill((other_ref, own_ref)))


def attend_body(
    first,
    count_ref,
    hidden_ref,
    start_ref,
    own_ref,
    other_ref,
    bias_ref,
    rows_ref,
    project_ref,
    probs_ref,
    mixed_ref,
    middle_ref,
    hidden_two_ref,
    score_ref,
    weight_ref,
):
    join_weights(count_ref, own_ref, other_ref, weight_ref)
    block_rows, width = hidden_ref.shape
    slots = 64
    images = block_rows // slots
    base = (pl.program_id(0) + first) * images
    for third in range(3):
        at = third * width
        weight = weight_ref[third]
        project_ref[:, at : at + width] = (
            dot_nn(hidden_ref[...], weight) + bias_ref[:, at : at + width]
        ).astype(jnp.bfloat16)
    lanes = lax.broadcasted_iota(jnp.int32, (slots, 128), 1)
    low_half = lanes < 64
    key_id = jnp.where(low_half, lanes, lanes - 64)
    pairs = width // 128
    blocks = [(image, pair) for image in range(images) for pair in range(pairs)]
    for place, (image, pair) in enumerate(blocks):
        here = slice(image * slots, (image + 1) * slots)
        at = pair * 128
        queries = project_ref[here, at : at + 128]
        keys = pair_stack(project_ref[here, width + at : width + at + 128], low_half)
        keep = key_id < count_ref[base + image]
        score_ref[place * slots : (place + 1) * slots, :] = jnp.where(
            keep, dot_nt(queries, keys) * 0.125, -1000000000.0
        )
    for image in range(images):
        here = slice(image * pairs * slots, (image + 1) * pairs * slots)
        scores = score_ref[here, :]
        wide_half = lax.broadcasted_iota(jnp.int32, scores.shape, 1) < 64
        probs = jnp.exp(scores - half_reduce(scores, wide_half, jnp.max, -3e38))
        score_ref[here, :] = probs / half_reduce(probs, wide_half, jnp.sum, 0.0)
    for place, (image, pair) in enumerate(blocks):
        here = slice(image * slots, (image + 1) * slots)
        at = pair * 128
        values = pair_stack(project_ref[here, 2 * width + at : 2 * width + at + 128], low_half)
        probs_low = score_ref[place * slots : (place + 1) * slots, :].astype(jnp.bfloat16)
        probs_ref[here, at : at + 128] = probs_low
        mixed_ref[here, at : at + 128] = dot_nn(probs_low, values).astype(jnp.bfloat16)
    middle = start_ref[...] + dot_nn(mixed_ref[...], weight_ref[3]) + rows_ref[0:1, :]
    middle_ref[...] = middle
    normed, _ = norm_rows(middle, 1e-06)
    hidden_two_ref[...] = (normed * rows_ref[1:2, :] + rows_ref[2:3, :]).astype(jnp.bfloat16)


def attend_rows(first, steps, earlier, counts, hidden_one, start, own, other, bias_full, rows_in):
    rows, width = hidden_one.shape
    block_rows = 128
    row_spec = lambda cols: pl.BlockSpec((block_rows, cols), lambda i, *_: (i + first, 0))
    low = jnp.bfloat16
    keep = list(earlier or ())

    def body(count_ref, *refs):
        refs = refs[:6] + refs[6 + len(keep) :]
        attend_body(first, count_ref, *refs)

    return pl.pallas_call(
        body,
        grid_spec=pltpu.PrefetchScalarGridSpec(
            num_scalar_prefetch=1,
            grid=(steps,),
            in_specs=[
                row_spec(width),
                row_spec(width),
                whole_spec(own.shape),
                whole_spec(other.shape),
                whole_spec(bias_full.shape),
                whole_spec(rows_in.shape),
                *(pl.BlockSpec(memory_space=pl.ANY) for _ in keep),
            ],
            out_specs=[
                row_spec(3 * width),
                row_spec(width),
                row_spec(width),
                row_spec(width),
                row_spec(width),
            ],
            scratch_shapes=[
                pltpu.VMEM((block_rows * width // 128, 128), jnp.float32),
                pltpu.VMEM((4, width, width), low),
            ],
        ),
        out_shape=[
            jax.ShapeDtypeStruct((rows, 3 * width), low),
            jax.ShapeDtypeStruct((rows, width), low),
            jax.ShapeDtypeStruct((rows, width), low),
            jax.ShapeDtypeStruct((rows, width), jnp.float32),
            jax.ShapeDtypeStruct((rows, width), low),
        ],
        input_output_aliases={7 + i: i for i in range(len(keep))},
        compiler_params=kernel_params(),
        cost_estimate=pl.CostEstimate(flops=0, bytes_accessed=0, transcendentals=0),
        name="attend_rows",
    )(counts, hidden_one, start, own, other, bias_full, rows_in, *keep)


def expand_step(hidden_ref, turned_ref, out_ref, up_ref, bias_ref, down_ref):
    low = jnp.bfloat16
    out_low = out_ref[...]
    width = out_low.shape[1]
    up = up_ref[...].reshape(width, -1)
    down = down_ref[...].reshape(-1, width)
    pre = dot_nn(hidden_ref[...], up) + bias_ref[...]
    cumulative = 0.5 + 0.5 * lax.erf(pre * 0.7071067811865476)
    slope = cumulative + pre * (jnp.exp(pre * pre * -0.5) * 0.3989422804014327)
    activated = (pre * cumulative).astype(low)
    pre_grad = dot_nt(out_low, down) * slope
    pre_low = pre_grad.astype(low)
    return (
        jnp.sum(pre_grad, 0, keepdims=True),
        dot_nn(activated, down),
        dot_nt(pre_low, up),
        dot_nn(turned_ref[...], pre_low),
        dot_tn(activated, out_low),
    )


def accumulate(ref, part):
    @pl.when(pl.program_id(0) == 0)
    def _():
        ref[...] = part

    @pl.when(pl.program_id(0) > 0)
    def _():
        ref[...] += part


def first_body(
    half_ref,
    hidden_ref,
    out_ref,
    up_ref,
    bias_ref,
    down_ref,
    grad_up_ref,
    grad_down_ref,
    bias_grad_ref,
    forward_ref,
    back_ref,
    turned_ref,
):
    @pl.when(pl.program_id(0) == 0)
    def _():
        turned_ref[...] = hidden_ref[...].T

    bias_grad, forward_part, back_part, grad_up, grad_down = expand_step(
        hidden_ref, turned_ref, out_ref, up_ref, bias_ref, down_ref
    )
    bias_grad_ref[...] = bias_grad
    grad_up_ref[...] = grad_up.astype(jnp.bfloat16)
    grad_down_ref[...] = grad_down.astype(jnp.bfloat16)
    accumulate(forward_ref, forward_part)
    accumulate(back_ref, back_part)


def second_body(
    half_ref,
    hidden_ref,
    out_ref,
    up_ref,
    bias_ref,
    down_ref,
    forward_ref,
    back_ref,
    middle_ref,
    valid_ref,
    rows_ref,
    grad_up_ref,
    grad_down_ref,
    bias_grad_ref,
    encoded_ref,
    middle_grad_ref,
    middle_low_ref,
    sums_ref,
    forward_acc,
    back_acc,
    turned_ref,
):
    step = pl.program_id(0)
    low = jnp.bfloat16

    @pl.when(step == 0)
    def _():
        turned_ref[...] = hidden_ref[...].T
        forward_acc[...] = forward_ref[...]
        back_acc[...] = back_ref[...]

    bias_grad, forward_part, back_part, grad_up, grad_down = expand_step(
        hidden_ref, turned_ref, out_ref, up_ref, bias_ref, down_ref
    )
    bias_grad_ref[...] = bias_grad
    grad_up_ref[...] = grad_up.astype(low)
    grad_down_ref[...] = grad_down.astype(low)
    forward_acc[...] += forward_part
    back_acc[...] += back_part

    @pl.when(step == pl.num_programs(0) - 1)
    def _():
        middle = middle_ref[...]
        encoded_ref[...] = (
            (middle + forward_acc[...] + rows_ref[0:1, :]) * valid_ref[...]
        ).astype(low)
        normed, inverse = norm_rows(middle, 1e-06)
        grad = back_acc[...]
        out_grad = out_ref[...].astype(jnp.float32)
        scaled = grad * rows_ref[1:2, :]
        middle_grad = out_grad + inverse * (
            scaled
            - jnp.mean(scaled, -1, keepdims=True)
            - normed * jnp.mean(scaled * normed, -1, keepdims=True)
        )
        middle_grad_ref[...] = middle_grad
        middle_low_ref[...] = middle_grad.astype(low)
        sums_ref[0:1, :] = jnp.sum(grad * normed, 0, keepdims=True)
        sums_ref[1:2, :] = jnp.sum(grad, 0, keepdims=True)
        sums_ref[2:3, :] = jnp.sum(middle_grad, 0, keepdims=True)
        sums_ref[3:4, :] = jnp.sum(out_grad, 0, keepdims=True)


def expand_call(name, body, half, rows, width, ins, extra_ins, extra_outs, scratch):
    packed = ins[2].shape
    low = jnp.bfloat16
    steps = packed[1] // 2
    full = whole_spec((rows, width))
    place = lambda i, half: steps * half[0] + i
    return pl.pallas_call(
        body,
        grid_spec=pltpu.PrefetchScalarGridSpec(
            num_scalar_prefetch=1,
            grid=(steps,),
            in_specs=[
                full,
                full,
                pl.BlockSpec(
                    (packed[0], 1, 1) + packed[3:], lambda i, half: (0, place(i, half), 0, 0, 0)
                ),
                pl.BlockSpec((1, width), lambda i, half: (0, place(i, half))),
                pl.BlockSpec(
                    (packed[0] // packed[1], packed[1], 1) + packed[3:],
                    lambda i, half: (place(i, half), 0, 1, 0, 0),
                ),
                *extra_ins,
            ],
            out_specs=[
                pl.BlockSpec((width, width), lambda i, half: (0, i)),
                pl.BlockSpec((width, width), lambda i, half: (i, 0)),
                pl.BlockSpec((1, width), lambda i, half: (0, i)),
                *(whole_spec(item.shape) for item in extra_outs),
            ],
            scratch_shapes=scratch,
        ),
        out_shape=[
            jax.ShapeDtypeStruct((width, steps * width), low),
            jax.ShapeDtypeStruct((steps * width, width), low),
            jax.ShapeDtypeStruct((1, steps * width), jnp.float32),
            *extra_outs,
        ],
        compiler_params=kernel_params(),
        cost_estimate=pl.CostEstimate(flops=0, bytes_accessed=0, transcendentals=0),
        name=name,
    )(half, *ins)


def expand_first(half, hidden_two, out_low, packed, bias):
    rows, width = hidden_two.shape
    total = jax.ShapeDtypeStruct((rows, width), jnp.float32)
    return expand_call(
        "expand_first",
        first_body,
        half,
        rows,
        width,
        (hidden_two, out_low, packed, bias, packed),
        [],
        [total, total],
        [pltpu.VMEM((width, rows), jnp.bfloat16)],
    )


def expand_second(
    half,
    hidden_two,
    out_low,
    packed,
    bias,
    forward_part,
    back_part,
    middle,
    valid_rows,
    rows_in,
):
    rows, width = hidden_two.shape
    full = whole_spec((rows, width))
    total = pltpu.VMEM((rows, width), jnp.float32)
    return expand_call(
        "expand_second",
        second_body,
        half,
        rows,
        width,
        (
            hidden_two,
            out_low,
            packed,
            bias,
            packed,
            forward_part,
            back_part,
            middle,
            valid_rows,
            rows_in,
        ),
        [full, full, full, whole_spec(valid_rows.shape), whole_spec(rows_in.shape)],
        [
            jax.ShapeDtypeStruct((rows, width), jnp.bfloat16),
            jax.ShapeDtypeStruct((rows, width), jnp.float32),
            jax.ShapeDtypeStruct((rows, width), jnp.bfloat16),
            jax.ShapeDtypeStruct((4, width), jnp.float32),
        ],
        [total, total, pltpu.VMEM((width, rows), jnp.bfloat16)],
    )


def attend_back_body(
    count_ref,
    project_ref,
    probs_ref,
    start_ref,
    middle_grad_ref,
    middle_low_ref,
    own_ref,
    other_ref,
    rows_ref,
    project_low_ref,
    conv_low_ref,
    sums_ref,
    third_ref,
    mixed_low,
    grad_ref,
    weight_ref,
):
    join_weights(count_ref, own_ref, other_ref, weight_ref)
    block_rows, width = start_ref.shape
    slots = 64
    low = jnp.bfloat16
    mixed_low[...] = dot_nt(middle_low_ref[...], weight_ref[3]).astype(low)
    lanes = lax.broadcasted_iota(jnp.int32, (slots, 128), 1)
    low_half = lanes < 64

    def fold(block):
        return jnp.where(low_half, block[:slots], block[slots:])

    pairs = width // 128
    images = block_rows // slots
    blocks = [(image, pair) for image in range(images) for pair in range(pairs)]
    for place, (image, pair) in enumerate(blocks):
        here = slice(image * slots, (image + 1) * slots)
        at = pair * 128
        values = pair_stack(project_ref[here, 2 * width + at : 2 * width + at + 128], low_half)
        mixed = mixed_low[here, at : at + 128]
        grad_ref[place * slots : (place + 1) * slots, :] = dot_nt(mixed, values)
        project_low_ref[here, 2 * width + at : 2 * width + at + 128] = fold(
            dot_tn(probs_ref[here, at : at + 128], mixed)
        ).astype(low)
    for image in range(images):
        rows = slice(image * slots, (image + 1) * slots)
        probs = jnp.concatenate(
            [probs_ref[rows, pair * 128 : (pair + 1) * 128] for pair in range(pairs)], 0
        ).astype(jnp.float32)
        here = slice(image * pairs * slots, (image + 1) * pairs * slots)
        prob_grad = grad_ref[here, :]
        wide_half = lax.broadcasted_iota(jnp.int32, prob_grad.shape, 1) < 64
        centre = half_reduce(prob_grad * probs, wide_half, jnp.sum, 0.0)
        grad_ref[here, :] = probs * (prob_grad - centre)
    for place, (image, pair) in enumerate(blocks):
        here = slice(image * slots, (image + 1) * slots)
        at = pair * 128
        queries = project_ref[here, at : at + 128]
        keys = pair_stack(project_ref[here, width + at : width + at + 128], low_half)
        score_low = grad_ref[place * slots : (place + 1) * slots, :].astype(low)
        project_low_ref[here, at : at + 128] = (dot_nn(score_low, keys) * 0.125).astype(low)
        project_low_ref[here, width + at : width + at + 128] = (
            fold(dot_tn(score_low, queries)) * 0.125
        ).astype(low)
    project_low = project_low_ref[...]
    grad = dot_nt(project_low[:, :width], weight_ref[0])
    for third in (1, 2):
        at = third * width
        grad = grad + dot_nt(project_low[:, at : at + width], weight_ref[third])
    normed, inverse = norm_rows(start_ref[...], 1e-06)
    scaled = grad * rows_ref[0:1, :]
    start_grad = middle_grad_ref[...] + inverse * (
        scaled
        - jnp.mean(scaled, -1, keepdims=True)
        - normed * jnp.mean(scaled * normed, -1, keepdims=True)
    )
    conv_low_ref[...] = start_grad.astype(low)
    sums = jnp.concatenate(
        [
            jnp.sum(grad * normed, 0, keepdims=True),
            jnp.sum(grad, 0, keepdims=True),
            jnp.sum(start_grad, 0, keepdims=True),
        ],
        0,
    )
    third = jnp.sum(project_low.astype(jnp.float32), 0, keepdims=True)

    @pl.when(pl.program_id(0) == 0)
    def _():
        sums_ref[...] = sums
        third_ref[...] = third

    @pl.when(pl.program_id(0) > 0)
    def _():
        sums_ref[...] += sums
        third_ref[...] += third


def attend_back(
    counts, project, probs_low, start, middle_grad, middle_low, own, other, rows_in, block_rows
):
    rows, width = start.shape
    row_spec = lambda cols: pl.BlockSpec((block_rows, cols), lambda i, *_: (i, 0))
    low = jnp.bfloat16
    return pl.pallas_call(
        attend_back_body,
        grid_spec=pltpu.PrefetchScalarGridSpec(
            num_scalar_prefetch=1,
            grid=(rows // block_rows,),
            in_specs=[
                row_spec(3 * width),
                row_spec(width),
                row_spec(width),
                row_spec(width),
                row_spec(width),
                whole_spec(own.shape),
                whole_spec(other.shape),
                whole_spec(rows_in.shape),
            ],
            out_specs=[
                row_spec(3 * width),
                row_spec(width),
                whole_spec((3, width)),
                whole_spec((1, 3 * width)),
            ],
            scratch_shapes=[
                pltpu.VMEM((block_rows, width), low),
                pltpu.VMEM((block_rows * width // 128, 128), jnp.float32),
                pltpu.VMEM((4, width, width), low),
            ],
        ),
        out_shape=[
            jax.ShapeDtypeStruct((rows, 3 * width), low),
            jax.ShapeDtypeStruct((rows, width), low),
            jax.ShapeDtypeStruct((3, width), jnp.float32),
            jax.ShapeDtypeStruct((1, 3 * width), jnp.float32),
        ],
        compiler_params=kernel_params(),
        cost_estimate=pl.CostEstimate(flops=0, bytes_accessed=0, transcendentals=0),
        name="attend_back",
    )(counts, project, probs_low, start, middle_grad, middle_low, own, other, rows_in)


def dot_full(one, two, dims, precision=highest):
    return lax.dot_general(
        one, two, (dims, ((), ())), precision=precision, preferred_element_type=jnp.float32
    )


def hyper_rows(
    precision,
    pick_rows,
    bias_mask,
    key_rows,
    hyper_project,
    hyper_output,
    hyper_gains,
    hyper_shifts,
    hyper_up,
    hyper_down,
):
    width = key_rows.shape[1]
    query_rows = dot_full(pick_rows, key_rows, ((1,), (0,)))
    queries = dot_full(query_rows, hyper_project[:, :width], ((1,), (0,)), precision)
    keys_all = dot_full(key_rows, hyper_project[:, width : 2 * width], ((1,), (0,)), precision)
    values_all = dot_full(key_rows, hyper_project[:, 2 * width :], ((1,), (0,)), precision)
    head_size = width // HH
    head_of = lax.broadcasted_iota(jnp.int32, (1, width), 1) // head_size
    mixed_rows = jnp.zeros_like(query_rows)
    for head in range(HH):
        here = (head_of == head).astype(jnp.float32)
        scores = dot_full(queries * here, keys_all, ((1,), (1,)), precision) * head_size ** (-0.5) + bias_mask
        peak = lax.stop_gradient(jnp.max(scores, -1, keepdims=True))
        weights = jnp.exp(scores - peak)
        weights = weights / jnp.sum(weights, -1, keepdims=True)
        mixed_rows = mixed_rows + dot_full(weights, values_all * here, ((1,), (0,)), precision)

    def norm(values, index):
        center = values - jnp.mean(values, -1, keepdims=True)
        inverse = lax.rsqrt(jnp.mean(center * center, -1, keepdims=True) + 1e-05)
        gain = hyper_gains[index : index + 1, :]
        return center * inverse * gain + hyper_shifts[index : index + 1, :]

    hidden = norm(query_rows + dot_full(mixed_rows, hyper_output, ((1,), (0,)), precision), 0)
    expand = dot_full(hidden, hyper_up, ((1,), (0,)), precision)
    expanded = expand * (0.5 + 0.5 * lax.erf(expand * 0.7071067811865476))
    return norm(hidden + dot_full(expanded, hyper_down, ((1,), (0,)), precision), 1)


def hyper_forward_body(*refs):
    refs[-1][...] = hyper_rows(highest, *(ref[...].astype(jnp.float32) for ref in refs[:-1]))


def hyper_forward(pick_rows, bias_mask, key_rows, params):
    return pl.pallas_call(
        hyper_forward_body,
        out_shape=jax.ShapeDtypeStruct((pick_rows.shape[0], key_rows.shape[1]), jnp.float32),
        compiler_params=kernel_params(),
        cost_estimate=pl.CostEstimate(flops=0, bytes_accessed=0, transcendentals=0),
        name="hyper_forward",
    )(pick_rows, bias_mask, key_rows, *params)


def hyper_backward_body(count, pick_ref, mask_ref, key_ref, *refs):
    params = [ref[...].astype(jnp.float32) for ref in refs[:6]]
    feats_ref, conv_ref, matrix_ref = refs[6:9]
    key_out, *param_outs = refs[9:16]
    matrix_out, shift_out = refs[16:]
    conv = conv_ref[...] * scaler
    hidden, pull = jax.vjp(
        lambda *items: hyper_rows(None, pick_ref[...], mask_ref[...], *items), key_ref[...], *params
    )
    rows = count + conv.shape[0]
    bias_grad = dot_full(conv, matrix_ref[...].astype(jnp.float32), ((1,), (1,)))
    blank = jnp.zeros((hidden.shape[0] - rows, hidden.shape[1]), jnp.float32)
    grads = pull(jnp.concatenate([feats_ref[...], bias_grad, blank], 0))
    key_out[...] = grads[0]
    for out, grad in zip(param_outs, grads[1:]):
        out[...] = grad
    matrix_out[...] = dot_full(hidden[count:rows], conv, ((0,), (0,)))
    shift_out[...] = jnp.sum(conv, 0, keepdims=True)


def hyper_backward(pick_rows, bias_mask, key_rows, params, feats_grad, conv_grad, bias_weight):
    out = lambda item: jax.ShapeDtypeStruct(item.shape, jnp.float32)
    return pl.pallas_call(
        partial(hyper_backward_body, feats_grad.shape[0]),
        out_shape=[
            out(key_rows),
            *(out(item) for item in params),
            out(bias_weight),
            jax.ShapeDtypeStruct((1, bias_weight.shape[1]), jnp.float32),
        ],
        compiler_params=kernel_params(),
        cost_estimate=pl.CostEstimate(flops=0, bytes_accessed=0, transcendentals=0),
        name="hyper_backward",
    )(pick_rows, bias_mask, key_rows, *params, feats_grad, conv_grad, bias_weight)


def hyper_layout(weight_tokens, bias_token, wave_rows):
    group_count, band_count, width = wave_rows.shape
    tokens = weight_tokens.shape[0]
    waves = group_count * band_count
    key_count = -(-(tokens + waves + 1) // 16) * 16
    query_count = -(-(waves + group_count) // 8) * 8
    key_rows = jnp.concatenate(
        [
            weight_tokens.astype(jnp.float32),
            wave_rows.reshape(waves, width),
            bias_token.astype(jnp.float32)[None, :],
            jnp.zeros((key_count - tokens - waves - 1, width), jnp.float32),
        ],
        0,
    )
    query_id = np.arange(query_count)[:, None]
    key_id = np.arange(key_count)[None, :]
    source = np.where(query_id < waves, tokens + query_id, tokens + waves)
    pick_rows = (key_id == source) & (query_id < waves + group_count)
    query_group = np.where(query_id < waves, query_id // band_count, query_id - waves)
    key_group = (key_id - tokens) // band_count
    allowed = (
        (key_id < tokens)
        | (key_id == tokens + waves)
        | ((key_id < tokens + waves) & (key_group == query_group))
    )
    return (
        jnp.asarray(pick_rows.astype(np.float32)),
        jnp.asarray(np.where(allowed, 0.0, -1e30).astype(np.float32)),
        key_rows,
    )


def spread_eye(rows, copies):
    count, width = rows.shape
    iota = lambda shape, axis: lax.broadcasted_iota(jnp.int32, shape, axis)
    wide = (iota((width, width * copies), 1) // copies == iota((width, width * copies), 0)).astype(
        jnp.bfloat16
    )
    tall = (iota((count * copies, count), 0) // copies == iota((count * copies, count), 1)).astype(
        jnp.bfloat16
    )
    spread = dot_nn(tall, dot_nn(rows, wide).astype(jnp.bfloat16))
    same = iota(spread.shape, 0) % copies == iota(spread.shape, 1) % copies
    return jnp.where(same, spread, 0.0).astype(jnp.bfloat16)


def make_kernel_body(feats_ref, weight_ref, bias_ref, part_ref, spread_ref):
    bands, block, width = part_ref.shape
    hidden = weight_ref.shape[0]

    @pl.when(pl.program_id(0) == 0)
    def _():
        spread_ref[...] = spread_eye(feats_ref[...], block)

    product = dot_nn(spread_ref[...], weight_ref[...].reshape(hidden * block, width))
    product = product.reshape(-1, bands, block, width)
    bias = bias_ref[...].astype(jnp.float32)
    part_ref[...] = (scaler * (product[0] + product[1] + bias[None])).astype(part_ref.dtype)


def make_kernel(band_feats, kernel_weight, kernel_bias):
    bands = band_feats.shape[0]
    hidden, rows, width = kernel_weight.shape
    block = 16
    feats = split_low(band_feats, 2, 0)
    if rows % block:
        product = jnp.einsum(
            "sh,hpd->spd", feats, kernel_weight, preferred_element_type=jnp.float32
        )
        total = jnp.sum(product.reshape(2, bands, rows, width), 0)
        return (scaler * (total + kernel_bias.astype(jnp.float32))).astype(jnp.bfloat16)
    return pl.pallas_call(
        make_kernel_body,
        grid=(rows // block,),
        in_specs=[
            whole_spec(feats.shape),
            pl.BlockSpec((hidden, block, width), lambda i: (0, i, 0)),
            pl.BlockSpec((block, width), lambda i: (i, 0)),
        ],
        out_specs=pl.BlockSpec((bands, block, width), lambda i: (0, i, 0)),
        out_shape=jax.ShapeDtypeStruct((bands, rows, width), jnp.bfloat16),
        scratch_shapes=[pltpu.VMEM((2 * bands * block, hidden * block), jnp.bfloat16)],
        compiler_params=kernel_params(),
        cost_estimate=pl.CostEstimate(flops=0, bytes_accessed=0, transcendentals=0),
        name="make_kernel",
    )(feats, kernel_weight, kernel_bias)


def table_body(feats_ref, out_ref):
    out_ref[...] = spread_eye(feats_ref[...], out_ref.shape[0] // feats_ref.shape[0])


def weight_table(feats, block):
    feats = (scaler * feats).astype(jnp.bfloat16).T
    if block != 16:
        return feats
    return pl.pallas_call(
        table_body,
        out_shape=jax.ShapeDtypeStruct(tuple(size * block for size in feats.shape), jnp.bfloat16),
        compiler_params=kernel_params(),
        cost_estimate=pl.CostEstimate(flops=0, bytes_accessed=0, transcendentals=0),
        name="weight_table",
    )(feats)


def weight_grad_body(table_ref, grad_ref, *refs):
    out_ref = refs[-1]
    hidden, block, width = out_ref.shape
    grad = grad_ref[...].reshape(-1, width)
    out_ref[...] = dot_nn(table_ref[...], grad).reshape(hidden, block, width)


def weight_grad(table, kernel_all):
    count, rows, width = kernel_all.shape
    block = 16
    if rows % block:
        return jnp.einsum("hs,spd->hpd", table, kernel_all, preferred_element_type=jnp.float32)
    hidden = table.shape[0] // block
    halves = 2
    return pl.pallas_call(
        weight_grad_body,
        grid=(rows // block, halves),
        in_specs=[
            pl.BlockSpec((hidden * block // halves, count * block), lambda i, j: (j, 0)),
            pl.BlockSpec((count, block, width), lambda i, j: (0, i, 0)),
        ],
        out_specs=pl.BlockSpec((hidden // halves, block, width), lambda i, j: (j, i, 0)),
        out_shape=jax.ShapeDtypeStruct((hidden, rows, width), jnp.float32),
        compiler_params=kernel_params(),
        cost_estimate=pl.CostEstimate(flops=0, bytes_accessed=0, transcendentals=0),
        name="weight_grad",
    )(table, kernel_all)


def feats_body(grad_ref, weight_ref, out_ref):
    bands, block, width = grad_ref.shape
    hidden = weight_ref.shape[0]
    product = dot_nt(
        grad_ref[...].reshape(bands * block, width), weight_ref[...].reshape(hidden * block, width)
    )
    iota = lambda shape, axis: lax.broadcasted_iota(jnp.int32, shape, axis)
    same = iota(product.shape, 0) % block == iota(product.shape, 1) % block
    kept = jnp.sum(jnp.where(same, product, 0.0).reshape(bands, block, hidden * block), 1)
    fold_shape = (hidden * block, hidden)
    fold = (iota(fold_shape, 0) // block == iota(fold_shape, 1)).astype(jnp.float32)
    out_ref[...] = scaler * dot_full(kept, fold, ((1,), (0,)))


def feats_piece(piece, kernel_weight, place):
    bands, block, width = piece.shape
    hidden = kernel_weight.shape[0]
    if block != 16:
        return scaler * jnp.einsum(
            "spd,hpd->sh",
            piece,
            kernel_weight[:, place * block : (place + 1) * block],
            preferred_element_type=jnp.float32,
        )
    return pl.pallas_call(
        feats_body,
        grid=(1,),
        in_specs=[
            whole_spec(piece.shape),
            pl.BlockSpec((hidden, block, width), lambda i: (0, place, 0)),
        ],
        out_specs=whole_spec((bands, hidden)),
        out_shape=jax.ShapeDtypeStruct((bands, hidden), jnp.float32),
        compiler_params=kernel_params(),
        cost_estimate=pl.CostEstimate(flops=0, bytes_accessed=0, transcendentals=0),
        name="feats_piece",
    )(piece, kernel_weight)


def finish_body(place_ref, own_ref, other_ref, in_ref, out_ref, up_ref, down_ref):
    rows, width = out_ref.shape
    half = rows // 2
    widen = lambda item: item.astype(jnp.float32)

    def emit(first, second):
        for core, ref in enumerate((first, second)):
            for y in range(2):
                for block in range(2):
                    at = (2 * core + block) * width
                    up_ref[y * half : (y + 1) * half, at : at + width] = widen(
                        ref[y, block * half : (block + 1) * half]
                    )
        in_ref[:, :width] = widen(first[0, rows : 2 * rows])
        in_ref[:, width : 2 * width] = widen(second[0, rows : 2 * rows])
        in_ref[:, 2 * width :] = widen(first[1, rows : 2 * rows])
        out_ref[...] = widen(second[1, rows : 2 * rows])

    def emit_down(ref):
        part = down_ref.shape[0] // 2
        for y in range(2):
            down_ref[y * part : (y + 1) * part] = widen(ref[y, 2 * rows :])

    pl.when(place_ref[0] == 0)(lambda: emit(own_ref, other_ref))
    pl.when(place_ref[0] == 1)(lambda: emit(other_ref, own_ref))
    pl.when(place_ref[1] == 1)(lambda: emit_down(own_ref))
    pl.when(place_ref[1] == 0)(lambda: emit_down(other_ref))


def finish_grads(place, own, other, rows, down_rows):
    width = own.shape[2]
    out = lambda *shape: jax.ShapeDtypeStruct(shape, jnp.float32)
    return pl.pallas_call(
        finish_body,
        in_specs=[
            pl.BlockSpec(memory_space=pltpu.SMEM),
            pl.BlockSpec(memory_space=pltpu.VMEM),
            pl.BlockSpec(memory_space=pltpu.VMEM),
        ],
        out_shape=[
            out(rows, 3 * width),
            out(rows, width),
            out(rows, 4 * width),
            out(down_rows, width),
        ],
        compiler_params=kernel_params(),
        cost_estimate=pl.CostEstimate(flops=0, bytes_accessed=0, transcendentals=0),
        name="finish_grads",
    )(place, own, other)


def on_device(
    group_size,
    dp_size,
    pixels,
    patch_index,
    kept_count,
    wavelength,
    weight_tokens,
    bias_token,
    hyper_project,
    hyper_output,
    hyper_gains,
    hyper_shifts,
    hyper_up,
    hyper_down,
    kernel_weight,
    kernel_bias,
    bias_weight,
    bias_shift,
    attention_in,
    attention_out,
    expand_weight,
    reduce_weight,
    norm_gains,
    norm_shifts,
    attention_bias,
    output_bias,
    expand_bias,
    reduce_bias,
    cotangent,
):
    floaty = jnp.float32
    low = jnp.bfloat16
    links = Links(group_size, dp_size)
    image_count, slot_count, band_count, pixel_count = pixels.shape[1:]
    model_width = cotangent.shape[-1]
    row_count = image_count * slot_count
    widen = lambda item: item.astype(floaty)
    hyper_params = (
        hyper_project,
        hyper_output,
        hyper_gains,
        hyper_shifts,
        hyper_up,
        hyper_down,
    )

    feed = gather_feed(links, expand_weight, reduce_weight)
    piece = attention_piece(links, attention_in, attention_out)
    piece = piece.reshape((1, 1, 1, 1) + piece.shape)
    block = gather_line(links, piece, 0)
    wave_rows = wave_embed(wavelength[0])
    own_hidden = hyper_forward(
        *hyper_layout(weight_tokens, bias_token, wave_rows[None]), hyper_params
    )
    band_feats = own_hidden[:band_count] + wave_rows
    bias_feat = own_hidden[band_count]
    kernel_part = make_kernel(band_feats, kernel_weight, kernel_bias)
    chunk_count = 3
    chunk_bands = band_count // chunk_count
    depth = chunk_bands * pixel_count
    kernel_part, block, wavelength, bias_feat = stage(kernel_part, block, wavelength, bias_feat)
    chunks = [
        kernel_part[i * chunk_bands : (i + 1) * chunk_bands][:, None, None]
        for i in range(chunk_count)
    ]

    line_one = gather_line(links, chunks[0], 1)
    other = links.xside(block)
    all_waves = spread_group(links, wavelength[0])
    line_one, other, chunks, pixels, all_waves = stage(line_one, other, chunks, pixels, all_waves)
    block = pair_up(block, other, links.x, 1)

    line_one, block, chunks = stage(line_one, block, chunks)
    line_two = gather_line(links, chunks[1], 1)
    other_one = links.xside(line_one)
    other = links.yside(block)
    pixel_rows = pixels.reshape(row_count, band_count * pixel_count)
    line_two, other_one, other, chunks, pixel_rows, all_waves, bias_feat = stage(
        line_two, other_one, other, chunks, pixel_rows, all_waves, bias_feat
    )
    kernel_one = pair_up(line_one, other_one, links.x, 2).reshape(depth, model_width)
    block = pair_up(block, other, links.y, 2)

    line_two, block, kernel_one, chunks = stage(line_two, block, kernel_one, chunks)
    line_three = gather_line(links, chunks[2], 1)
    other_two = links.xside(line_two)
    other = links.core(block)
    valid_rows = (
        lax.broadcasted_iota(jnp.int32, (image_count, slot_count), 1) < kept_count[0][:, None]
    )
    valid_rows = valid_rows.reshape(row_count, 1).astype(floaty)
    out_low = cotangent.reshape(row_count, model_width) * valid_rows.astype(low)
    conv_bias = scaler * (
        jnp.dot(bias_feat, widen(bias_weight), precision=highest) + widen(bias_shift)
    )
    spots = place_spots(patch_index[0].reshape(row_count), 3)
    table = split_low(jnp.concatenate([place_table(model_width), conv_bias[None, :]], 0), 3, 0)
    table = jnp.pad(table, ((0, 128 - table.shape[0]), (0, 0)))
    embed_part = dot_nn(spots, table) + dot_nn(pixel_rows[:, :depth], kernel_one)
    line_three, other_two, other, embed_part, out_low, all_waves = stage(
        line_three, other_two, other, embed_part, out_low, all_waves
    )
    kernel_two = pair_up(line_two, other_two, links.x, 2).reshape(depth, model_width)
    own = block.reshape(8, 2, model_width // 8, model_width)
    other = other.reshape(own.shape)
    counts = jnp.concatenate([kept_count[0], links.c.reshape(1)])

    line_three, kernel_two, all_waves = stage(line_three, kernel_two, all_waves)
    other_three = links.xside(line_three)
    embed_part = embed_part + dot_nn(pixel_rows[:, depth : 2 * depth], kernel_two)
    wave_all = jax.vmap(wave_embed)(all_waves)
    pick_rows, bias_mask, key_rows = hyper_layout(weight_tokens, bias_token, wave_all)
    all_hidden = hyper_forward(pick_rows, bias_mask, key_rows, hyper_params)
    wave_count = group_size * band_count
    feats_all = all_hidden[:wave_count] + wave_all.reshape(wave_count, HE)
    shard_pixels = kernel_bias.shape[0]
    piece_count = 2
    piece_pixels = shard_pixels // piece_count
    table_all = weight_table(feats_all, piece_pixels)
    other_three, embed_part, table_all = stage(other_three, embed_part, table_all)
    kernel_three = pair_up(line_three, other_three, links.x, 2).reshape(depth, model_width)

    gains = widen(norm_gains)
    shifts = widen(norm_shifts)
    start, hidden_one = embed_rows(
        embed_part, pixel_rows, kernel_three, jnp.stack([gains[0], shifts[0]]), 256
    )
    bias_full = jnp.concatenate(
        [widen(attention_bias[0]), jnp.zeros((model_width,), floaty), widen(attention_bias[1])]
    )[None, :]
    attended = attend_rows(
        0,
        6,
        None,
        counts,
        hidden_one,
        start,
        own,
        other,
        bias_full,
        jnp.stack([widen(output_bias), gains[1], shifts[1]]),
    )
    project, probs_low, mixed_rows, middle, hidden_two = attended

    half_other = (1 - links.c).reshape(1)
    half_own = links.c.reshape(1)
    wide_bias = widen(expand_bias)[None, :]
    up_other, down_other, bias_other, forward_part, back_part = expand_first(
        half_other, hidden_two, out_low, feed, wide_bias
    )
    up_other, down_other, forward_part = stage(up_other, down_other, forward_part)
    up_other = links.core(up_other)
    down_other = links.core(down_other)
    up_own, down_own, bias_own, encoded, middle_grad, middle_low, sums_two = expand_second(
        half_own,
        hidden_two,
        out_low,
        feed,
        wide_bias,
        forward_part,
        back_part,
        middle,
        valid_rows,
        jnp.stack([widen(reduce_bias), gains[1]]),
    )
    encoded = encoded.reshape(cotangent.shape)
    up_other, down_other, up_own, down_own, middle_low = stage(
        up_other, down_other, up_own, down_own, middle_low
    )
    shard_rows = model_width // dp_size
    down_rows = reduce_weight.shape[0]
    up_shape = (links.line, 2, shard_rows, up_own.shape[1])
    up_pair = [up_own.reshape(up_shape), up_other.reshape(up_shape)]
    down_shape = (-1, 2, down_rows // 2, model_width)
    down_pair = [down_own.reshape(down_shape), down_other.reshape(down_shape)]

    send_up = add_low(*(pick(item, 1 - links.x, 1) for item in up_pair))
    send_down = add_low(*(pick(item, 1 - links.y, 1) for item in down_pair))
    send_up, send_down, middle_low = stage(send_up, send_down, middle_low)
    other_up = links.xside(send_up)
    other_down = links.yside(send_down)
    project_low, conv_low, sums_one, third_sums = attend_back(
        counts, project, probs_low, start, middle_grad, middle_low, own, other, gains[0:1], 256
    )
    kernel_grad = contract_rows(pixel_rows, conv_low).astype(low)
    kernel_grad = kernel_grad.reshape(band_count, links.line, 2, shard_pixels, model_width)
    piece_of = lambda i, side: pick(
        kernel_grad[:, :, :, i * piece_pixels : (i + 1) * piece_pixels], side, 2
    )
    send_one = piece_of(0, 1 - links.x)
    other_up, other_down, kernel_grad, send_one = stage(
        other_up, other_down, kernel_grad, send_one
    )
    up_sum = add_low(*(pick(item, links.x, 1) for item in up_pair), other_up)
    up_sum = up_sum.reshape(links.line, 2, shard_rows // 2, -1)
    down_sum = add_low(*(pick(item, links.y, 1) for item in down_pair), other_down)
    small = jnp.concatenate(
        [
            sums_one[0:1],
            sums_two[0:1],
            sums_one[1:2],
            sums_two[1:2],
            third_sums[:, :model_width],
            third_sums[:, 2 * model_width :],
            sums_two[2:4],
            pair_up(bias_own, bias_other, links.c, 1).reshape(-1, model_width),
            sums_one[2:3],
        ],
        0,
    )

    def halve_down(block, stride):
        block = block.reshape(2, -1, down_rows // 2, model_width)
        bit = lax.axis_index("dp") // stride % 2
        return pick(block, 1 - bit, 0), pick(block, bit, 0)

    send_up = pick(up_sum, 1 - links.y, 1)
    stride = dp_size // 4
    send_down, keep_down = halve_down(down_sum, stride)
    other_one = links.xside(send_one)
    send_up, send_down, keep_down, small, project_low = stage(
        send_up, send_down, keep_down, small, project_low
    )
    other_up = links.yside(send_up)
    other_down = links.zside(send_down, stride)
    step = 2
    while step < dp_size:
        small = small + links.zside(small, step)
        step *= 2
    grad_units = [
        contract_rows(hidden_one, project_low[:, i * model_width : (i + 1) * model_width])
        for i in range(3)
    ] + [contract_rows(mixed_rows, middle_low)]
    grad_units = [unit.astype(low) for unit in grad_units]
    units_of = lambda side: jnp.stack(
        [
            jnp.where(side == 0, grad_units[0], grad_units[1]),
            jnp.where(side == 0, grad_units[2], grad_units[3]),
        ]
    )
    send_units = units_of(1 - links.c)
    send_two = piece_of(1, 1 - links.x)
    other_one, other_up, other_down, small, send_units, send_two, kernel_grad = stage(
        other_one, other_up, other_down, small, send_units, send_two, kernel_grad
    )
    line_parts = lambda block: block.reshape(band_count, links.line, -1, model_width)
    finish_piece = lambda terms: add_low(*terms).reshape(band_count, -1, model_width)
    ready = line_parts(add_low(piece_of(0, links.x), other_one))

    ready, send_two, send_units, conv_low, other_up, other_down = stage(
        ready, send_two, send_units, conv_low, other_up, other_down
    )
    other_two = links.xside(send_two)
    total_one = send_line(links, ready, 1, links.zside)
    other_units = links.core(send_units)
    up_sum = add_low(pick(up_sum, links.y, 1), other_up)
    down_sum = add_low(keep_down, other_down)
    other_two, total_one, other_units, up_sum, down_sum, conv_low = stage(
        other_two, total_one, other_units, up_sum, down_sum, conv_low
    )
    ready = line_parts(add_low(piece_of(1, links.x), other_two))
    units = add_low(units_of(links.c), other_units)
    while stride > 2:
        stride //= 2
        send_down, keep_down = halve_down(down_sum, stride)
        down_sum = add_low(keep_down, links.zside(send_down, stride))

    send_units = pick(units, 1 - links.y, 0)
    send_down, keep_down = halve_down(down_sum, 1)
    ready, send_units, send_down, keep_down, total_one, conv_low = stage(
        ready, send_units, send_down, keep_down, total_one, conv_low
    )
    total_two = send_line(links, ready, 1, links.zside)
    other_units = links.yside(send_units)
    other_down = links.xside(send_down)
    low_one = finish_piece(total_one)
    feats_one = feats_piece(low_one, kernel_weight, 0)
    wide_kernel = jnp.concatenate([kernel_one, kernel_two, kernel_three], 0)
    pixel_grad = pixel_gradient(conv_low, wide_kernel, image_count, band_count)
    total_two, other_units, other_down, feats_one, low_one, pixel_grad = stage(
        total_two, other_units, other_down, feats_one, low_one, pixel_grad
    )
    pixel_grad = pixel_grad.transpose(0, 2, 1, 3)[None]
    low_two = finish_piece(total_two)

    feats_part = feats_one + feats_piece(low_two, kernel_weight, 1)
    tiny = jnp.concatenate([small, feats_part.reshape(-1, model_width)], 0)
    tiny, units, other_units, low_two = stage(tiny, units, other_units, low_two)
    tiny = tiny + links.xside(tiny)
    units = add_low(pick(units, links.y, 0), other_units)
    units = units.reshape(links.line, 2, shard_rows, model_width)
    send_units = pick(units, 1 - links.x, 1)
    kernel_low = jnp.concatenate([low_one, low_two], 1)
    tiny, send_units, kernel_low, units = stage(tiny, send_units, kernel_low, units)
    other_units = links.xside(send_units)
    other_low = links.yside(kernel_low)
    small_count = small.shape[0]
    feats_part = tiny[small_count:].reshape(feats_part.shape)
    step = 2
    while step < dp_size:
        feats_part = feats_part + links.zside(feats_part, step)
        step *= 2
    small = tiny[: small_count - 1]
    conv_all = tiny[small_count - 1 : small_count]
    other_small = links.core(tiny[:small_count])
    small = small + other_small[:-1]
    conv_all = pair_up(conv_all, other_small[-1:], links.c, 0)
    down_sum = add_low(keep_down, other_down).reshape(down_rows // 2, model_width)
    feats_part, other_units, small, conv_all, down_sum = stage(
        feats_part, other_units, small, conv_all, down_sum
    )
    units = add_low(pick(units, links.x, 1), other_units).reshape(links.line, -1, model_width)
    half_shard = shard_rows // 2
    up_blocks = up_sum.reshape(links.line, half_shard, 2, model_width).transpose(0, 2, 1, 3)
    both = jnp.concatenate([up_blocks.reshape(units.shape), units], 1)

    tiny = jnp.concatenate([small, conv_all, feats_part.reshape(-1, model_width)], 0)
    tiny, both, down_sum = stage(tiny, both, down_sum)
    both = send_line(links, both, 0, links.zside)
    other_down = links.owner_line(down_sum)
    other_tiny = links.yside(tiny)
    small = small + other_tiny[: small_count - 1]
    conv_all = pair_up(conv_all, other_tiny[small_count - 1 : small_count + 1], links.y, 0)
    feats_part = feats_part[None]
    feats_y = other_tiny[small_count + 1 :].reshape(feats_part.shape)
    feats_two = pair_up(feats_part, feats_y, links.y, 0)
    feats_c = links.core(feats_two)
    feats_grad = pair_up(feats_two[:, None], feats_c[:, None], links.c, 1).reshape(-1, HE)
    key_grad, *param_grads, bias_weight_grad, bias_shift_grad = hyper_backward(
        pick_rows,
        bias_mask,
        key_rows,
        hyper_params,
        feats_grad,
        conv_all,
        bias_weight,
    )
    kernel_all = pair_up(kernel_low[None], other_low[None], links.y, 0)[:, None]
    both, other_down, key_grad, kernel_all, small = stage(
        both, other_down, key_grad, kernel_all, small
    )
    both = jnp.concatenate([add_low(*both), add_low(down_sum, other_down)], 0)[None]

    both, kernel_all = stage(both, kernel_all)
    other_both = links.yside(both)
    other_all = links.core(kernel_all)
    kernel_all = pair_up(kernel_all, other_all, links.c, 1)
    kernel_all = kernel_all.reshape((wave_count,) + kernel_low.shape[1:])
    weight_shard_grad = weight_grad(table_all, kernel_all)
    bias_shard_grad = scaler * jnp.sum(kernel_all.astype(floaty), 0)
    token_count = weight_tokens.shape[0]
    other_both, weight_shard_grad, bias_shard_grad = stage(
        other_both, weight_shard_grad, bias_shard_grad
    )
    both = pair_up(both, other_both, links.y, 0)
    other_both = links.core(both)
    is_owner = lax.axis_index("dp") // (dp_size // 2) == links.c
    if shard_rows % 32 == 0:
        place = jnp.stack([links.c, is_owner.astype(jnp.int32)])
        block_shards = finish_grads(place, both, other_both, shard_rows, down_rows)
    else:
        down_total = jnp.where(is_owner, both[:, 2 * shard_rows :], other_both[:, 2 * shard_rows :])
        cores = pair_up(both[:, None], other_both[:, None], links.c, 1)
        up_total = cores[:, :, :shard_rows].reshape(2, 2, 2, half_shard, model_width)
        unit_all = cores[:, :, shard_rows : 2 * shard_rows].reshape(4, shard_rows, model_width)
        block_shards = (
            widen(jnp.concatenate([unit_all[i] for i in range(3)], 1)),
            widen(unit_all[3]),
            widen(up_total.transpose(0, 3, 1, 2, 4).reshape(shard_rows, -1)),
            widen(down_total.reshape(down_rows, model_width)),
        )
    return (
        encoded,
        pixel_grad,
        key_grad[:token_count],
        key_grad[token_count + wave_count],
        *param_grads,
        weight_shard_grad,
        bias_shard_grad,
        bias_weight_grad,
        bias_shift_grad.reshape(-1),
        *block_shards,
        small[0:2],
        small[2:4],
        small[4:6],
        small[6],
        small[8:].reshape(-1),
        small[7],
    )


def solution(mesh):
    placed = (
        P("group", "dp", None, None, None),
        P("group", "dp", None),
        P("group", "dp"),
        P("group", None),
        P(),
        P(),
        P(),
        P(),
        P(),
        P(),
        P(),
        P(),
        P(None, "dp", None),
        P("dp", None),
        P(),
        P(),
        P("dp", None),
        P("dp", None),
        P("dp", None),
        P("dp", None),
        P(),
        P(),
        P(),
        P(),
        P(),
        P(),
        P("group", "dp", None, None),
    )
    return jax.shard_map(
        partial(on_device, mesh.shape["group"], mesh.shape["dp"]),
        mesh=mesh,
        in_specs=placed,
        out_specs=(
            P("group", "dp", None, None),
            P("group", "dp", None, None, None),
            P(),
            P(),
            P(),
            P(),
            P(),
            P(),
            P(),
            P(),
            P(None, "dp", None),
            P("dp", None),
            P(),
            P(),
            P("dp", None),
            P("dp", None),
            P("dp", None),
            P("dp", None),
            P(),
            P(),
            P(),
            P(),
            P(),
            P(),
        ),
        check_vma=False,
    )
```

```python
from functools import partial

import jax
import jax.numpy as jnp
import numpy as np
from jax import lax
from jax.experimental import pallas as pl
from jax.experimental.pallas import tpu as pltpu
from jax.sharding import PartitionSpec as P

HE = 128
HH = 4
SIDE = 14


scaler = 0.01
highest = lax.Precision.HIGHEST


def contract_rows(operand, partner):
    return lax.dot_general(
        operand, partner, (((0,), (0,)), ((), ())), preferred_element_type=jnp.float32
    )


def wave_embed(wave_ids):
    half_width = HE // 2
    frequency = 1.0 / 10000.0 ** (jnp.arange(half_width, dtype=jnp.float32) / half_width)
    angles = wave_ids.astype(jnp.float32)[:, None] * frequency
    return jnp.concatenate([jnp.sin(angles), jnp.cos(angles)], -1)


def place_table(model_width):
    quarter = model_width // 4
    frequency = 1.0 / 10000.0 ** (jnp.arange(quarter, dtype=jnp.float32) / quarter)
    angle = jnp.arange(SIDE, dtype=jnp.float32)[:, None] * frequency
    waves = jnp.concatenate([jnp.sin(angle), jnp.cos(angle)], -1)
    blank = jnp.zeros_like(waves)
    return jnp.concatenate(
        [jnp.concatenate([waves, blank], -1), jnp.concatenate([blank, waves], -1)], 0
    )


def place_spots(patch_ids, copies):
    lanes = jnp.arange(128, dtype=jnp.int32)[None, :]
    spot = lanes % (2 * SIDE + 1)
    row_id = (patch_ids // SIDE)[:, None]
    col_id = (patch_ids % SIDE)[:, None] + SIDE
    hit = (spot == row_id) | (spot == col_id) | (spot == 2 * SIDE)
    return (hit & (lanes < copies * (2 * SIDE + 1))).astype(jnp.bfloat16)


def split_low(values, count, axis):
    pieces = []
    for _ in range(count):
        piece = values.astype(jnp.bfloat16)
        pieces.append(piece)
        values = values - piece.astype(jnp.float32)
    return jnp.concatenate(pieces, axis)


def stage(*values):
    return lax.optimization_barrier(values)


class Links:
    def __init__(self, group_size, dp_size):
        self.group_size = group_size
        self.dp_size = dp_size
        group_id = lax.axis_index("group")
        dp_id = lax.axis_index("dp")
        self.y = group_id // 2
        self.c = group_id % 2
        self.x = dp_id % 2
        self.digits = []
        stride = 2
        while stride < dp_size:
            size = min(4, dp_size // stride)
            self.digits.insert(0, (size, stride, dp_id // stride % size))
            stride *= size
        self.line = dp_size // 2
        self.z = dp_id // 2

    def core(self, block):
        return lax.ppermute(block, "group", [(i, i ^ 1) for i in range(self.group_size)])

    def yside(self, block):
        return lax.ppermute(block, "group", [(i, i ^ 2) for i in range(self.group_size)])

    def xside(self, block):
        return lax.ppermute(block, "dp", [(i, i ^ 1) for i in range(self.dp_size)])

    def zside(self, block, step):
        return lax.ppermute(block, "dp", [(i, i ^ step) for i in range(self.dp_size)])

    def owner_pairs(self, target_of):
        pairs = []
        for group_id in range(self.group_size):
            for dp_id in range(self.dp_size):
                target = target_of(group_id, dp_id)
                if target is not None:
                    pairs.append(
                        (group_id * self.dp_size + dp_id, target[0] * self.dp_size + target[1])
                    )
        return pairs

    def owner_line(self, block):
        top = self.dp_size // 2
        pairs = self.owner_pairs(lambda g, d: (g, d ^ top) if d // top != g % 2 else None)
        return lax.ppermute(block, ("group", "dp"), pairs)

    def owner_core(self, block):
        top = self.dp_size // 2
        pairs = self.owner_pairs(lambda g, d: (g ^ 1, d) if d // top == g % 2 else None)
        return lax.ppermute(block, ("group", "dp"), pairs)


def pick(block, index, axis, count=1):
    return lax.dynamic_slice_in_dim(block, index, count, axis)


def add_low(*items):
    total = items[0].astype(jnp.float32)
    for item in items[1:]:
        total = total + item.astype(jnp.float32)
    return total.astype(jnp.bfloat16)


def pair_up(block, other, bit, axis):
    return jnp.where(
        bit == 0,
        jnp.concatenate([block, other], axis),
        jnp.concatenate([other, block], axis),
    )


def place_digit(block, received, me, axis):
    size = len(received) + 1
    shape = block.shape[:axis] + (size,) + block.shape[axis + 1 :]
    out = jnp.zeros(shape, block.dtype)
    for step, piece in zip(range(size), [block] + received):
        at = tuple(me ^ step if i == axis else 0 for i in range(len(shape)))
        out = lax.dynamic_update_slice(out, piece, at)
    return out


def gather_line(links, piece, axis):
    lead, tail = piece.shape[:axis], piece.shape[axis + 1 :]
    count = len(links.digits)
    block = piece.reshape(lead + (1,) * count + tail)
    for place, (size, stride, me) in reversed(list(enumerate(links.digits))):
        received = [links.zside(block, stride * step) for step in range(1, size)]
        block = place_digit(block, received, me, axis + place)
    return block.reshape(lead + (links.line,) + tail)


def send_line(links, block, axis, sender):
    lead, tail = block.shape[:axis], block.shape[axis + 1 :]
    block = block.reshape(lead + tuple(size for size, _, _ in links.digits) + tail)
    for place, (size, stride, me) in enumerate(links.digits):
        if place:
            block = add_low(*terms)
        terms = [pick(block, me, axis + place)] + [
            sender(pick(block, me ^ step, axis + place), stride * step) for step in range(1, size)
        ]
    return [term.reshape(lead + tail) for term in terms]


def attention_piece(links, attention_in, attention_out):
    width = attention_out.shape[1]
    thirds = [attention_in[:, i * width : (i + 1) * width] for i in range(3)]
    return lax.dynamic_index_in_dim(
        jnp.stack(thirds + [attention_out]), lax.axis_index("group"), 0, False
    )


def gather_feed(links, expand_weight, reduce_weight):
    width = reduce_weight.shape[1]
    count = links.group_size
    group_id = lax.axis_index("group")
    up = pick(expand_weight, group_id * width, 1, width)
    rows = reduce_weight.shape[0] // count
    down = pick(reduce_weight, group_id * rows, 0, rows)
    wide = lax.all_gather(jnp.stack([up, down]), ("dp", "group"), axis=0)
    wide = wide.reshape(links.dp_size, count, 2, rows, width)
    if rows % 16:
        up = wide[:, :, 0].transpose(1, 0, 2, 3).reshape(count, 8, width // 8, width)
        down = wide[:, :, 1].reshape(8, count, width // 8, width)
        wide = jnp.stack([up.transpose(1, 0, 2, 3), down], 2)
    return wide


def spread_group(links, piece):
    piece = piece.reshape((1, 1) + piece.shape)
    piece = pair_up(piece, links.yside(piece), links.y, 0)
    piece = pair_up(piece, links.core(piece), links.c, 1)
    return piece.reshape((-1,) + piece.shape[2:])


def sum_dp(links, values):
    step = 1
    while step < links.dp_size:
        values = values + links.zside(values, step)
        step *= 2
    return values


VMEM_BYTES = 60 * 1024 * 1024


def kernel_params():
    return pltpu.CompilerParams(vmem_limit_bytes=VMEM_BYTES)


def whole_spec(shape):
    return pl.BlockSpec(shape, lambda *_: (0,) * len(shape))


def norm_rows(values, epsilon):
    center = values - jnp.mean(values, -1, keepdims=True)
    inverse = lax.rsqrt(jnp.mean(center * center, -1, keepdims=True) + epsilon)
    return center * inverse, inverse


def dot_nn(one, two):
    return lax.dot_general(one, two, (((1,), (0,)), ((), ())), preferred_element_type=jnp.float32)


def dot_nt(one, two):
    return lax.dot_general(one, two, (((1,), (1,)), ((), ())), preferred_element_type=jnp.float32)


def dot_tn(one, two):
    return lax.dot_general(one, two, (((0,), (0,)), ((), ())), preferred_element_type=jnp.float32)


def embed_body(side_ref, part_ref, pixel_ref, own_ref, other_ref, norm_ref, *refs):
    start_ref, hidden_ref, kernel_ref = refs
    bands, line, pixels, width = own_ref.shape

    def fill(refs):
        for band in range(bands):
            for place in range(line):
                for side in range(2):
                    at = ((band * line + place) * 2 + side) * pixels
                    kernel_ref[at : at + pixels, :] = refs[side][band, place]

    first = pl.program_id(0) == 0
    pl.when(first & (side_ref[0] == 0))(lambda: fill((own_ref, other_ref)))
    pl.when(first & (side_ref[0] == 1))(lambda: fill((other_ref, own_ref)))
    start = part_ref[...] + dot_nn(pixel_ref[...], kernel_ref[...])
    start_ref[...] = start
    normed, _ = norm_rows(start, 1e-06)
    hidden_ref[...] = (normed * norm_ref[0:1, :] + norm_ref[1:2, :]).astype(jnp.bfloat16)


def embed_rows(side, part, pixel_rows, own, other, norm_one, block_rows):
    rows, width = part.shape
    bands, line, _, pixels, _ = own.shape
    if pixels % 16:
        wide = pair_up(own, other, side, 2)
        side = jnp.zeros_like(side)
        own, other = jnp.split(wide.reshape(bands, 2, -1, width), 2, 1)
        bands, line, pixels = bands, 1, own.shape[2]
    own = own.reshape(bands, line, pixels, width)
    other = other.reshape(own.shape)
    depth = bands * line * 2 * pixels
    last = pixel_rows.shape[1] // depth - 1
    row_spec = lambda cols: pl.BlockSpec((block_rows, cols), lambda i: (i, 0))
    return pl.pallas_call(
        embed_body,
        grid=(rows // block_rows,),
        in_specs=[
            pl.BlockSpec(memory_space=pltpu.SMEM),
            row_spec(width),
            pl.BlockSpec((block_rows, depth), lambda i: (i, last)),
            whole_spec(own.shape),
            whole_spec(own.shape),
            whole_spec(norm_one.shape),
        ],
        out_specs=[row_spec(width), row_spec(width)],
        out_shape=[
            jax.ShapeDtypeStruct((rows, width), jnp.float32),
            jax.ShapeDtypeStruct((rows, width), jnp.bfloat16),
        ],
        scratch_shapes=[pltpu.VMEM((depth, width), jnp.bfloat16)],
        compiler_params=kernel_params(),
        cost_estimate=pl.CostEstimate(flops=0, bytes_accessed=0, transcendentals=0),
        name="embed_rows",
    )(side.reshape(1), part, pixel_rows, own, other, norm_one)


def pixel_grad_body(grad_ref, kernel_ref, out_ref):
    images, bands, slots, depth = out_ref.shape
    for band in range(bands):
        part = dot_nt(grad_ref[...], kernel_ref[band * depth : (band + 1) * depth, :])
        out_ref[:, band] = part.astype(out_ref.dtype).reshape(images, slots, depth)


def pixel_gradient(conv_low, wide_kernel, images, bands):
    rows, width = conv_low.shape
    slots = rows // images
    depth = wide_kernel.shape[0] // bands
    block = images // 3
    return pl.pallas_call(
        pixel_grad_body,
        grid=(3,),
        in_specs=[
            pl.BlockSpec((block * slots, width), lambda i: (i, 0)),
            whole_spec(wide_kernel.shape),
        ],
        out_specs=pl.BlockSpec((block, bands, slots, depth), lambda i: (i, 0, 0, 0)),
        out_shape=jax.ShapeDtypeStruct((images, bands, slots, depth), jnp.bfloat16),
        compiler_params=kernel_params(),
        cost_estimate=pl.CostEstimate(flops=0, bytes_accessed=0, transcendentals=0),
        name="pixel_gradient",
    )(conv_low, wide_kernel)


def pair_stack(block, low_half):
    zero = jnp.zeros_like(block)
    return jnp.concatenate(
        [jnp.where(low_half, block, zero), jnp.where(low_half, zero, block)], 0
    )


def half_reduce(values, low_half, reducer, filler):
    first = reducer(jnp.where(low_half, values, filler), -1, keepdims=True)
    second = reducer(jnp.where(low_half, filler, values), -1, keepdims=True)
    return jnp.where(low_half, first, second)


def join_weights(count_ref, own_ref, other_ref, weight_ref):
    width = weight_ref.shape[1]

    def fill(refs):
        for unit in range(4):
            weight_ref[unit] = refs[unit % 2][:, unit // 2].reshape(width, width)

    core = count_ref[count_ref.shape[0] - 1]
    first = pl.program_id(0) == 0
    pl.when(first & (core == 0))(lambda: fill((own_ref, other_ref)))
    pl.when(first & (core == 1))(lambda: fill((other_ref, own_ref)))


def attend_body(
    first,
    count_ref,
    hidden_ref,
    start_ref,
    own_ref,
    other_ref,
    bias_ref,
    rows_ref,
    project_ref,
    probs_ref,
    mixed_ref,
    middle_ref,
    hidden_two_ref,
    score_ref,
    weight_ref,
):
    join_weights(count_ref, own_ref, other_ref, weight_ref)
    block_rows, width = hidden_ref.shape
    slots = 64
    images = block_rows // slots
    base = (pl.program_id(0) + first) * images
    for third in range(3):
        at = third * width
        weight = weight_ref[third]
        project_ref[:, at : at + width] = (
            dot_nn(hidden_ref[...], weight) + bias_ref[:, at : at + width]
        ).astype(jnp.bfloat16)
    lanes = lax.broadcasted_iota(jnp.int32, (slots, 128), 1)
    low_half = lanes < 64
    key_id = jnp.where(low_half, lanes, lanes - 64)
    pairs = width // 128
    blocks = [(image, pair) for image in range(images) for pair in range(pairs)]
    for place, (image, pair) in enumerate(blocks):
        here = slice(image * slots, (image + 1) * slots)
        at = pair * 128
        queries = project_ref[here, at : at + 128]
        keys = pair_stack(project_ref[here, width + at : width + at + 128], low_half)
        keep = key_id < count_ref[base + image]
        score_ref[place * slots : (place + 1) * slots, :] = jnp.where(
            keep, dot_nt(queries, keys) * 0.125, -1000000000.0
        )
    for image in range(images):
        here = slice(image * pairs * slots, (image + 1) * pairs * slots)
        scores = score_ref[here, :]
        wide_half = lax.broadcasted_iota(jnp.int32, scores.shape, 1) < 64
        probs = jnp.exp(scores - half_reduce(scores, wide_half, jnp.max, -3e38))
        score_ref[here, :] = probs / half_reduce(probs, wide_half, jnp.sum, 0.0)
    for place, (image, pair) in enumerate(blocks):
        here = slice(image * slots, (image + 1) * slots)
        at = pair * 128
        values = pair_stack(project_ref[here, 2 * width + at : 2 * width + at + 128], low_half)
        probs_low = score_ref[place * slots : (place + 1) * slots, :].astype(jnp.bfloat16)
        probs_ref[here, at : at + 128] = probs_low
        mixed_ref[here, at : at + 128] = dot_nn(probs_low, values).astype(jnp.bfloat16)
    middle = start_ref[...] + dot_nn(mixed_ref[...], weight_ref[3]) + rows_ref[0:1, :]
    middle_ref[...] = middle
    normed, _ = norm_rows(middle, 1e-06)
    hidden_two_ref[...] = (normed * rows_ref[1:2, :] + rows_ref[2:3, :]).astype(jnp.bfloat16)


def attend_rows(first, steps, earlier, counts, hidden_one, start, own, other, bias_full, rows_in):
    rows, width = hidden_one.shape
    block_rows = 128
    row_spec = lambda cols: pl.BlockSpec((block_rows, cols), lambda i, *_: (i + first, 0))
    low = jnp.bfloat16
    keep = list(earlier or ())

    def body(count_ref, *refs):
        refs = refs[:6] + refs[6 + len(keep) :]
        attend_body(first, count_ref, *refs)

    return pl.pallas_call(
        body,
        grid_spec=pltpu.PrefetchScalarGridSpec(
            num_scalar_prefetch=1,
            grid=(steps,),
            in_specs=[
                row_spec(width),
                row_spec(width),
                whole_spec(own.shape),
                whole_spec(other.shape),
                whole_spec(bias_full.shape),
                whole_spec(rows_in.shape),
                *(pl.BlockSpec(memory_space=pl.ANY) for _ in keep),
            ],
            out_specs=[
                row_spec(3 * width),
                row_spec(width),
                row_spec(width),
                row_spec(width),
                row_spec(width),
            ],
            scratch_shapes=[
                pltpu.VMEM((block_rows * width // 128, 128), jnp.float32),
                pltpu.VMEM((4, width, width), low),
            ],
        ),
        out_shape=[
            jax.ShapeDtypeStruct((rows, 3 * width), low),
            jax.ShapeDtypeStruct((rows, width), low),
            jax.ShapeDtypeStruct((rows, width), low),
            jax.ShapeDtypeStruct((rows, width), jnp.float32),
            jax.ShapeDtypeStruct((rows, width), low),
        ],
        input_output_aliases={7 + i: i for i in range(len(keep))},
        compiler_params=kernel_params(),
        cost_estimate=pl.CostEstimate(flops=0, bytes_accessed=0, transcendentals=0),
        name="attend_rows",
    )(counts, hidden_one, start, own, other, bias_full, rows_in, *keep)


def expand_step(hidden_ref, turned_ref, out_ref, up_ref, bias_ref, down_ref):
    low = jnp.bfloat16
    out_low = out_ref[...]
    width = out_low.shape[1]
    up = up_ref[...].reshape(width, -1)
    down = down_ref[...].reshape(-1, width)
    pre = dot_nn(hidden_ref[...], up) + bias_ref[...]
    cumulative = 0.5 + 0.5 * lax.erf(pre * 0.7071067811865476)
    slope = cumulative + pre * (jnp.exp(pre * pre * -0.5) * 0.3989422804014327)
    activated = (pre * cumulative).astype(low)
    pre_grad = dot_nt(out_low, down) * slope
    pre_low = pre_grad.astype(low)
    return (
        jnp.sum(pre_grad, 0, keepdims=True),
        dot_nn(activated, down),
        dot_nt(pre_low, up),
        dot_nn(turned_ref[...], pre_low),
        dot_tn(activated, out_low),
    )


def accumulate(ref, part):
    @pl.when(pl.program_id(0) == 0)
    def _():
        ref[...] = part

    @pl.when(pl.program_id(0) > 0)
    def _():
        ref[...] += part


def first_body(
    half_ref,
    hidden_ref,
    out_ref,
    up_ref,
    bias_ref,
    down_ref,
    grad_up_ref,
    grad_down_ref,
    bias_grad_ref,
    forward_ref,
    back_ref,
    turned_ref,
):
    @pl.when(pl.program_id(0) == 0)
    def _():
        turned_ref[...] = hidden_ref[...].T

    bias_grad, forward_part, back_part, grad_up, grad_down = expand_step(
        hidden_ref, turned_ref, out_ref, up_ref, bias_ref, down_ref
    )
    bias_grad_ref[...] = bias_grad
    grad_up_ref[...] = grad_up.astype(jnp.bfloat16)
    grad_down_ref[...] = grad_down.astype(jnp.bfloat16)
    accumulate(forward_ref, forward_part)
    accumulate(back_ref, back_part)


def second_body(
    half_ref,
    hidden_ref,
    out_ref,
    up_ref,
    bias_ref,
    down_ref,
    forward_ref,
    back_ref,
    middle_ref,
    valid_ref,
    rows_ref,
    grad_up_ref,
    grad_down_ref,
    bias_grad_ref,
    encoded_ref,
    middle_grad_ref,
    middle_low_ref,
    sums_ref,
    forward_acc,
    back_acc,
    turned_ref,
):
    step = pl.program_id(0)
    low = jnp.bfloat16

    @pl.when(step == 0)
    def _():
        turned_ref[...] = hidden_ref[...].T
        forward_acc[...] = forward_ref[...]
        back_acc[...] = back_ref[...]

    bias_grad, forward_part, back_part, grad_up, grad_down = expand_step(
        hidden_ref, turned_ref, out_ref, up_ref, bias_ref, down_ref
    )
    bias_grad_ref[...] = bias_grad
    grad_up_ref[...] = grad_up.astype(low)
    grad_down_ref[...] = grad_down.astype(low)
    forward_acc[...] += forward_part
    back_acc[...] += back_part

    @pl.when(step == pl.num_programs(0) - 1)
    def _():
        middle = middle_ref[...]
        encoded_ref[...] = (
            (middle + forward_acc[...] + rows_ref[0:1, :]) * valid_ref[...]
        ).astype(low)
        normed, inverse = norm_rows(middle, 1e-06)
        grad = back_acc[...]
        out_grad = out_ref[...].astype(jnp.float32)
        scaled = grad * rows_ref[1:2, :]
        middle_grad = out_grad + inverse * (
            scaled
            - jnp.mean(scaled, -1, keepdims=True)
            - normed * jnp.mean(scaled * normed, -1, keepdims=True)
        )
        middle_grad_ref[...] = middle_grad
        middle_low_ref[...] = middle_grad.astype(low)
        sums_ref[0:1, :] = jnp.sum(grad * normed, 0, keepdims=True)
        sums_ref[1:2, :] = jnp.sum(grad, 0, keepdims=True)
        sums_ref[2:3, :] = jnp.sum(middle_grad, 0, keepdims=True)
        sums_ref[3:4, :] = jnp.sum(out_grad, 0, keepdims=True)


def expand_call(name, body, half, rows, width, ins, extra_ins, extra_outs, scratch):
    packed = ins[2].shape
    low = jnp.bfloat16
    steps = packed[1] // 2
    full = whole_spec((rows, width))
    place = lambda i, half: steps * half[0] + i
    return pl.pallas_call(
        body,
        grid_spec=pltpu.PrefetchScalarGridSpec(
            num_scalar_prefetch=1,
            grid=(steps,),
            in_specs=[
                full,
                full,
                pl.BlockSpec(
                    (packed[0], 1, 1) + packed[3:], lambda i, half: (0, place(i, half), 0, 0, 0)
                ),
                pl.BlockSpec((1, width), lambda i, half: (0, place(i, half))),
                pl.BlockSpec(
                    (packed[0] // packed[1], packed[1], 1) + packed[3:],
                    lambda i, half: (place(i, half), 0, 1, 0, 0),
                ),
                *extra_ins,
            ],
            out_specs=[
                pl.BlockSpec((width, width), lambda i, half: (0, i)),
                pl.BlockSpec((width, width), lambda i, half: (i, 0)),
                pl.BlockSpec((1, width), lambda i, half: (0, i)),
                *(whole_spec(item.shape) for item in extra_outs),
            ],
            scratch_shapes=scratch,
        ),
        out_shape=[
            jax.ShapeDtypeStruct((width, steps * width), low),
            jax.ShapeDtypeStruct((steps * width, width), low),
            jax.ShapeDtypeStruct((1, steps * width), jnp.float32),
            *extra_outs,
        ],
        compiler_params=kernel_params(),
        cost_estimate=pl.CostEstimate(flops=0, bytes_accessed=0, transcendentals=0),
        name=name,
    )(half, *ins)


def expand_first(half, hidden_two, out_low, packed, bias):
    rows, width = hidden_two.shape
    total = jax.ShapeDtypeStruct((rows, width), jnp.float32)
    return expand_call(
        "expand_first",
        first_body,
        half,
        rows,
        width,
        (hidden_two, out_low, packed, bias, packed),
        [],
        [total, total],
        [pltpu.VMEM((width, rows), jnp.bfloat16)],
    )


def expand_second(
    half,
    hidden_two,
    out_low,
    packed,
    bias,
    forward_part,
    back_part,
    middle,
    valid_rows,
    rows_in,
):
    rows, width = hidden_two.shape
    full = whole_spec((rows, width))
    total = pltpu.VMEM((rows, width), jnp.float32)
    return expand_call(
        "expand_second",
        second_body,
        half,
        rows,
        width,
        (
            hidden_two,
            out_low,
            packed,
            bias,
            packed,
            forward_part,
            back_part,
            middle,
            valid_rows,
            rows_in,
        ),
        [full, full, full, whole_spec(valid_rows.shape), whole_spec(rows_in.shape)],
        [
            jax.ShapeDtypeStruct((rows, width), jnp.bfloat16),
            jax.ShapeDtypeStruct((rows, width), jnp.float32),
            jax.ShapeDtypeStruct((rows, width), jnp.bfloat16),
            jax.ShapeDtypeStruct((4, width), jnp.float32),
        ],
        [total, total, pltpu.VMEM((width, rows), jnp.bfloat16)],
    )


def attend_back_body(
    count_ref,
    project_ref,
    probs_ref,
    start_ref,
    middle_grad_ref,
    middle_low_ref,
    own_ref,
    other_ref,
    rows_ref,
    project_low_ref,
    conv_low_ref,
    sums_ref,
    third_ref,
    mixed_low,
    grad_ref,
    weight_ref,
):
    join_weights(count_ref, own_ref, other_ref, weight_ref)
    block_rows, width = start_ref.shape
    slots = 64
    low = jnp.bfloat16
    mixed_low[...] = dot_nt(middle_low_ref[...], weight_ref[3]).astype(low)
    lanes = lax.broadcasted_iota(jnp.int32, (slots, 128), 1)
    low_half = lanes < 64

    def fold(block):
        return jnp.where(low_half, block[:slots], block[slots:])

    pairs = width // 128
    images = block_rows // slots
    blocks = [(image, pair) for image in range(images) for pair in range(pairs)]
    for place, (image, pair) in enumerate(blocks):
        here = slice(image * slots, (image + 1) * slots)
        at = pair * 128
        values = pair_stack(project_ref[here, 2 * width + at : 2 * width + at + 128], low_half)
        mixed = mixed_low[here, at : at + 128]
        grad_ref[place * slots : (place + 1) * slots, :] = dot_nt(mixed, values)
        project_low_ref[here, 2 * width + at : 2 * width + at + 128] = fold(
            dot_tn(probs_ref[here, at : at + 128], mixed)
        ).astype(low)
    for image in range(images):
        rows = slice(image * slots, (image + 1) * slots)
        probs = jnp.concatenate(
            [probs_ref[rows, pair * 128 : (pair + 1) * 128] for pair in range(pairs)], 0
        ).astype(jnp.float32)
        here = slice(image * pairs * slots, (image + 1) * pairs * slots)
        prob_grad = grad_ref[here, :]
        wide_half = lax.broadcasted_iota(jnp.int32, prob_grad.shape, 1) < 64
        centre = half_reduce(prob_grad * probs, wide_half, jnp.sum, 0.0)
        grad_ref[here, :] = probs * (prob_grad - centre)
    for place, (image, pair) in enumerate(blocks):
        here = slice(image * slots, (image + 1) * slots)
        at = pair * 128
        queries = project_ref[here, at : at + 128]
        keys = pair_stack(project_ref[here, width + at : width + at + 128], low_half)
        score_low = grad_ref[place * slots : (place + 1) * slots, :].astype(low)
        project_low_ref[here, at : at + 128] = (dot_nn(score_low, keys) * 0.125).astype(low)
        project_low_ref[here, width + at : width + at + 128] = (
            fold(dot_tn(score_low, queries)) * 0.125
        ).astype(low)
    project_low = project_low_ref[...]
    grad = dot_nt(project_low[:, :width], weight_ref[0])
    for third in (1, 2):
        at = third * width
        grad = grad + dot_nt(project_low[:, at : at + width], weight_ref[third])
    normed, inverse = norm_rows(start_ref[...], 1e-06)
    scaled = grad * rows_ref[0:1, :]
    start_grad = middle_grad_ref[...] + inverse * (
        scaled
        - jnp.mean(scaled, -1, keepdims=True)
        - normed * jnp.mean(scaled * normed, -1, keepdims=True)
    )
    conv_low_ref[...] = start_grad.astype(low)
    sums = jnp.concatenate(
        [
            jnp.sum(grad * normed, 0, keepdims=True),
            jnp.sum(grad, 0, keepdims=True),
            jnp.sum(start_grad, 0, keepdims=True),
        ],
        0,
    )
    third = jnp.sum(project_low.astype(jnp.float32), 0, keepdims=True)

    @pl.when(pl.program_id(0) == 0)
    def _():
        sums_ref[...] = sums
        third_ref[...] = third

    @pl.when(pl.program_id(0) > 0)
    def _():
        sums_ref[...] += sums
        third_ref[...] += third


def attend_back(
    counts, project, probs_low, start, middle_grad, middle_low, own, other, rows_in, block_rows
):
    rows, width = start.shape
    row_spec = lambda cols: pl.BlockSpec((block_rows, cols), lambda i, *_: (i, 0))
    low = jnp.bfloat16
    return pl.pallas_call(
        attend_back_body,
        grid_spec=pltpu.PrefetchScalarGridSpec(
            num_scalar_prefetch=1,
            grid=(rows // block_rows,),
            in_specs=[
                row_spec(3 * width),
                row_spec(width),
                row_spec(width),
                row_spec(width),
                row_spec(width),
                whole_spec(own.shape),
                whole_spec(other.shape),
                whole_spec(rows_in.shape),
            ],
            out_specs=[
                row_spec(3 * width),
                row_spec(width),
                whole_spec((3, width)),
                whole_spec((1, 3 * width)),
            ],
            scratch_shapes=[
                pltpu.VMEM((block_rows, width), low),
                pltpu.VMEM((block_rows * width // 128, 128), jnp.float32),
                pltpu.VMEM((4, width, width), low),
            ],
        ),
        out_shape=[
            jax.ShapeDtypeStruct((rows, 3 * width), low),
            jax.ShapeDtypeStruct((rows, width), low),
            jax.ShapeDtypeStruct((3, width), jnp.float32),
            jax.ShapeDtypeStruct((1, 3 * width), jnp.float32),
        ],
        compiler_params=kernel_params(),
        cost_estimate=pl.CostEstimate(flops=0, bytes_accessed=0, transcendentals=0),
        name="attend_back",
    )(counts, project, probs_low, start, middle_grad, middle_low, own, other, rows_in)


def dot_full(one, two, dims, precision=highest):
    return lax.dot_general(
        one, two, (dims, ((), ())), precision=precision, preferred_element_type=jnp.float32
    )


def hyper_rows(
    precision,
    pick_rows,
    bias_mask,
    key_rows,
    hyper_project,
    hyper_output,
    hyper_gains,
    hyper_shifts,
    hyper_up,
    hyper_down,
):
    width = key_rows.shape[1]
    query_rows = dot_full(pick_rows, key_rows, ((1,), (0,)))
    queries = dot_full(query_rows, hyper_project[:, :width], ((1,), (0,)), precision)
    keys_all = dot_full(key_rows, hyper_project[:, width : 2 * width], ((1,), (0,)), precision)
    values_all = dot_full(key_rows, hyper_project[:, 2 * width :], ((1,), (0,)), precision)
    head_size = width // HH
    head_of = lax.broadcasted_iota(jnp.int32, (1, width), 1) // head_size
    mixed_rows = jnp.zeros_like(query_rows)
    for head in range(HH):
        here = (head_of == head).astype(jnp.float32)
        scores = dot_full(queries * here, keys_all, ((1,), (1,)), precision) * head_size ** (-0.5) + bias_mask
        peak = lax.stop_gradient(jnp.max(scores, -1, keepdims=True))
        weights = jnp.exp(scores - peak)
        weights = weights / jnp.sum(weights, -1, keepdims=True)
        mixed_rows = mixed_rows + dot_full(weights, values_all * here, ((1,), (0,)), precision)

    def norm(values, index):
        center = values - jnp.mean(values, -1, keepdims=True)
        inverse = lax.rsqrt(jnp.mean(center * center, -1, keepdims=True) + 1e-05)
        gain = hyper_gains[index : index + 1, :]
        return center * inverse * gain + hyper_shifts[index : index + 1, :]

    hidden = norm(query_rows + dot_full(mixed_rows, hyper_output, ((1,), (0,)), precision), 0)
    expand = dot_full(hidden, hyper_up, ((1,), (0,)), precision)
    expanded = expand * (0.5 + 0.5 * lax.erf(expand * 0.7071067811865476))
    return norm(hidden + dot_full(expanded, hyper_down, ((1,), (0,)), precision), 1)


def hyper_forward_body(*refs):
    refs[-1][...] = hyper_rows(highest, *(ref[...].astype(jnp.float32) for ref in refs[:-1]))


def hyper_forward(pick_rows, bias_mask, key_rows, params):
    return pl.pallas_call(
        hyper_forward_body,
        out_shape=jax.ShapeDtypeStruct((pick_rows.shape[0], key_rows.shape[1]), jnp.float32),
        compiler_params=kernel_params(),
        cost_estimate=pl.CostEstimate(flops=0, bytes_accessed=0, transcendentals=0),
        name="hyper_forward",
    )(pick_rows, bias_mask, key_rows, *params)


def hyper_backward_body(count, pick_ref, mask_ref, key_ref, *refs):
    params = [ref[...].astype(jnp.float32) for ref in refs[:6]]
    feats_ref, conv_ref, matrix_ref = refs[6:9]
    key_out, *param_outs = refs[9:16]
    matrix_out, shift_out = refs[16:]
    conv = conv_ref[...] * scaler
    hidden, pull = jax.vjp(
        lambda *items: hyper_rows(None, pick_ref[...], mask_ref[...], *items), key_ref[...], *params
    )
    rows = count + conv.shape[0]
    bias_grad = dot_full(conv, matrix_ref[...].astype(jnp.float32), ((1,), (1,)))
    blank = jnp.zeros((hidden.shape[0] - rows, hidden.shape[1]), jnp.float32)
    grads = pull(jnp.concatenate([feats_ref[...], bias_grad, blank], 0))
    key_out[...] = grads[0]
    for out, grad in zip(param_outs, grads[1:]):
        out[...] = grad
    matrix_out[...] = dot_full(hidden[count:rows], conv, ((0,), (0,)))
    shift_out[...] = jnp.sum(conv, 0, keepdims=True)


def hyper_backward(pick_rows, bias_mask, key_rows, params, feats_grad, conv_grad, bias_weight):
    out = lambda item: jax.ShapeDtypeStruct(item.shape, jnp.float32)
    return pl.pallas_call(
        partial(hyper_backward_body, feats_grad.shape[0]),
        out_shape=[
            out(key_rows),
            *(out(item) for item in params),
            out(bias_weight),
            jax.ShapeDtypeStruct((1, bias_weight.shape[1]), jnp.float32),
        ],
        compiler_params=kernel_params(),
        cost_estimate=pl.CostEstimate(flops=0, bytes_accessed=0, transcendentals=0),
        name="hyper_backward",
    )(pick_rows, bias_mask, key_rows, *params, feats_grad, conv_grad, bias_weight)


def hyper_layout(weight_tokens, bias_token, wave_rows):
    group_count, band_count, width = wave_rows.shape
    tokens = weight_tokens.shape[0]
    waves = group_count * band_count
    key_count = -(-(tokens + waves + 1) // 16) * 16
    query_count = -(-(waves + group_count) // 8) * 8
    key_rows = jnp.concatenate(
        [
            weight_tokens.astype(jnp.float32),
            wave_rows.reshape(waves, width),
            bias_token.astype(jnp.float32)[None, :],
            jnp.zeros((key_count - tokens - waves - 1, width), jnp.float32),
        ],
        0,
    )
    query_id = np.arange(query_count)[:, None]
    key_id = np.arange(key_count)[None, :]
    source = np.where(query_id < waves, tokens + query_id, tokens + waves)
    pick_rows = (key_id == source) & (query_id < waves + group_count)
    query_group = np.where(query_id < waves, query_id // band_count, query_id - waves)
    key_group = (key_id - tokens) // band_count
    allowed = (
        (key_id < tokens)
        | (key_id == tokens + waves)
        | ((key_id < tokens + waves) & (key_group == query_group))
    )
    return (
        jnp.asarray(pick_rows.astype(np.float32)),
        jnp.asarray(np.where(allowed, 0.0, -1e30).astype(np.float32)),
        key_rows,
    )


def spread_eye(rows, copies):
    count, width = rows.shape
    iota = lambda shape, axis: lax.broadcasted_iota(jnp.int32, shape, axis)
    wide = (iota((width, width * copies), 1) // copies == iota((width, width * copies), 0)).astype(
        jnp.bfloat16
    )
    tall = (iota((count * copies, count), 0) // copies == iota((count * copies, count), 1)).astype(
        jnp.bfloat16
    )
    spread = dot_nn(tall, dot_nn(rows, wide).astype(jnp.bfloat16))
    same = iota(spread.shape, 0) % copies == iota(spread.shape, 1) % copies
    return jnp.where(same, spread, 0.0).astype(jnp.bfloat16)


def make_kernel_body(feats_ref, weight_ref, bias_ref, part_ref, spread_ref):
    bands, block, width = part_ref.shape
    hidden = weight_ref.shape[0]

    @pl.when(pl.program_id(0) == 0)
    def _():
        spread_ref[...] = spread_eye(feats_ref[...], block)

    product = dot_nn(spread_ref[...], weight_ref[...].reshape(hidden * block, width))
    product = product.reshape(-1, bands, block, width)
    bias = bias_ref[...].astype(jnp.float32)
    part_ref[...] = (scaler * (product[0] + product[1] + bias[None])).astype(part_ref.dtype)


def make_kernel(band_feats, kernel_weight, kernel_bias):
    bands = band_feats.shape[0]
    hidden, rows, width = kernel_weight.shape
    block = 16
    feats = split_low(band_feats, 2, 0)
    if rows % block:
        product = jnp.einsum(
            "sh,hpd->spd", feats, kernel_weight, preferred_element_type=jnp.float32
        )
        total = jnp.sum(product.reshape(2, bands, rows, width), 0)
        return (scaler * (total + kernel_bias.astype(jnp.float32))).astype(jnp.bfloat16)
    return pl.pallas_call(
        make_kernel_body,
        grid=(rows // block,),
        in_specs=[
            whole_spec(feats.shape),
            pl.BlockSpec((hidden, block, width), lambda i: (0, i, 0)),
            pl.BlockSpec((block, width), lambda i: (i, 0)),
        ],
        out_specs=pl.BlockSpec((bands, block, width), lambda i: (0, i, 0)),
        out_shape=jax.ShapeDtypeStruct((bands, rows, width), jnp.bfloat16),
        scratch_shapes=[pltpu.VMEM((2 * bands * block, hidden * block), jnp.bfloat16)],
        compiler_params=kernel_params(),
        cost_estimate=pl.CostEstimate(flops=0, bytes_accessed=0, transcendentals=0),
        name="make_kernel",
    )(feats, kernel_weight, kernel_bias)


def table_body(feats_ref, out_ref):
    out_ref[...] = spread_eye(feats_ref[...], out_ref.shape[0] // feats_ref.shape[0])


def weight_table(feats, block):
    feats = (scaler * feats).astype(jnp.bfloat16).T
    if block != 16:
        return feats
    return pl.pallas_call(
        table_body,
        out_shape=jax.ShapeDtypeStruct(tuple(size * block for size in feats.shape), jnp.bfloat16),
        compiler_params=kernel_params(),
        cost_estimate=pl.CostEstimate(flops=0, bytes_accessed=0, transcendentals=0),
        name="weight_table",
    )(feats)


def weight_grad_body(table_ref, grad_ref, *refs):
    out_ref = refs[-1]
    hidden, block, width = out_ref.shape
    grad = grad_ref[...].reshape(-1, width)
    out_ref[...] = dot_nn(table_ref[...], grad).reshape(hidden, block, width)


def weight_grad(table, kernel_all):
    count, rows, width = kernel_all.shape
    block = 16
    if rows % block:
        return jnp.einsum("hs,spd->hpd", table, kernel_all, preferred_element_type=jnp.float32)
    hidden = table.shape[0] // block
    halves = 2
    return pl.pallas_call(
        weight_grad_body,
        grid=(rows // block, halves),
        in_specs=[
            pl.BlockSpec((hidden * block // halves, count * block), lambda i, j: (j, 0)),
            pl.BlockSpec((count, block, width), lambda i, j: (0, i, 0)),
        ],
        out_specs=pl.BlockSpec((hidden // halves, block, width), lambda i, j: (j, i, 0)),
        out_shape=jax.ShapeDtypeStruct((hidden, rows, width), jnp.float32),
        compiler_params=kernel_params(),
        cost_estimate=pl.CostEstimate(flops=0, bytes_accessed=0, transcendentals=0),
        name="weight_grad",
    )(table, kernel_all)


def feats_body(grad_ref, weight_ref, out_ref):
    bands, block, width = grad_ref.shape
    hidden = weight_ref.shape[0]
    product = dot_nt(
        grad_ref[...].reshape(bands * block, width), weight_ref[...].reshape(hidden * block, width)
    )
    iota = lambda shape, axis: lax.broadcasted_iota(jnp.int32, shape, axis)
    same = iota(product.shape, 0) % block == iota(product.shape, 1) % block
    kept = jnp.sum(jnp.where(same, product, 0.0).reshape(bands, block, hidden * block), 1)
    fold_shape = (hidden * block, hidden)
    fold = (iota(fold_shape, 0) // block == iota(fold_shape, 1)).astype(jnp.float32)
    out_ref[...] = scaler * dot_full(kept, fold, ((1,), (0,)))


def feats_piece(piece, kernel_weight, place):
    bands, block, width = piece.shape
    hidden = kernel_weight.shape[0]
    if block != 16:
        return scaler * jnp.einsum(
            "spd,hpd->sh",
            piece,
            kernel_weight[:, place * block : (place + 1) * block],
            preferred_element_type=jnp.float32,
        )
    return pl.pallas_call(
        feats_body,
        grid=(1,),
        in_specs=[
            whole_spec(piece.shape),
            pl.BlockSpec((hidden, block, width), lambda i: (0, place, 0)),
        ],
        out_specs=whole_spec((bands, hidden)),
        out_shape=jax.ShapeDtypeStruct((bands, hidden), jnp.float32),
        compiler_params=kernel_params(),
        cost_estimate=pl.CostEstimate(flops=0, bytes_accessed=0, transcendentals=0),
        name="feats_piece",
    )(piece, kernel_weight)


def finish_body(place_ref, own_ref, other_ref, in_ref, out_ref, up_ref, down_ref):
    rows, width = out_ref.shape
    half = rows // 2
    widen = lambda item: item.astype(jnp.float32)

    def emit(first, second):
        for core, ref in enumerate((first, second)):
            for y in range(2):
                for block in range(2):
                    at = (2 * core + block) * width
                    up_ref[y * half : (y + 1) * half, at : at + width] = widen(
                        ref[y, block * half : (block + 1) * half]
                    )
        in_ref[:, :width] = widen(first[0, rows : 2 * rows])
        in_ref[:, width : 2 * width] = widen(second[0, rows : 2 * rows])
        in_ref[:, 2 * width :] = widen(first[1, rows : 2 * rows])
        out_ref[...] = widen(second[1, rows : 2 * rows])

    def emit_down(ref):
        part = down_ref.shape[0] // 2
        for y in range(2):
            down_ref[y * part : (y + 1) * part] = widen(ref[y, 2 * rows :])

    pl.when(place_ref[0] == 0)(lambda: emit(own_ref, other_ref))
    pl.when(place_ref[0] == 1)(lambda: emit(other_ref, own_ref))
    pl.when(place_ref[1] == 1)(lambda: emit_down(own_ref))
    pl.when(place_ref[1] == 0)(lambda: emit_down(other_ref))


def finish_grads(place, own, other, rows, down_rows):
    width = own.shape[2]
    out = lambda *shape: jax.ShapeDtypeStruct(shape, jnp.float32)
    return pl.pallas_call(
        finish_body,
        in_specs=[
            pl.BlockSpec(memory_space=pltpu.SMEM),
            pl.BlockSpec(memory_space=pltpu.VMEM),
            pl.BlockSpec(memory_space=pltpu.VMEM),
        ],
        out_shape=[
            out(rows, 3 * width),
            out(rows, width),
            out(rows, 4 * width),
            out(down_rows, width),
        ],
        compiler_params=kernel_params(),
        cost_estimate=pl.CostEstimate(flops=0, bytes_accessed=0, transcendentals=0),
        name="finish_grads",
    )(place, own, other)


def on_device(
    group_size,
    dp_size,
    pixels,
    patch_index,
    kept_count,
    wavelength,
    weight_tokens,
    bias_token,
    hyper_project,
    hyper_output,
    hyper_gains,
    hyper_shifts,
    hyper_up,
    hyper_down,
    kernel_weight,
    kernel_bias,
    bias_weight,
    bias_shift,
    attention_in,
    attention_out,
    expand_weight,
    reduce_weight,
    norm_gains,
    norm_shifts,
    attention_bias,
    output_bias,
    expand_bias,
    reduce_bias,
    cotangent,
):
    floaty = jnp.float32
    low = jnp.bfloat16
    links = Links(group_size, dp_size)
    image_count, slot_count, band_count, pixel_count = pixels.shape[1:]
    model_width = cotangent.shape[-1]
    row_count = image_count * slot_count
    widen = lambda item: item.astype(floaty)
    hyper_params = (
        hyper_project,
        hyper_output,
        hyper_gains,
        hyper_shifts,
        hyper_up,
        hyper_down,
    )

    feed = gather_feed(links, expand_weight, reduce_weight)
    piece = attention_piece(links, attention_in, attention_out)
    piece = piece.reshape((1, 1, 1, 1) + piece.shape)
    block = gather_line(links, piece, 0)
    wave_rows = wave_embed(wavelength[0])
    own_hidden = hyper_forward(
        *hyper_layout(weight_tokens, bias_token, wave_rows[None]), hyper_params
    )
    band_feats = own_hidden[:band_count] + wave_rows
    bias_feat = own_hidden[band_count]
    kernel_part = make_kernel(band_feats, kernel_weight, kernel_bias)
    chunk_count = 3
    chunk_bands = band_count // chunk_count
    depth = chunk_bands * pixel_count
    kernel_part, block, wavelength, bias_feat = stage(kernel_part, block, wavelength, bias_feat)
    chunks = [
        kernel_part[i * chunk_bands : (i + 1) * chunk_bands][:, None, None]
        for i in range(chunk_count)
    ]

    line_one = gather_line(links, chunks[0], 1)
    other = links.xside(block)
    all_waves = spread_group(links, wavelength[0])
    line_one, other, chunks, pixels, all_waves = stage(line_one, other, chunks, pixels, all_waves)
    block = pair_up(block, other, links.x, 1)

    line_one, block, chunks = stage(line_one, block, chunks)
    line_two = gather_line(links, chunks[1], 1)
    other_one = links.xside(line_one)
    other = links.yside(block)
    pixel_rows = pixels.reshape(row_count, band_count * pixel_count)
    line_two, other_one, other, chunks, pixel_rows, all_waves, bias_feat = stage(
        line_two, other_one, other, chunks, pixel_rows, all_waves, bias_feat
    )
    kernel_one = pair_up(line_one, other_one, links.x, 2).reshape(depth, model_width)
    block = pair_up(block, other, links.y, 2)

    line_two, block, kernel_one, chunks = stage(line_two, block, kernel_one, chunks)
    line_three = gather_line(links, chunks[2], 1)
    other_two = links.xside(line_two)
    other = links.core(block)
    valid_rows = (
        lax.broadcasted_iota(jnp.int32, (image_count, slot_count), 1) < kept_count[0][:, None]
    )
    valid_rows = valid_rows.reshape(row_count, 1).astype(floaty)
    out_low = cotangent.reshape(row_count, model_width) * valid_rows.astype(low)
    conv_bias = scaler * (
        jnp.dot(bias_feat, widen(bias_weight), precision=highest) + widen(bias_shift)
    )
    spots = place_spots(patch_index[0].reshape(row_count), 3)
    table = split_low(jnp.concatenate([place_table(model_width), conv_bias[None, :]], 0), 3, 0)
    table = jnp.pad(table, ((0, 128 - table.shape[0]), (0, 0)))
    embed_part = dot_nn(spots, table) + dot_nn(pixel_rows[:, :depth], kernel_one)
    line_three, other_two, other, embed_part, out_low, all_waves = stage(
        line_three, other_two, other, embed_part, out_low, all_waves
    )
    kernel_two = pair_up(line_two, other_two, links.x, 2).reshape(depth, model_width)
    own = block.reshape(8, 2, model_width // 8, model_width)
    other = other.reshape(own.shape)
    counts = jnp.concatenate([kept_count[0], links.c.reshape(1)])

    line_three, kernel_two, all_waves = stage(line_three, kernel_two, all_waves)
    other_three = links.xside(line_three)
    embed_part = embed_part + dot_nn(pixel_rows[:, depth : 2 * depth], kernel_two)
    wave_all = jax.vmap(wave_embed)(all_waves)
    pick_rows, bias_mask, key_rows = hyper_layout(weight_tokens, bias_token, wave_all)
    all_hidden = hyper_forward(pick_rows, bias_mask, key_rows, hyper_params)
    wave_count = group_size * band_count
    feats_all = all_hidden[:wave_count] + wave_all.reshape(wave_count, HE)
    shard_pixels = kernel_bias.shape[0]
    piece_count = 2
    piece_pixels = shard_pixels // piece_count
    table_all = weight_table(feats_all, piece_pixels)
    other_three, embed_part, table_all = stage(other_three, embed_part, table_all)
    kernel_three = pair_up(line_three, other_three, links.x, 2).reshape(depth, model_width)

    gains = widen(norm_gains)
    shifts = widen(norm_shifts)
    start, hidden_one = embed_rows(
        links.x,
        embed_part,
        pixel_rows,
        line_three,
        other_three,
        jnp.stack([gains[0], shifts[0]]),
        256,
    )
    bias_full = jnp.concatenate(
        [widen(attention_bias[0]), jnp.zeros((model_width,), floaty), widen(attention_bias[1])]
    )[None, :]
    attended = attend_rows(
        0,
        6,
        None,
        counts,
        hidden_one,
        start,
        own,
        other,
        bias_full,
        jnp.stack([widen(output_bias), gains[1], shifts[1]]),
    )
    project, probs_low, mixed_rows, middle, hidden_two = attended

    half_other = (1 - links.c).reshape(1)
    half_own = links.c.reshape(1)
    wide_bias = widen(expand_bias)[None, :]
    up_other, down_other, bias_other, forward_part, back_part = expand_first(
        half_other, hidden_two, out_low, feed, wide_bias
    )
    up_other, down_other, forward_part = stage(up_other, down_other, forward_part)
    up_other = links.core(up_other)
    down_other = links.core(down_other)
    up_own, down_own, bias_own, encoded, middle_grad, middle_low, sums_two = expand_second(
        half_own,
        hidden_two,
        out_low,
        feed,
        wide_bias,
        forward_part,
        back_part,
        middle,
        valid_rows,
        jnp.stack([widen(reduce_bias), gains[1]]),
    )
    encoded = encoded.reshape(cotangent.shape)
    up_other, down_other, up_own, down_own, middle_low = stage(
        up_other, down_other, up_own, down_own, middle_low
    )
    shard_rows = model_width // dp_size
    down_rows = reduce_weight.shape[0]
    up_shape = (links.line, 2, shard_rows, up_own.shape[1])
    up_pair = [up_own.reshape(up_shape), up_other.reshape(up_shape)]
    down_shape = (-1, 2, down_rows // 2, model_width)
    down_pair = [down_own.reshape(down_shape), down_other.reshape(down_shape)]

    send_up = add_low(*(pick(item, 1 - links.x, 1) for item in up_pair))
    send_down = add_low(*(pick(item, 1 - links.y, 1) for item in down_pair))
    send_up, send_down, middle_low = stage(send_up, send_down, middle_low)
    other_up = links.xside(send_up)
    other_down = links.yside(send_down)
    project_low, conv_low, sums_one, third_sums = attend_back(
        counts, project, probs_low, start, middle_grad, middle_low, own, other, gains[0:1], 256
    )
    kernel_grad = contract_rows(pixel_rows, conv_low).astype(low)
    kernel_grad = kernel_grad.reshape(band_count, links.line, 2, shard_pixels, model_width)
    piece_of = lambda i, side: pick(
        kernel_grad[:, :, :, i * piece_pixels : (i + 1) * piece_pixels], side, 2
    )
    send_one = piece_of(0, 1 - links.x)
    other_up, other_down, kernel_grad, send_one = stage(
        other_up, other_down, kernel_grad, send_one
    )
    up_sum = add_low(*(pick(item, links.x, 1) for item in up_pair), other_up)
    up_sum = up_sum.reshape(links.line, 2, shard_rows // 2, -1)
    down_sum = add_low(*(pick(item, links.y, 1) for item in down_pair), other_down)
    small = jnp.concatenate(
        [
            sums_one[0:1],
            sums_two[0:1],
            sums_one[1:2],
            sums_two[1:2],
            third_sums[:, :model_width],
            third_sums[:, 2 * model_width :],
            sums_two[2:4],
            pair_up(bias_own, bias_other, links.c, 1).reshape(-1, model_width),
            sums_one[2:3],
        ],
        0,
    )

    def halve_down(block, stride):
        block = block.reshape(2, -1, down_rows // 2, model_width)
        bit = lax.axis_index("dp") // stride % 2
        return pick(block, 1 - bit, 0), pick(block, bit, 0)

    send_up = pick(up_sum, 1 - links.y, 1)
    stride = dp_size // 4
    send_down, keep_down = halve_down(down_sum, stride)
    other_one = links.xside(send_one)
    send_up, send_down, keep_down, small, project_low = stage(
        send_up, send_down, keep_down, small, project_low
    )
    other_up = links.yside(send_up)
    other_down = links.zside(send_down, stride)
    step = 2
    while step < dp_size:
        small = small + links.zside(small, step)
        step *= 2
    grad_units = [
        contract_rows(hidden_one, project_low[:, i * model_width : (i + 1) * model_width])
        for i in range(3)
    ] + [contract_rows(mixed_rows, middle_low)]
    grad_units = [unit.astype(low) for unit in grad_units]
    units_of = lambda side: jnp.stack(
        [
            jnp.where(side == 0, grad_units[0], grad_units[1]),
            jnp.where(side == 0, grad_units[2], grad_units[3]),
        ]
    )
    send_units = units_of(1 - links.c)
    send_two = piece_of(1, 1 - links.x)
    other_one, other_up, other_down, small, send_units, send_two, kernel_grad = stage(
        other_one, other_up, other_down, small, send_units, send_two, kernel_grad
    )
    line_parts = lambda block: block.reshape(band_count, links.line, -1, model_width)
    finish_piece = lambda terms: add_low(*terms).reshape(band_count, -1, model_width)
    ready = line_parts(add_low(piece_of(0, links.x), other_one))

    ready, send_two, send_units, conv_low, other_up, other_down = stage(
        ready, send_two, send_units, conv_low, other_up, other_down
    )
    other_two = links.xside(send_two)
    total_one = send_line(links, ready, 1, links.zside)
    other_units = links.core(send_units)
    up_sum = add_low(pick(up_sum, links.y, 1), other_up)
    down_sum = add_low(keep_down, other_down)
    other_two, total_one, other_units, up_sum, down_sum, conv_low = stage(
        other_two, total_one, other_units, up_sum, down_sum, conv_low
    )
    ready = line_parts(add_low(piece_of(1, links.x), other_two))
    units = add_low(units_of(links.c), other_units)
    while stride > 2:
        stride //= 2
        send_down, keep_down = halve_down(down_sum, stride)
        down_sum = add_low(keep_down, links.zside(send_down, stride))

    send_units = pick(units, 1 - links.y, 0)
    send_down, keep_down = halve_down(down_sum, 1)
    ready, send_units, send_down, keep_down, total_one, conv_low = stage(
        ready, send_units, send_down, keep_down, total_one, conv_low
    )
    total_two = send_line(links, ready, 1, links.zside)
    other_units = links.yside(send_units)
    other_down = links.xside(send_down)
    low_one = finish_piece(total_one)
    feats_one = feats_piece(low_one, kernel_weight, 0)
    wide_kernel = jnp.concatenate([kernel_one, kernel_two, kernel_three], 0)
    pixel_grad = pixel_gradient(conv_low, wide_kernel, image_count, band_count)
    total_two, other_units, other_down, feats_one, low_one, pixel_grad = stage(
        total_two, other_units, other_down, feats_one, low_one, pixel_grad
    )
    pixel_grad = pixel_grad.transpose(0, 2, 1, 3)[None]
    low_two = finish_piece(total_two)

    feats_part = feats_one + feats_piece(low_two, kernel_weight, 1)
    tiny = jnp.concatenate([small, feats_part.reshape(-1, model_width)], 0)
    tiny, units, other_units, low_two = stage(tiny, units, other_units, low_two)
    tiny = tiny + links.xside(tiny)
    units = add_low(pick(units, links.y, 0), other_units)
    units = units.reshape(links.line, 2, shard_rows, model_width)
    send_units = pick(units, 1 - links.x, 1)
    kernel_low = jnp.concatenate([low_one, low_two], 1)
    tiny, send_units, kernel_low, units = stage(tiny, send_units, kernel_low, units)
    other_units = links.xside(send_units)
    other_low = links.yside(kernel_low)
    small_count = small.shape[0]
    feats_part = tiny[small_count:].reshape(feats_part.shape)
    step = 2
    while step < dp_size:
        feats_part = feats_part + links.zside(feats_part, step)
        step *= 2
    small = tiny[: small_count - 1]
    conv_all = tiny[small_count - 1 : small_count]
    other_small = links.core(tiny[:small_count])
    small = small + other_small[:-1]
    conv_all = pair_up(conv_all, other_small[-1:], links.c, 0)
    down_sum = add_low(keep_down, other_down).reshape(down_rows // 2, model_width)
    feats_part, other_units, small, conv_all, down_sum = stage(
        feats_part, other_units, small, conv_all, down_sum
    )
    units = add_low(pick(units, links.x, 1), other_units).reshape(links.line, -1, model_width)
    half_shard = shard_rows // 2
    up_blocks = up_sum.reshape(links.line, half_shard, 2, model_width).transpose(0, 2, 1, 3)
    both = jnp.concatenate([up_blocks.reshape(units.shape), units], 1)

    tiny = jnp.concatenate([small, conv_all, feats_part.reshape(-1, model_width)], 0)
    tiny, both, down_sum = stage(tiny, both, down_sum)
    both = send_line(links, both, 0, links.zside)
    other_down = links.owner_line(down_sum)
    other_tiny = links.yside(tiny)
    small = small + other_tiny[: small_count - 1]
    conv_all = pair_up(conv_all, other_tiny[small_count - 1 : small_count + 1], links.y, 0)
    feats_part = feats_part[None]
    feats_y = other_tiny[small_count + 1 :].reshape(feats_part.shape)
    feats_two = pair_up(feats_part, feats_y, links.y, 0)
    feats_c = links.core(feats_two)
    feats_grad = pair_up(feats_two[:, None], feats_c[:, None], links.c, 1).reshape(-1, HE)
    key_grad, *param_grads, bias_weight_grad, bias_shift_grad = hyper_backward(
        pick_rows,
        bias_mask,
        key_rows,
        hyper_params,
        feats_grad,
        conv_all,
        bias_weight,
    )
    kernel_all = pair_up(kernel_low[None], other_low[None], links.y, 0)[:, None]
    token_count = weight_tokens.shape[0]
    token_grad = key_grad[:token_count]
    bias_token_grad = key_grad[token_count + wave_count]
    small_parts = [small[0:2], small[2:4], small[4:6], small[6], small[8:].reshape(-1), small[7]]
    bias_shift_grad = bias_shift_grad.reshape(-1)
    both, other_down, token_grad, bias_token_grad, bias_shift_grad, kernel_all, small_parts = stage(
        both, other_down, token_grad, bias_token_grad, bias_shift_grad, kernel_all, small_parts
    )
    both = jnp.concatenate([add_low(*both), add_low(down_sum, other_down)], 0)[None]

    both, kernel_all = stage(both, kernel_all)
    other_both = links.yside(both)
    other_all = links.core(kernel_all)
    kernel_all = pair_up(kernel_all, other_all, links.c, 1)
    kernel_all = kernel_all.reshape((wave_count,) + kernel_low.shape[1:])
    weight_shard_grad = weight_grad(table_all, kernel_all)
    bias_shard_grad = scaler * jnp.sum(kernel_all.astype(floaty), 0)
    other_both, weight_shard_grad, bias_shard_grad = stage(
        other_both, weight_shard_grad, bias_shard_grad
    )
    both = pair_up(both, other_both, links.y, 0)
    other_both = links.core(both)
    is_owner = lax.axis_index("dp") // (dp_size // 2) == links.c
    if shard_rows % 32 == 0:
        place = jnp.stack([links.c, is_owner.astype(jnp.int32)])
        block_shards = finish_grads(place, both, other_both, shard_rows, down_rows)
    else:
        down_total = jnp.where(is_owner, both[:, 2 * shard_rows :], other_both[:, 2 * shard_rows :])
        cores = pair_up(both[:, None], other_both[:, None], links.c, 1)
        up_total = cores[:, :, :shard_rows].reshape(2, 2, 2, half_shard, model_width)
        unit_all = cores[:, :, shard_rows : 2 * shard_rows].reshape(4, shard_rows, model_width)
        block_shards = (
            widen(jnp.concatenate([unit_all[i] for i in range(3)], 1)),
            widen(unit_all[3]),
            widen(up_total.transpose(0, 3, 1, 2, 4).reshape(shard_rows, -1)),
            widen(down_total.reshape(down_rows, model_width)),
        )
    return (
        encoded,
        pixel_grad,
        token_grad,
        bias_token_grad,
        *param_grads,
        weight_shard_grad,
        bias_shard_grad,
        bias_weight_grad,
        bias_shift_grad,
        *block_shards,
        *small_parts,
    )


def solution(mesh):
    placed = (
        P("group", "dp", None, None, None),
        P("group", "dp", None),
        P("group", "dp"),
        P("group", None),
        P(),
        P(),
        P(),
        P(),
        P(),
        P(),
        P(),
        P(),
        P(None, "dp", None),
        P("dp", None),
        P(),
        P(),
        P("dp", None),
        P("dp", None),
        P("dp", None),
        P("dp", None),
        P(),
        P(),
        P(),
        P(),
        P(),
        P(),
        P("group", "dp", None, None),
    )
    return jax.shard_map(
        partial(on_device, mesh.shape["group"], mesh.shape["dp"]),
        mesh=mesh,
        in_specs=placed,
        out_specs=(
            P("group", "dp", None, None),
            P("group", "dp", None, None, None),
            P(),
            P(),
            P(),
            P(),
            P(),
            P(),
            P(),
            P(),
            P(None, "dp", None),
            P("dp", None),
            P(),
            P(),
            P("dp", None),
            P("dp", None),
            P("dp", None),
            P("dp", None),
            P(),
            P(),
            P(),
            P(),
            P(),
            P(),
        ),
        check_vma=False,
    )
```
